32 devices in a mesh: row: 8 (over z, y), col: 4 (over x, core).
Axes of the slice: x: 2, y: 2, z: 4, core: 2. Of those that a mesh axis runs over, the one named last changes fastest.
Arguments:
- density: bfloat16 [2, 256, 3, 128, 128], P(None, ('row', 'col')), may hold values from -1 to 3, as said below
- core_hamiltonian: bfloat16 [2, 256, 3, 128, 128], P(None, ('row', 'col')), may hold values from -2 to 2, as said below
- grid_term_old: float32 [256, 128, 128], P(('row', 'col')), may hold values from -0.25 to 0.25
- lead_blocks: int32 [8], replicated, may hold values from 0 to 255, as said below
- absorption: float32 [8], replicated, may hold values from 0.5 to 2
- collocation: bfloat16 [768, 2048, 128], P(('row', 'col')), may hold values from -0.5 to 0.5
- brick_block: int32 [8, 96], P(None, 'col'), may hold values from 0 to 255, as said below
Outputs:
- density_next: bfloat16 [2, 256, 3, 128, 128], P(None, ('row', 'col'))
- grid_term: float32 [256, 128, 128], P(('row', 'col'))
The draws below stay inside these ranges and needn't reach their ends.
Inputs may be any that keep to these rules, and one draw needn't show every extreme that they name: density is Hermitian: block (j, i) is the conjugate transpose of block (i, j); slots outside the matrix are zero. core_hamiltonian is Hermitian: block (j, i) is the conjugate transpose of block (i, j); slots outside the matrix are zero. `lead_blocks`: Distinct; 4 of them among the first 16 block rows and the others among the last 16. `brick_block`: entry [r, c * 24 + t] is the block of brick t of device (row r, col c); that block is held by a device of the same col. Among the bricks of one device at most 3 have blocks on devices of one row index, and in every device some row index has exactly 3.
All inputs are finite; a program needn't handle non-finite values.
Results may differ from the reference program's by a relative error of at most 0.007.
Values may be sent and summed in bfloat16 or wider, within the bound.
No kernel may reach another device: no remote copies, remote signals or barrier semaphores. Data moves between devices by JAX's collectives and lax.ppermute only.
A program may use at most 128 MiB of HBM per device.

```python
import math
import jax
import jax.numpy as jnp
from jax import lax

BS = 128
K = 1
SLOTS = 3
NBD = 8
NB = 256
G = 2048
BRD = 24
BRICKS = 768
CAP = 3
LEADS = 8
SPAN = 16
N_ROW = 8
N_COL = 4


def hermitian_band(raw):
    block_rows = raw.shape[1]
    rows_index = jnp.arange(block_rows)
    columns = []
    for slot_index in range(SLOTS):
        offset = slot_index - K
        mirror = jnp.roll(raw[:, :, SLOTS - 1 - slot_index], -offset, axis=1)
        mirror = jnp.swapaxes(mirror, -1, -2)
        valid = ((rows_index + offset >= 0) & (rows_index + offset < block_rows)).astype(jnp.float32)[:, None, None]
        real_part = 0.5 * (raw[0, :, slot_index] + mirror[0]) * valid
        imag_part = 0.5 * (raw[1, :, slot_index] - mirror[1]) * valid
        columns.append(jnp.stack([real_part, imag_part]))
    return jnp.stack(columns, axis=2)


def with_diagonal(band, values):
    identity = jnp.eye(BS, dtype=jnp.float32)
    return band.at[0, :, K].add(values[:, :, None] * identity)


def slot_profile(inner, outer):
    slot_iota = jnp.arange(SLOTS)
    return jnp.where(slot_iota == K, inner, outer).astype(jnp.float32)[None, None, :, None, None]


def draw_density(key, part):
    key = jax.random.fold_in(key, 21)
    key_raw, key_occ = jax.random.split(key)
    shape = (2, NB, SLOTS, BS, BS)
    raw = jnp.clip(0.15 * jax.random.normal(key_raw, shape, jnp.float32), -0.9, 0.9)
    occupation = jax.random.uniform(key_occ, (NB, BS), jnp.float32, 0.2, 1.8)
    return with_diagonal(hermitian_band(raw), occupation).astype(jnp.bfloat16)


def draw_core_hamiltonian(key, part):
    key = jax.random.fold_in(key, 22)
    key_raw, key_site = jax.random.split(key)
    shape = (2, NB, SLOTS, BS, BS)
    unit = jnp.clip(jax.random.normal(key_raw, shape, jnp.float32), -6.0, 6.0)
    raw = unit * slot_profile(0.02, 0.15)
    onsite = jax.random.uniform(key_site, (NB, BS), jnp.float32, -1.0, 1.0)
    return with_diagonal(hermitian_band(raw), onsite).astype(jnp.bfloat16)


def draw_lead_blocks(key, part):
    key = jax.random.fold_in(key, 23)
    key_low, key_high = jax.random.split(key)
    half_count = LEADS // 2
    lower = jax.random.permutation(key_low, SPAN)[:half_count]
    upper = NB - SPAN + jax.random.permutation(key_high, SPAN)[:half_count]
    return jnp.concatenate([lower, upper]).astype(jnp.int32)


def brick_sources(key):
    key_heavy, key_order, key_shuffle, key_local = jax.random.split(key, 4)
    heavy_row = jax.random.randint(key_heavy, (), 0, N_ROW)
    slot_order = jax.random.permutation(key_order, (N_ROW - 1) * CAP)[:BRD - CAP]
    others = (heavy_row + 1 + slot_order // CAP) % N_ROW
    sources = jnp.concatenate([jnp.ones((CAP,), jnp.int32) * heavy_row, others.astype(jnp.int32)])
    sources = jax.random.permutation(key_shuffle, sources)
    local_block = jax.random.randint(key_local, (BRD,), 0, NBD)
    return (sources, local_block)


def draw_brick_block(key, part):
    key = jax.random.fold_in(key, 31)
    device_keys = jax.random.split(key, N_ROW * N_COL)
    sources, local_block = jax.vmap(brick_sources)(device_keys)
    column = jnp.arange(N_ROW * N_COL, dtype=jnp.int32) % N_COL
    blocks = (sources * N_COL + column[:, None]) * NBD + local_block
    return blocks.reshape(N_ROW, N_COL * BRD).astype(jnp.int32)


def block_scale(key, dims, pieces, smallest, high):
    loudness, own = 1.0, jax.random.fold_in(key, 6)
    for position, parts in pieces:
        draws = jnp.exp(jax.random.uniform(jax.random.fold_in(own, position), (parts,), jnp.float32, smallest / len(pieces), high / len(pieces)))
        loudness = loudness * jnp.repeat(draws, dims[position] // parts).reshape([-1 if axis == position else 1 for axis in range(len(dims))])
    return loudness


def gaussian(stream_key, dims, scale, reach, cuts=(), held_as=jnp.bfloat16):
    loudness = block_scale(stream_key, dims, cuts, -0.22, 0.18) if cuts else 1.0
    result = jax.random.normal(stream_key, dims, jnp.float32) * scale * loudness
    return jnp.minimum(jnp.maximum(result, -reach), reach).astype(held_as)


def setup_inputs(seed: int = 0) -> dict:
    splits = jax.random.split(jax.random.key(seed), 8)
    return {
        "density": draw_density(jax.random.fold_in(splits[7], 71), 0),
        "core_hamiltonian": draw_core_hamiltonian(jax.random.fold_in(splits[7], 71), 0),
        "grid_term_old": gaussian(splits[2], (NB, BS, BS), 0.04, 0.25, ((0, 32),), jnp.float32),
        "lead_blocks": draw_lead_blocks(jax.random.fold_in(splits[7], 71), 0),
        "absorption": jnp.clip(jnp.exp(jax.random.uniform(splits[4], (LEADS,), jnp.float32, math.log(0.5), math.log(2.0))), 0.5, 2.0),
        "collocation": gaussian(splits[5], (BRICKS, G, BS), BS ** -0.5, 0.5, ((0, 32),)),
        "brick_block": draw_brick_block(jax.random.fold_in(splits[7], 71), 0),
    }


HALF_STEP = 0.2
GRID_FACTOR = 0.1

def band_product(left_band, right_ext):
    row_count = left_band.shape[1]
    slot_total = left_band.shape[2]
    band_reach = (slot_total - 1) // 2
    left_re = left_band[0].astype(jnp.float32)
    left_im = left_band[1].astype(jnp.float32)
    right_re = right_ext[0].astype(jnp.float32)
    right_im = right_ext[1].astype(jnp.float32)
    columns = []
    for slot_index in range(slot_total):
        total_re = jnp.zeros(left_re[:, 0].shape, jnp.float32)
        total_im = jnp.zeros(left_re[:, 0].shape, jnp.float32)
        for middle in range(slot_total):
            other_slot = slot_index - middle + band_reach
            if other_slot < 0 or other_slot >= slot_total:
                continue
            first_re = left_re[:, middle]
            first_im = left_im[:, middle]
            second_re = right_re[middle:middle + row_count, other_slot]
            second_im = right_im[middle:middle + row_count, other_slot]
            total_re = total_re + jnp.einsum('rab,rbc->rac', first_re, second_re) - jnp.einsum('rab,rbc->rac', first_im, second_im)
            total_im = total_im + jnp.einsum('rab,rbc->rac', first_re, second_im) + jnp.einsum('rab,rbc->rac', first_im, second_re)
        columns.append(jnp.stack([total_re, total_im]))
    return jnp.stack(columns, axis=2)

def pad_rows(band, width):
    return jnp.pad(band, ((0, 0), (width, width), (0, 0), (0, 0), (0, 0)))

def with_gamma(hermit, gamma):
    band_reach = (hermit.shape[2] - 1) // 2
    identity = jnp.eye(hermit.shape[-1], dtype=jnp.float32)
    diag_im = hermit[1, :, band_reach].astype(jnp.float32) + gamma[:, None, None] * identity
    return hermit.at[1, :, band_reach].set(diag_im.astype(jnp.bfloat16))

def add_diag(band, extra):
    band_reach = (band.shape[2] - 1) // 2
    diag_re = band[0, :, band_reach].astype(jnp.float32) + extra
    return band.at[0, :, band_reach].set(diag_re.astype(jnp.bfloat16))

def propagate(density, hermit, gamma):
    band_reach = (density.shape[2] - 1) // 2
    left_band = with_gamma(hermit, -gamma)
    right_band = with_gamma(hermit, gamma)
    product = band_product(left_band, pad_rows(density, band_reach)).astype(jnp.bfloat16)
    second = band_product(left_band, pad_rows(product, band_reach))
    second_order = 0.5 * HALF_STEP * HALF_STEP
    dens_f = density.astype(jnp.float32)
    prod_f = product.astype(jnp.float32)
    moved_re = dens_f[0] + HALF_STEP * prod_f[1] - second_order * second[0]
    moved_im = dens_f[1] - HALF_STEP * prod_f[0] - second_order * second[1]
    moved = jnp.stack([moved_re, moved_im]).astype(jnp.bfloat16)
    right_ext = pad_rows(right_band, band_reach)
    right_once = band_product(moved, right_ext).astype(jnp.bfloat16)
    right_twice = band_product(right_once, right_ext)
    moved_f = moved.astype(jnp.float32)
    once_f = right_once.astype(jnp.float32)
    out_re = moved_f[0] - HALF_STEP * once_f[1] - second_order * right_twice[0]
    out_im = moved_f[1] + HALF_STEP * once_f[0] - second_order * right_twice[1]
    return jnp.stack([out_re, out_im]).astype(jnp.bfloat16)

def brick_partials(collocation, blocks, diag_blocks):
    chosen = jnp.take(diag_blocks, blocks, axis=0).astype(jnp.float32)
    colloc_f = collocation.astype(jnp.float32)
    grid_density = lax.optimization_barrier(jnp.sum(jnp.einsum('tga,tab->tgb', colloc_f, chosen) * colloc_f, axis=-1))
    potential = grid_density / jnp.sqrt(1.0 + grid_density * grid_density)
    weighted = lax.optimization_barrier((potential[:, :, None] * colloc_f).astype(jnp.bfloat16)).astype(jnp.float32)
    prefactor = GRID_FACTOR * collocation.shape[2] / collocation.shape[1]
    return (prefactor * jnp.einsum('tga,tgb->tab', colloc_f, weighted)).astype(jnp.bfloat16)

def reference(density, core_hamiltonian, grid_term_old, lead_blocks, absorption, collocation, brick_block):
    block_rows = density.shape[1]
    band_reach = (density.shape[2] - 1) // 2
    block_width = density.shape[-1]
    rows_index = jnp.arange(block_rows, dtype=jnp.int32)
    equal = lead_blocks[None, :] == rows_index[:, None]
    gamma = lax.optimization_barrier(jnp.sum(jnp.where(equal, absorption[None, :], jnp.zeros((), absorption.dtype)), axis=1))
    symmetric_old = 0.5 * (grid_term_old + jnp.swapaxes(grid_term_old, 1, 2))
    hermit_old = add_diag(core_hamiltonian, symmetric_old)
    half_density = propagate(density, hermit_old, gamma)
    diag_blocks = half_density[0, :, band_reach]
    per_device = brick_block.shape[1] // N_COL
    blocks_grouped = brick_block.reshape(-1, per_device)
    colloc_grouped = collocation.reshape(blocks_grouped.shape[0], per_device, collocation.shape[1], block_width)
    partials = lax.map(lambda pair: brick_partials(pair[0], pair[1], diag_blocks), (colloc_grouped, blocks_grouped))
    grid_term = jax.ops.segment_sum(partials.reshape(-1, block_width, block_width).astype(jnp.float32), blocks_grouped.reshape(-1), num_segments=block_rows)
    hermit_new = add_diag(core_hamiltonian, grid_term)
    density_next = propagate(half_density, hermit_new, gamma)
    return (density_next, grid_term)
```

```python
import functools

import jax
import jax.numpy as jnp
from jax import lax
from jax.experimental import pallas as pl
from jax.experimental.pallas import tpu as pltpu
from jax.sharding import PartitionSpec as P

CAP = 3
HALF_STEP = 0.2
SECOND_ORDER = 0.5 * HALF_STEP * HALF_STEP
GRID_FACTOR = 0.1
F32 = jnp.float32
BF16 = jnp.bfloat16
VMEM_LIMIT = 60 * 1024 * 1024


def call(kernel, out_shape, flops, scalars=0, grid=(), in_specs=None, out_specs=None, scratch=()):
    whole = pl.BlockSpec(memory_space=pltpu.VMEM)
    return pl.pallas_call(
        kernel,
        out_shape=out_shape,
        grid_spec=pltpu.PrefetchScalarGridSpec(
            num_scalar_prefetch=scalars,
            grid=grid,
            in_specs=in_specs,
            out_specs=jax.tree.map(lambda _: whole, out_shape) if out_specs is None else out_specs,
            scratch_shapes=scratch,
        ),
        compiler_params=pltpu.CompilerParams(vmem_limit_bytes=VMEM_LIMIT),
        cost_estimate=pl.CostEstimate(flops=flops, bytes_accessed=4 << 20, transcendentals=0),
    )


def block_spec(shape, index):
    return pl.BlockSpec(shape, lambda *_: index)


def joined(re, im):
    return jnp.concatenate([re, im], axis=1)


def dagger(value):
    width = value.shape[0]
    re = value[:, :width].astype(F32).T
    im = value[:, width:].astype(F32).T
    return joined(re, -im).astype(BF16)


def as_right(value):
    width = value.shape[0]
    return jnp.concatenate([value, joined(-value[:, width:], value[:, :width])], axis=0)


def band_column(left, right, j, low, high):
    total = {}
    for mid in (j - 1, j, j + 1):
        rows = [i for i in range(max(mid, j) - 1, min(mid, j) + 2) if low <= i <= high]
        if not rows:
            continue
        stacked = jnp.concatenate([left(i, mid) for i in rows], axis=0)
        result = jnp.dot(stacked, as_right(right(mid, j)), preferred_element_type=F32)
        width = result.shape[0] // len(rows)
        for n, i in enumerate(rows):
            part = result[n * width : (n + 1) * width]
            total[i] = part if i not in total else total[i] + part
    return total


def times_i(value):
    width = value.shape[0]
    return joined(-value[:, width:], value[:, :width])


def propagate(count, get_q, get_left, get_right, hp_ref, moved_ref, wh_ref, write):
    def get(ref):
        return lambda i, j: ref[i + 1, j - i + 1]

    for j in range(-1, count + 1):
        for i, value in band_column(get_left, get_q, j, -1, count).items():
            hp_ref[i + 1, j - i + 1] = value.astype(BF16)
    for j in range(-1, count + 1):
        for i, value in band_column(get_left, get(hp_ref), j, 0, count - 1).items():
            hp = hp_ref[i + 1, j - i + 1].astype(F32)
            moved = get_q(i, j).astype(F32) - HALF_STEP * times_i(hp) - SECOND_ORDER * value
            moved_ref[i + 1, j - i + 1] = moved.astype(BF16)
    for j in range(-1, count + 1):
        for i, value in band_column(get(moved_ref), get_right, j, 0, count - 1).items():
            wh_ref[i + 1, j - i + 1] = value.astype(BF16)
    for j in range(-1, count + 1):
        for i, value in band_column(get(wh_ref), get_right, j, 0, count - 1).items():
            moved = moved_ref[i + 1, j - i + 1].astype(F32)
            wh = wh_ref[i + 1, j - i + 1].astype(F32)
            out = moved + HALF_STEP * times_i(wh) - SECOND_ORDER * value
            write(i, j, out.astype(BF16))


def symmetric(value):
    return 0.5 * (value + value.T)


def send_kernel(parity, q_hi, q_hi2, q_lo, q_lo2, h_hi, h_hi2, h_lo, h_lo2, g_hi, g_lo, send_a, send_b):
    def h_diag(h_ref, g_ref):
        return (h_ref[0, 0, 0].astype(F32) + symmetric(g_ref[0])).astype(BF16)

    right = [q_hi[0, 0, 0], q_hi[1, 0, 0], q_hi2[0, 0, 0], q_hi2[1, 0, 0],
             h_diag(h_hi, g_hi), h_hi[1, 0, 0], h_hi2[0, 0, 0], h_hi2[1, 0, 0], h_hi[0, 0, 0]]
    left = [q_lo[0, 0, 0], q_lo[1, 0, 0], q_lo2[0, 0, 0], q_lo2[1, 0, 0],
            h_diag(h_lo, g_lo), h_lo[1, 0, 0], h_lo2[0, 0, 0], h_lo2[1, 0, 0], h_lo[0, 0, 0]]
    even = parity[0] == 0

    @pl.when(even)
    def _():
        for n, (x, y) in enumerate(zip(right, left)):
            send_a[n] = x
            send_b[n] = y

    @pl.when(jnp.logical_not(even))
    def _():
        for n, (x, y) in enumerate(zip(right, left)):
            send_a[n] = y
            send_b[n] = x


def halo_reader(parity, got_a, got_b):
    even = parity[0] == 0

    def low(n):
        return jnp.where(even, got_b[n], got_a[n])

    def high(n):
        return jnp.where(even, got_a[n], got_b[n])

    return low, high


def set_diagonals(count, gamma, diag_re, diag_im, left_ref, right_ref):
    width = diag_re(0).shape[0]
    rows = lax.broadcasted_iota(jnp.int32, (width, width), 0)
    columns = lax.broadcasted_iota(jnp.int32, (width, width), 1)
    for i in range(-1, count + 1):
        re = diag_re(i)
        im = diag_im(i).astype(F32)
        shift = jnp.where(rows == columns, gamma[i + 1], 0.0)
        left_ref[i + 1] = joined(re, (im - shift).astype(BF16))
        right_ref[i + 1] = joined(re, (im + shift).astype(BF16))


def band_access(count, core, far_low, far_high, low_edge, high_edge, diag_ref):
    def get(i, j):
        if i == j:
            return diag_ref[i + 1]
        if i == -1:
            return far_low() if j == -2 else low_edge[...]
        if i == count:
            return far_high() if j == count + 1 else high_edge[...]
        return joined(core[0, i, j - i + 1], core[1, i, j - i + 1])

    return get


def first_kernel(count, parity, gamma, pick, dens, core, grid_old, got_a, got_b,
                 half, outgoing, send_a, send_b,
                 hp_ref, moved_ref, wh_ref, left_ref, right_ref, edges):
    low, high = halo_reader(parity, got_a, got_b)

    def band(ref, i, j):
        return joined(ref[0, i, j - i + 1], ref[1, i, j - i + 1])

    edges[0] = dagger(band(dens, 0, -1))
    edges[1] = dagger(band(dens, count - 1, count))
    edges[2] = dagger(band(core, 0, -1))
    edges[3] = dagger(band(core, count - 1, count))

    def get_q(i, j):
        if i == -2:
            return joined(low(2), low(3))
        if i == -1:
            return joined(low(0), low(1)) if j == -1 else edges[0]
        if i == count:
            return joined(high(0), high(1)) if j == count else edges[1]
        if i == count + 1:
            return joined(high(2), high(3))
        return band(dens, i, j)

    def diag_re(i):
        if i == -1:
            return low(4)
        if i == count:
            return high(4)
        return (core[0, i, 1].astype(F32) + symmetric(grid_old[i])).astype(BF16)

    def diag_im(i):
        return low(5) if i == -1 else high(5) if i == count else core[1, i, 1]

    set_diagonals(count, gamma, diag_re, diag_im, left_ref, right_ref)

    def far_low():
        return joined(low(6), low(7))

    def far_high():
        return joined(high(6), high(7))

    get_left = band_access(count, core, far_low, far_high, edges.at[2], edges.at[3], left_ref)
    get_right = band_access(count, core, far_low, far_high, edges.at[2], edges.at[3], right_ref)

    def write(i, j, value):
        width = value.shape[0]
        half[0, i, j - i + 1] = value[:, :width]
        half[1, i, j - i + 1] = value[:, width:]

    propagate(count, get_q, get_left, get_right, hp_ref, moved_ref, wh_ref, write)

    right = [(count - 1, 1), (count - 1, 2), (count - 2, 2)]
    left = [(0, 1), (0, 0), (1, 0)]

    def send(to_a, to_b):
        for n in range(3):
            for part in range(2):
                send_a[2 * n + part] = half[part, to_a[n][0], to_a[n][1]]
                send_b[2 * n + part] = half[part, to_b[n][0], to_b[n][1]]

    @pl.when(parity[0] == 0)
    def _():
        send(right, left)

    @pl.when(parity[0] != 0)
    def _():
        send(left, right)

    def place(n, carry):
        outgoing[n] = half[0, pick[n], 1]
        return carry

    lax.fori_loop(0, outgoing.shape[0], place, 0)


def brick_kernel(bricks, where_ref, colloc, incoming, returned):
    step = pl.program_id(0)
    points, width = colloc.shape[1:]
    slots = returned.shape[0]
    scale = GRID_FACTOR * width / points

    @pl.when(step == 0)
    def _():
        if slots > bricks:
            returned[...] = jnp.zeros_like(returned)

    c0, c1 = colloc[0], colloc[1]
    s0 = where_ref[2 * step]
    s1 = where_ref[2 * step + 1]
    q0 = incoming[s0].astype(F32).T
    q1 = incoming[s1].astype(F32).T
    zero = jnp.zeros_like(q0)
    both = jnp.concatenate([joined(q0, zero), joined(zero, q1)], axis=0).astype(BF16)
    turned = jnp.concatenate([c0.T, c1.T], axis=0)
    wide = turned.astype(F32)
    projected = jnp.dot(both, turned, preferred_element_type=F32) * wide
    weighted = []
    for n in range(2):
        rows = slice(n * width, (n + 1) * width)
        dens = jnp.sum(projected[rows], axis=0, keepdims=True)
        potential = dens * lax.rsqrt(1.0 + dens * dens)
        weighted.append((potential * wide[rows]).astype(BF16))
    result = jnp.dot(jnp.concatenate(weighted, axis=0), joined(c0, c1), preferred_element_type=F32)
    returned[s0] = (scale * result[:width, :width]).T.astype(BF16)
    returned[s1] = (scale * result[width:, width:]).T.astype(BF16)


def collect_kernel(count, parity, place, arriving, core, grid_term, send_a, send_b):
    grid_term[...] = jnp.zeros_like(grid_term)

    def add(n, carry):
        @pl.when(place[n] >= 0)
        def _():
            grid_term[place[n]] += arriving[n].astype(F32)

        return carry

    lax.fori_loop(0, arriving.shape[0], add, 0)
    right = (core[0, count - 1, 0].astype(F32) + grid_term[count - 1]).astype(BF16)
    left = (core[0, 0, 0].astype(F32) + grid_term[0]).astype(BF16)
    even = parity[0] == 0
    send_a[0] = jnp.where(even, right, left)
    send_b[0] = jnp.where(even, left, right)


def second_kernel(count, parity, gamma, half, core, grid_term, core_a, core_b, half_a, half_b, diag_a, diag_b,
                  out, hp_ref, moved_ref, wh_ref, left_ref, right_ref, edges):
    core_low, core_high = halo_reader(parity, core_a, core_b)
    half_low, half_high = halo_reader(parity, half_a, half_b)
    diag_low, diag_high = halo_reader(parity, diag_a, diag_b)

    def band(ref, i, j):
        return joined(ref[0, i, j - i + 1], ref[1, i, j - i + 1])

    edges[0] = dagger(band(core, 0, -1))
    edges[1] = dagger(band(core, count - 1, count))

    def get_q(i, j):
        if i < 0:
            n = 0 if i == -1 and j == -1 else 2 if i == -1 else 4
            return joined(half_low(n), half_low(n + 1))
        if i >= count:
            n = 0 if i == count and j == count else 2 if i == count else 4
            return joined(half_high(n), half_high(n + 1))
        return band(half, i, j)

    def diag_re(i):
        if i == -1:
            return diag_low(0)
        if i == count:
            return diag_high(0)
        return (core[0, i, 1].astype(F32) + grid_term[i]).astype(BF16)

    def diag_im(i):
        return core_low(5) if i == -1 else core_high(5) if i == count else core[1, i, 1]

    set_diagonals(count, gamma, diag_re, diag_im, left_ref, right_ref)

    def far_low():
        return joined(core_low(6), core_low(7))

    def far_high():
        return joined(core_high(6), core_high(7))

    get_left = band_access(count, core, far_low, far_high, edges.at[0], edges.at[1], left_ref)
    get_right = band_access(count, core, far_low, far_high, edges.at[0], edges.at[1], right_ref)

    def write(i, j, value):
        width = value.shape[0]
        out[0, i, j - i + 1] = value[:, :width]
        out[1, i, j - i + 1] = value[:, width:]

    propagate(count, get_q, get_left, get_right, hp_ref, moved_ref, wh_ref, write)


def rows_gamma(lead_blocks, absorption, first_row, row_count):
    rows_here = first_row + jnp.arange(row_count, dtype=jnp.int32)
    equal = lead_blocks[None, :] == rows_here[:, None]
    return jnp.sum(jnp.where(equal, absorption[None, :], 0.0), axis=1)


def exchange(send_a, send_b, total):
    first = [(i, i ^ 1) for i in range(total)]
    second = [(i, i + 1) if i % 2 else (i, i - 1) for i in range(1, total - 1)]
    axes = ("row", "col")
    return lax.ppermute(send_a, axes, first), lax.ppermute(send_b, axes, second)


def shards(density, core, grid_old, lead_blocks, absorption, collocation, brick_block):
    count = density.shape[1]
    width = density.shape[-1]
    row_size = lax.axis_size("row")
    col_size = lax.axis_size("col")
    total = row_size * col_size
    position = lax.axis_index(("row", "col"))
    parity = (position % 2).astype(jnp.int32).reshape(1)
    gamma = rows_gamma(lead_blocks, absorption, position * count - 1, count + 2)
    bricks = brick_block.shape[1]
    slots = row_size * CAP
    vmem = pl.BlockSpec(memory_space=pltpu.VMEM)

    own_row = lax.axis_index("row")
    source_row = brick_block // count // col_size
    local_block = brick_block % count
    earlier = jnp.arange(bricks)[None, :] < jnp.arange(bricks)[:, None]
    same_source = source_row[:, :, None] == source_row[:, None, :]
    slot_number = jnp.sum((same_source & earlier[None]).astype(jnp.int32), axis=2)
    own_source = lax.dynamic_index_in_dim(source_row, own_row, 0, keepdims=False)
    own_slot = lax.dynamic_index_in_dim(slot_number, own_row, 0, keepdims=False)
    where_own = own_source * CAP + own_slot
    mine = (source_row == own_row)[:, :, None] & (
        slot_number[:, :, None] == jnp.arange(CAP, dtype=jnp.int32)[None, None, :]
    )
    place = jnp.max(jnp.where(mine, local_block[:, :, None], -1), axis=1).reshape(slots)
    pick = jnp.maximum(place, 0)

    block = (2, 1, 1, width, width)
    grid_block = (1, width, width)
    last = count - 1
    message = jax.ShapeDtypeStruct((9, width, width), BF16)
    send_a, send_b = call(
        send_kernel,
        (message, message),
        flops=1 << 20,
        scalars=1,
        grid=(1,),
        in_specs=[block_spec(block, (0, i, k, 0, 0)) for i, k in
                  ((last, 1), (last - 1, 2), (0, 1), (1, 0), (last, 1), (last, 0), (0, 1), (0, 2))]
        + [block_spec(grid_block, (last, 0, 0)), block_spec(grid_block, (0, 0, 0))],
    )(parity, *([density] * 4), *([core] * 4), grid_old, grid_old)
    got_a, got_b = exchange(send_a, send_b, total)

    def band_scratch(rows):
        return pltpu.VMEM((rows, 3, width, 2 * width), BF16)

    prop_scratch = [band_scratch(count + 2)] * 3 + [pltpu.VMEM((count + 2, width, 2 * width), BF16)] * 2
    prop_flops = 8 * 7 * 4 * count * width**3
    half_message = jax.ShapeDtypeStruct((6, width, width), BF16)
    half, outgoing, send_a, send_b = call(
        functools.partial(first_kernel, count),
        (
            jax.ShapeDtypeStruct(density.shape, BF16),
            jax.ShapeDtypeStruct((slots, width, width), BF16),
            half_message,
            half_message,
        ),
        flops=prop_flops,
        scalars=3,
        in_specs=[vmem] * 5,
        scratch=prop_scratch + [pltpu.VMEM((4, width, 2 * width), BF16)],
    )(parity, gamma, pick, density, core, grid_old, got_a, got_b)

    incoming = lax.all_to_all(outgoing, "row", split_axis=0, concat_axis=0, tiled=True)
    half_a, half_b = exchange(send_a, send_b, total)

    points = collocation.shape[1]
    returned = call(
        functools.partial(brick_kernel, bricks),
        jax.ShapeDtypeStruct((slots, width, width), BF16),
        flops=4 * bricks * points * width**2,
        scalars=1,
        grid=(bricks // 2,),
        in_specs=[pl.BlockSpec((2, points, width), lambda t, *_: (t, 0, 0)), vmem],
    )(where_own, collocation, incoming)
    arriving = lax.all_to_all(returned, "row", split_axis=0, concat_axis=0, tiled=True)

    diag_message = jax.ShapeDtypeStruct((1, width, width), BF16)
    grid_term, send_a, send_b = call(
        functools.partial(collect_kernel, count),
        (jax.ShapeDtypeStruct((count, width, width), F32), diag_message, diag_message),
        flops=1 << 20,
        scalars=2,
        grid=(1,),
        in_specs=[vmem, block_spec((1, count, 1, width, width), (0, 0, 1, 0, 0))],
    )(parity, place, arriving, core)
    diag_a, diag_b = exchange(send_a, send_b, total)

    density_next = call(
        functools.partial(second_kernel, count),
        jax.ShapeDtypeStruct(density.shape, BF16),
        flops=prop_flops,
        scalars=2,
        in_specs=[vmem] * 9,
        scratch=prop_scratch + [pltpu.VMEM((2, width, 2 * width), BF16)],
    )(parity, gamma, half, core, grid_term, got_a, got_b, half_a, half_b, diag_a, diag_b)
    return (density_next, grid_term)


def solution(mesh):
    band = P(None, ("row", "col"), None, None, None)
    blocks = P(("row", "col"), None, None)
    return jax.shard_map(
        shards,
        mesh=mesh,
        in_specs=(band, band, blocks, P(), P(), blocks, P(None, "col")),
        out_specs=(band, blocks),
        check_vma=False,
    )
```

```python
import functools

import jax
import jax.numpy as jnp
from jax import lax
from jax.experimental import pallas as pl
from jax.experimental.pallas import tpu as pltpu
from jax.sharding import PartitionSpec as P

CAP = 3
HALF_STEP = 0.2
SECOND_ORDER = 0.5 * HALF_STEP * HALF_STEP
GRID_FACTOR = 0.1
F32 = jnp.float32
BF16 = jnp.bfloat16
PROP_FLOPS = 1 << 32
MIB = 1024 * 1024
TILE = 16


def call(kernel, out_shape, flops, vmem, scalars=0, grid=(), in_specs=None, out_specs=None, scratch=(), aliases={}):
    whole = pl.BlockSpec(memory_space=pltpu.VMEM)
    return pl.pallas_call(
        kernel,
        out_shape=out_shape,
        grid_spec=pltpu.PrefetchScalarGridSpec(
            num_scalar_prefetch=scalars,
            grid=grid,
            in_specs=in_specs,
            out_specs=jax.tree.map(lambda _: whole, out_shape) if out_specs is None else out_specs,
            scratch_shapes=scratch,
        ),
        input_output_aliases=aliases,
        compiler_params=pltpu.CompilerParams(vmem_limit_bytes=vmem * MIB),
        cost_estimate=pl.CostEstimate(flops=flops, bytes_accessed=4 << 20, transcendentals=0),
    )


def in_hbm(x):
    return pltpu.with_memory_space_constraint(x, pltpu.HBM)


def block_spec(shape, index):
    return pl.BlockSpec(shape, lambda *_: index)


def joined(re, im):
    return jnp.concatenate([re, im], axis=1)


def dagger(value):
    width = value.shape[0]
    re = value[:, :width].astype(F32).T
    im = value[:, width:].astype(F32).T
    return joined(re, -im).astype(BF16)


def as_right(value):
    width = value.shape[0]
    return jnp.concatenate([value, joined(-value[:, width:], value[:, :width])], axis=0)


def band_column(left, right, j, low, high):
    total = {}
    for mid in (j - 1, j, j + 1):
        rows = [i for i in range(max(mid, j) - 1, min(mid, j) + 2) if low <= i <= high]
        if not rows:
            continue
        stacked = jnp.concatenate([left(i, mid) for i in rows], axis=0)
        result = jnp.dot(stacked, as_right(right(mid, j)), preferred_element_type=F32)
        width = result.shape[0] // len(rows)
        for n, i in enumerate(rows):
            part = result[n * width : (n + 1) * width]
            total[i] = part if i not in total else total[i] + part
    return total


def times_i(value):
    width = value.shape[0]
    return joined(-value[:, width:], value[:, :width])


def taylor_first(columns, low, high, get_left, get_q, hp_ref):
    for j in columns:
        for i, value in band_column(get_left, get_q, j, low, high).items():
            hp_ref[i + 1, j - i + 1] = value.astype(BF16)


def propagate(low, high, get_q, get_hp, get_left, get_right, moved_ref, wh_ref, write):
    def get(ref):
        return lambda i, j: ref[i + 1, j - i + 1]

    columns = range(low - 1, high + 2)
    for j in columns:
        for i, value in band_column(get_left, get_hp, j, low, high).items():
            moved = get_q(i, j).astype(F32) - HALF_STEP * times_i(get_hp(i, j).astype(F32)) - SECOND_ORDER * value
            moved_ref[i + 1, j - i + 1] = moved.astype(BF16)
    for j in columns:
        for i, value in band_column(get(moved_ref), get_right, j, low, high).items():
            wh_ref[i + 1, j - i + 1] = value.astype(BF16)
    for j in columns:
        for i, value in band_column(get(wh_ref), get_right, j, low, high).items():
            moved = moved_ref[i + 1, j - i + 1].astype(F32)
            wh = wh_ref[i + 1, j - i + 1].astype(F32)
            write(i, j, (moved + HALF_STEP * times_i(wh) - SECOND_ORDER * value).astype(BF16))


def lanes_rows(shape):
    return lax.broadcasted_iota(jnp.int32, shape, 1), lax.broadcasted_iota(jnp.int32, shape, 0)


def pack_hermitian(re, im):
    lane, row = lanes_rows(re.shape)
    return jnp.where(row <= lane, re, im)


def unpack_hermitian(packed):
    lane, row = lanes_rows(packed.shape)
    packed = packed.astype(F32)
    turned = packed.T
    re = jnp.where(row <= lane, packed, turned)
    im = jnp.where(row > lane, packed, jnp.where(row < lane, -turned, 0.0))
    return joined(re, im).astype(BF16)


def pack_symmetric(block, folded):
    lane, row = lanes_rows(block.shape)
    half = block.shape[0] // 2
    both = jnp.where(lane == row, block, block + block.T) if folded else block
    lane, row = lanes_rows((half, block.shape[1]))
    packed = jnp.where(lane >= row, both[:half], pltpu.roll(both[half:], half, 1))
    diagonal = jnp.sum(jnp.where(lane == row + half, both[half:], 0.0), axis=0, keepdims=True)
    return packed, diagonal


def unpack_triangle(packed, diagonal):
    half, width = packed.shape
    lane, row = lanes_rows(packed.shape)
    top = jnp.where(lane >= row, packed, 0.0)
    below = jnp.where(lane < row + half, pltpu.roll(packed, half, 1), jnp.where(lane == row + half, diagonal, 0.0))
    return jnp.concatenate([top, jnp.where(lane < half, 0.0, below)], axis=0)


def symmetric(value):
    return 0.5 * (value + value.T)


def send_kernel(count, dens, core, grid_old, owners, send_a, send_b, place, sources, slots, bands, grids, sems):
    last = count - 1
    places = [(dens, last, 1), (dens, last - 1, 2), (core, last, 1), (core, last, 0),
              (dens, 0, 1), (dens, 1, 0), (core, 0, 1), (core, 0, 2)]
    copies = [
        pltpu.make_async_copy(ref.at[:, i, k], bands.at[n], sems.at[n]) for n, (ref, i, k) in enumerate(places)
    ]
    copies += [
        pltpu.make_async_copy(grid_old.at[i], grids.at[n], sems.at[8 + n]) for n, i in enumerate((last, 0))
    ]
    for copy in copies:
        copy.start()

    lane, _ = lanes_rows(owners.shape)
    source = owners[...] // count // lax.axis_size("col")
    slot = jnp.zeros(owners.shape, jnp.int32)
    for t in range(owners.shape[1] - 1):
        slot += jnp.where((lane > t) & (source == source[:, t : t + 1]), 1, 0)
    mine = jnp.where(source == lax.axis_index("row"), owners[...] % count, -1)
    table = jnp.zeros(owners.shape, jnp.int32)
    for n in range(CAP):
        table = jnp.where(lane == n, jnp.max(jnp.where(slot == n, mine, -1), axis=1, keepdims=True), table)
    place[...] = table
    sources[...] = source
    slots[...] = slot
    for copy in copies:
        copy.wait()

    def message(first, grid):
        h_re = (bands[first + 2, 0].astype(F32) + symmetric(grids[grid])).astype(BF16)
        return [pack_hermitian(bands[first, 0], bands[first, 1]), bands[first + 1, 0], bands[first + 1, 1],
                pack_hermitian(h_re, bands[first + 2, 1]), bands[first + 3, 0], bands[first + 3, 1]]

    right = message(0, 0)
    left = message(4, 1)
    even = lax.axis_index("col") % 2 == 0

    @pl.when(even)
    def _():
        for n, (x, y) in enumerate(zip(right, left)):
            send_a[n] = x
            send_b[n] = y

    @pl.when(jnp.logical_not(even))
    def _():
        for n, (x, y) in enumerate(zip(right, left)):
            send_a[n] = y
            send_b[n] = x


def halo_reader(got_a, got_b):
    even = lax.axis_index("col") % 2 == 0

    def low(n):
        return jnp.where(even, got_b[n], got_a[n])

    def high(n):
        return jnp.where(even, got_a[n], got_b[n])

    return low, high


def set_diagonals(rows, count, leads, absorption, diag_re, diag_im, left_ref, right_ref):
    width = left_ref.shape[1]
    lane, row = lanes_rows((width, width))
    first = (lax.axis_index("row") * lax.axis_size("col") + lax.axis_index("col")) * count
    for i in rows:
        re = diag_re(i)
        im = diag_im(i).astype(F32)
        gamma = jnp.float32(0.0)
        for n in range(leads.shape[0]):
            gamma += jnp.where(leads[n] == first + i, absorption[n], 0.0)
        shift = jnp.where(lane == row, gamma, 0.0)
        left_ref[i + 1] = joined(re, (im - shift).astype(BF16))
        right_ref[i + 1] = joined(re, (im + shift).astype(BF16))


def band_at(ref):
    return lambda i, j: joined(ref[0, i, j - i + 1], ref[1, i, j - i + 1])


def band_writer(ref):
    def write(i, j, value):
        width = value.shape[0]
        ref[0, i, j - i + 1] = value[:, :width]
        ref[1, i, j - i + 1] = value[:, width:]

    return write


def old_diagonals(rows, count, leads, absorption, core, grid_old, left_ref, right_ref, ends=None):
    width = core.shape[-1]

    def diag_re(i):
        if i == -1:
            return ends[0][:, :width]
        if i == count:
            return ends[1][:, :width]
        return (core[0, i, 1].astype(F32) + symmetric(grid_old[i])).astype(BF16)

    def diag_im(i):
        return ends[0][:, width:] if i == -1 else ends[1][:, width:] if i == count else core[1, i, 1]

    set_diagonals(rows, count, leads, absorption, diag_re, diag_im, left_ref, right_ref)


def new_diagonals(rows, count, leads, absorption, core, grid_term, left_ref, right_ref, ends=None, ends_re=None):
    width = core.shape[-1]

    def diag_re(i):
        if i == -1:
            return ends_re[0]
        if i == count:
            return ends_re[1]
        return (core[0, i, 1].astype(F32) + grid_term[i]).astype(BF16)

    def diag_im(i):
        return ends[0][:, width:] if i == -1 else ends[1][:, width:] if i == count else core[1, i, 1]

    set_diagonals(rows, count, leads, absorption, diag_re, diag_im, left_ref, right_ref)


def band_access(count, core, far_low, far_high, low_edge, high_edge, diag_ref):
    def get(i, j):
        if i == j:
            return diag_ref[i + 1]
        if i == -1:
            return far_low() if j == -2 else low_edge[...]
        if i == count:
            return far_high() if j == count + 1 else high_edge[...]
        return joined(core[0, i, j - i + 1], core[1, i, j - i + 1])

    return get


def first_inner_kernel(count, leads, absorption, dens, core, grid_old, hp_ref, half, moved_ref, wh_ref, left_ref, right_ref):
    old_diagonals(range(count), count, leads, absorption, core, grid_old, left_ref, right_ref)
    get_left = band_access(count, core, None, None, None, None, left_ref)
    get_right = band_access(count, core, None, None, None, None, right_ref)
    get_q = band_at(dens)

    def get_hp(i, j):
        return hp_ref[i + 1, j - i + 1]

    taylor_first(range(count), 1, count - 2, get_left, get_q, hp_ref)
    propagate(2, count - 3, get_q, get_hp, get_left, get_right, moved_ref, wh_ref, band_writer(half))


def first_outer_kernel(count, leads, absorption, place, dens, core, grid_old, got_a, got_b, hp_in, half_in,
                       half_out, outgoing, send_a_out, send_b_out,
                       hp_ref, moved_ref, wh_ref, left_ref, right_ref, edges, packed, diagonals, half, out_buf, send_a, send_b, sems):
    low, high = halo_reader(got_a, got_b)
    last = count - 1
    edges[0] = dagger(band_at(dens)(0, -1))
    edges[1] = dagger(band_at(dens)(last, count))
    edges[2] = dagger(band_at(core)(0, -1))
    edges[3] = dagger(band_at(core)(last, count))
    edges[4] = unpack_hermitian(low(0))
    edges[5] = unpack_hermitian(high(0))
    ends = unpack_hermitian(low(3)), unpack_hermitian(high(3))
    rows = [-1, 0, 1, 2, count - 3, count - 2, last, count]
    old_diagonals(rows, count, leads, absorption, core, grid_old, left_ref, right_ref, ends)
    half[:, 2 : count - 2] = half_in[:, 2 : count - 2]

    def get_q(i, j):
        if i == -2:
            return joined(low(1), low(2))
        if i == -1:
            return edges[4] if j == -1 else edges[0]
        if i == count:
            return edges[5] if j == count else edges[1]
        if i == count + 1:
            return joined(high(1), high(2))
        return band_at(dens)(i, j)

    def get_hp(i, j):
        ref = hp_in if 1 <= i <= count - 2 else hp_ref
        return ref[i + 1, j - i + 1]

    def far_low():
        return joined(low(4), low(5))

    def far_high():
        return joined(high(4), high(5))

    get_left = band_access(count, core, far_low, far_high, edges.at[2], edges.at[3], left_ref)
    get_right = band_access(count, core, far_low, far_high, edges.at[2], edges.at[3], right_ref)
    write = band_writer(half)
    taylor_first(range(-1, 2), -1, 0, get_left, get_q, hp_ref)
    taylor_first(range(last - 1, count + 1), last, count, get_left, get_q, hp_ref)
    propagate(0, 1, get_q, get_hp, get_left, get_right, moved_ref, wh_ref, write)
    propagate(last - 1, last, get_q, get_hp, get_left, get_right, moved_ref, wh_ref, write)
    copies = [pltpu.make_async_copy(half, half_out, sems.at[0])]
    copies[0].start()

    right = [(last, 1), (last, 2), (last - 1, 2)]
    left = [(0, 1), (0, 0), (1, 0)]

    def send(to_a, to_b):
        for n in range(3):
            for part in range(2):
                send_a[2 * n + part] = half[part, to_a[n][0], to_a[n][1]]
                send_b[2 * n + part] = half[part, to_b[n][0], to_b[n][1]]

    even = lax.axis_index("col") % 2 == 0

    @pl.when(even)
    def _():
        send(right, left)

    @pl.when(jnp.logical_not(even))
    def _():
        send(left, right)

    for source, target, n in ((send_a, send_a_out, 1), (send_b, send_b_out, 2)):
        copies.append(pltpu.make_async_copy(source, target, sems.at[n]))
        copies[-1].start()

    for i in range(count):
        top, diagonal = pack_symmetric(half[0, i, 1].astype(F32), True)
        packed[i] = top.astype(BF16)
        diagonals[i] = jnp.broadcast_to(diagonal, diagonals.shape[1:])

    height, width = packed.shape[1:]
    _, row = lanes_rows((TILE, width))

    def put(p, carry):
        tail = jnp.zeros((TILE, width), F32)
        for n in range(CAP):
            source = jnp.maximum(place[p, n], 0)
            out_buf[p, n * height : (n + 1) * height] = packed[source]
            tail = jnp.where(row == n, diagonals[source][:1], tail)
        out_buf[p, CAP * height :] = tail.astype(BF16)
        return carry

    lax.fori_loop(0, out_buf.shape[0], put, 0)
    copies.append(pltpu.make_async_copy(out_buf, outgoing, sems.at[3]))
    copies[-1].start()
    for copy in copies:
        copy.wait()


def brick_kernel(chunk, groups, sources, slots, far, incoming, returned, colloc, sems):
    bricks, points, width = colloc.shape
    own = lax.axis_index("row")
    scale = GRID_FACTOR * width / points
    height = width // 2
    tail = CAP * height
    _, tail_row = lanes_rows((TILE, width))

    loads = {
        start: pltpu.make_async_copy(far.at[pl.ds(start, size)], colloc.at[pl.ds(start, size)], sems.at[n])
        for n, (start, size) in enumerate(groups)
    }
    for load in loads.values():
        load.start()
    returned[...] = jnp.zeros_like(returned)

    def block(t):
        start = pl.multiple_of(slots[own, t] * height, height)
        diagonal = jnp.sum(
            jnp.where(tail_row == slots[own, t], incoming[sources[own, t], tail : tail + TILE].astype(F32), 0.0),
            axis=0,
            keepdims=True,
        )
        return unpack_triangle(incoming[sources[own, t], pl.ds(start, height)].astype(F32), diagonal)

    def put(t, result):
        start = pl.multiple_of(slots[own, t] * height, height)
        packed, diagonal = pack_symmetric(scale * result, False)
        returned[sources[own, t], pl.ds(start, height)] = packed.astype(BF16)
        old = returned[sources[own, t], tail : tail + TILE].astype(F32)
        returned[sources[own, t], tail : tail + TILE] = jnp.where(tail_row == slots[own, t], diagonal, old).astype(BF16)

    for t in range(0, bricks, 2):
        q0, q1 = block(t), block(t + 1)
        zero = jnp.zeros_like(q0)
        both = jnp.concatenate([joined(q0, zero), joined(zero, q1)], axis=0).astype(BF16)
        columns = []
        if t in loads:
            loads[t].wait()
        for g in range(0, points, chunk):
            turned = jnp.concatenate([colloc[t, g : g + chunk].T, colloc[t + 1, g : g + chunk].T], axis=0)
            wide = turned.astype(F32)
            projected = jnp.dot(both, turned, preferred_element_type=F32) * wide
            weighted = []
            for n in range(2):
                rows = slice(n * width, (n + 1) * width)
                dens = jnp.sum(projected[rows], axis=0, keepdims=True)
                potential = dens * lax.rsqrt(1.0 + dens * dens)
                weighted.append((potential * wide[rows]).astype(BF16))
            columns.append(jnp.concatenate(weighted, axis=0))
        result = jnp.dot(
            jnp.concatenate(columns, axis=1), joined(colloc[t], colloc[t + 1]), preferred_element_type=F32
        )
        put(t, result[:width, :width])
        put(t + 1, result[width:, width:])


def collect_kernel(count, place, arriving, core, grid_term, send_a, send_b, total, tails):
    width = arriving.shape[-1]
    height = width // 2
    total[...] = jnp.zeros_like(total)
    tails[...] = jnp.zeros_like(tails)

    def add(p, carry):
        last = arriving[p, CAP * height :].astype(F32)
        for n in range(CAP):
            at = place[p, n]

            @pl.when(at >= 0)
            def _():
                total[at] += arriving[p, n * height : (n + 1) * height].astype(F32)
                tails[at] += jnp.broadcast_to(last[n : n + 1], tails.shape[1:])

        return carry

    lax.fori_loop(0, arriving.shape[0], add, 0)
    lane, row = lanes_rows((width, width))
    for i in range(count):
        triangle = unpack_triangle(total[i], tails[i][:1])
        grid_term[i] = jnp.where(lane == row, triangle, triangle + triangle.T)
    right = (core[0, count - 1, 0].astype(F32) + grid_term[count - 1]).astype(BF16)
    left = (core[0, 0, 0].astype(F32) + grid_term[0]).astype(BF16)
    even = lax.axis_index("col") % 2 == 0
    send_a[0] = jnp.where(even, right, left)
    send_b[0] = jnp.where(even, left, right)


def half_access(count, half, half_a, half_b):
    low, high = halo_reader(half_a, half_b)

    def get_q(i, j):
        if i < 0:
            n = 0 if i == -1 and j == -1 else 2 if i == -1 else 4
            return joined(low(n), low(n + 1))
        if i >= count:
            n = 0 if i == count and j == count else 2 if i == count else 4
            return joined(high(n), high(n + 1))
        return band_at(half)(i, j)

    return get_q


def second_inner_kernel(count, leads, absorption, half, core, grid_term, half_a, half_b,
                        out, hp_ref, moved_ref, wh_ref, left_ref, right_ref):
    new_diagonals(range(count), count, leads, absorption, core, grid_term, left_ref, right_ref)
    get_left = band_access(count, core, None, None, None, None, left_ref)
    get_right = band_access(count, core, None, None, None, None, right_ref)
    get_q = half_access(count, half, half_a, half_b)

    def get_hp(i, j):
        return hp_ref[i + 1, j - i + 1]

    taylor_first(range(-1, count + 1), 0, count - 1, get_left, get_q, hp_ref)
    propagate(1, count - 2, get_q, get_hp, get_left, get_right, moved_ref, wh_ref, band_writer(out))


def second_outer_kernel(count, leads, absorption, half, core, grid_term, core_a, core_b, half_a, half_b, diag_a, diag_b,
                        hp_in, out_in, out, hp_ref, moved_ref, wh_ref, left_ref, right_ref, edges, ready, sems):
    core_low, core_high = halo_reader(core_a, core_b)
    diag_low, diag_high = halo_reader(diag_a, diag_b)
    last = count - 1
    edges[0] = dagger(band_at(core)(0, -1))
    edges[1] = dagger(band_at(core)(last, count))
    ends = unpack_hermitian(core_low(3)), unpack_hermitian(core_high(3))
    rows = [-1, 0, 1, count - 2, last, count]
    new_diagonals(rows, count, leads, absorption, core, grid_term, left_ref, right_ref, ends, (diag_low(0), diag_high(0)))
    get_q = half_access(count, half, half_a, half_b)

    def far_low():
        return joined(core_low(4), core_low(5))

    def far_high():
        return joined(core_high(4), core_high(5))

    get_left = band_access(count, core, far_low, far_high, edges.at[0], edges.at[1], left_ref)
    get_right = band_access(count, core, far_low, far_high, edges.at[0], edges.at[1], right_ref)

    def get_hp(i, j):
        ref = hp_in if 0 <= i < count else hp_ref
        return ref[i + 1, j - i + 1]

    def write(i, j, value):
        width = value.shape[0]
        n = 0 if i == 0 else 1
        ready[0, n, j - i + 1] = value[:, :width]
        ready[1, n, j - i + 1] = value[:, width:]

    taylor_first(range(-1, 1), -1, -1, get_left, get_q, hp_ref)
    taylor_first(range(last, count + 1), count, count, get_left, get_q, hp_ref)
    copies = []
    for n, i in enumerate((0, last)):
        propagate(i, i, get_q, get_hp, get_left, get_right, moved_ref, wh_ref, write)
        copies.append(pltpu.make_async_copy(ready.at[:, n], out.at[:, i], sems.at[n]))
        copies[-1].start()
    for copy in copies:
        copy.wait()


def exchange(send_a, send_b, total):
    first = [(i, i ^ 1) for i in range(total)]
    second = [(i, i + 1) if i % 2 else (i, i - 1) for i in range(1, total - 1)]
    axes = ("row", "col")
    return lax.ppermute(send_a, axes, first), lax.ppermute(send_b, axes, second)


def shards(density, core, grid_old, lead_blocks, absorption, collocation, brick_block):
    count = density.shape[1]
    width = density.shape[-1]
    row_size = lax.axis_size("row")
    total = row_size * lax.axis_size("col")
    bricks = brick_block.shape[1]
    vmem = pl.BlockSpec(memory_space=pltpu.VMEM)
    hbm = pl.BlockSpec(memory_space=pltpu.HBM)

    message = jax.ShapeDtypeStruct((6, width, width), BF16)
    table = jax.ShapeDtypeStruct(brick_block.shape, jnp.int32)
    send_a, send_b, place, sources, slots = call(
        functools.partial(send_kernel, count),
        (message, message, table, table, table),
        flops=1 << 20,
        vmem=8,
        in_specs=[hbm] * 3 + [vmem],
        scratch=[
            pltpu.VMEM((8, 2, width, width), BF16),
            pltpu.VMEM((2, width, width), F32),
            pltpu.SemaphoreType.DMA((10,)),
        ],
    )(*(in_hbm(x) for x in (density, core, grid_old)), brick_block)
    got_a, got_b = exchange(send_a, send_b, total)

    def band_scratch(rows):
        return pltpu.VMEM((rows, 3, width, 2 * width), BF16)

    def sides(n):
        return pltpu.VMEM((n, width, 2 * width), BF16)

    hp_shape = jax.ShapeDtypeStruct((count + 2, 3, width, 2 * width), BF16)
    inner_scratch = [band_scratch(count + 2)] * 2 + [sides(count + 2)] * 2
    outer_scratch = [band_scratch(count + 2)] * 3 + [sides(count + 2)] * 2
    hp, half_inner = call(
        functools.partial(first_inner_kernel, count),
        (hp_shape, jax.ShapeDtypeStruct(density.shape, BF16)),
        flops=PROP_FLOPS,
        vmem=16,
        scalars=2,
        in_specs=[vmem] * 3,
        scratch=inner_scratch,
    )(lead_blocks, absorption, density, core, grid_old)
    packed_rows = CAP * width // 2 + TILE
    packed_shape = jax.ShapeDtypeStruct((row_size, packed_rows, width), BF16)
    half_message = pltpu.HBM((6, width, width), BF16)
    half, outgoing, send_a, send_b = call(
        functools.partial(first_outer_kernel, count),
        (
            pltpu.HBM(density.shape, BF16),
            pltpu.HBM(packed_shape.shape, BF16),
            half_message,
            half_message,
        ),
        flops=PROP_FLOPS,
        vmem=20,
        scalars=3,
        in_specs=[vmem] * 7,
        scratch=outer_scratch
        + [
            pltpu.VMEM((6, width, 2 * width), BF16),
            pltpu.VMEM((count, width // 2, width), BF16),
            pltpu.VMEM((count, 8, width), F32),
            pltpu.VMEM(density.shape, BF16),
            pltpu.VMEM(packed_shape.shape, BF16),
            pltpu.VMEM(half_message.shape, BF16),
            pltpu.VMEM(half_message.shape, BF16),
            pltpu.SemaphoreType.DMA((4,)),
        ],
        out_specs=(hbm,) * 4,
    )(lead_blocks, absorption, place, density, core, grid_old, got_a, got_b, hp, half_inner)

    incoming = lax.all_to_all(outgoing, "row", split_axis=0, concat_axis=0, tiled=True)
    half_a, half_b = exchange(send_a, send_b, total)

    points = collocation.shape[1]
    ends = [0, bricks // 6, bricks // 2, bricks]
    groups = [(a, b - a) for a, b in zip(ends, ends[1:])]
    returned = call(
        functools.partial(brick_kernel, points // 4, groups),
        packed_shape,
        flops=4 * bricks * points * width**2,
        vmem=20,
        scalars=2,
        in_specs=[hbm, vmem],
        scratch=[pltpu.VMEM(collocation.shape, BF16), pltpu.SemaphoreType.DMA((3,))],
    )(sources, slots, in_hbm(collocation), incoming)
    arriving = lax.all_to_all(returned, "row", split_axis=0, concat_axis=0, tiled=True)

    diag_message = jax.ShapeDtypeStruct((1, width, width), BF16)
    grid_term, send_a, send_b = call(
        functools.partial(collect_kernel, count),
        (jax.ShapeDtypeStruct((count, width, width), F32), diag_message, diag_message),
        flops=1 << 20,
        vmem=8,
        scalars=1,
        grid=(1,),
        in_specs=[vmem, block_spec((1, count, 1, width, width), (0, 0, 1, 0, 0))],
        scratch=[pltpu.VMEM((count, width // 2, width), F32), pltpu.VMEM((count, 8, width), F32)],
    )(place, arriving, core)
    diag_a, diag_b = exchange(send_a, send_b, total)

    inner, hp = call(
        functools.partial(second_inner_kernel, count),
        (jax.ShapeDtypeStruct(density.shape, BF16), hp_shape),
        flops=PROP_FLOPS,
        vmem=16,
        scalars=2,
        in_specs=[vmem] * 5,
        scratch=inner_scratch,
    )(lead_blocks, absorption, half, core, grid_term, half_a, half_b)
    density_next = call(
        functools.partial(second_outer_kernel, count),
        pltpu.HBM(density.shape, BF16),
        flops=PROP_FLOPS,
        vmem=16,
        scalars=2,
        in_specs=[vmem] * 10 + [hbm],
        out_specs=hbm,
        scratch=outer_scratch + [sides(2), pltpu.VMEM((2, 2, 3, width, width), BF16), pltpu.SemaphoreType.DMA((2,))],
        aliases={12: 0},
    )(lead_blocks, absorption, half, core, grid_term, got_a, got_b, half_a, half_b, diag_a, diag_b, hp, in_hbm(inner))
    return (density_next, grid_term)


def solution(mesh):
    band = P(None, ("row", "col"), None, None, None)
    blocks = P(("row", "col"), None, None)
    return jax.shard_map(
        shards,
        mesh=mesh,
        in_specs=(band, band, blocks, P(), P(), blocks, P(None, "col")),
        out_specs=(band, blocks),
        check_vma=False,
    )
```

```python
import functools

import jax
import jax.numpy as jnp
from jax import lax
from jax.experimental import pallas as pl
from jax.experimental.pallas import tpu as pltpu
from jax.sharding import PartitionSpec as P

CAP = 3
HALF_STEP = 0.2
SECOND_ORDER = 0.5 * HALF_STEP * HALF_STEP
GRID_FACTOR = 0.1
F32 = jnp.float32
BF16 = jnp.bfloat16
PROP_FLOPS = 1 << 32
MIB = 1024 * 1024
TILE = 16


def call(kernel, out_shape, flops, vmem, scalars=0, grid=(), in_specs=None, out_specs=None, scratch=(), aliases={}):
    whole = pl.BlockSpec(memory_space=pltpu.VMEM)
    return pl.pallas_call(
        kernel,
        out_shape=out_shape,
        grid_spec=pltpu.PrefetchScalarGridSpec(
            num_scalar_prefetch=scalars,
            grid=grid,
            in_specs=in_specs,
            out_specs=jax.tree.map(lambda _: whole, out_shape) if out_specs is None else out_specs,
            scratch_shapes=scratch,
        ),
        input_output_aliases=aliases,
        compiler_params=pltpu.CompilerParams(vmem_limit_bytes=vmem * MIB),
        cost_estimate=pl.CostEstimate(flops=flops, bytes_accessed=4 << 20, transcendentals=0),
    )


def in_hbm(x):
    return pltpu.with_memory_space_constraint(x, pltpu.HBM)


def block_spec(shape, index):
    return pl.BlockSpec(shape, lambda *_: index)


def joined(re, im):
    return jnp.concatenate([re, im], axis=1)


def dagger(value):
    width = value.shape[0]
    re = value[:, :width].astype(F32).T
    im = value[:, width:].astype(F32).T
    return joined(re, -im).astype(BF16)


def as_right(value):
    width = value.shape[0]
    return jnp.concatenate([value, joined(-value[:, width:], value[:, :width])], axis=0)


def band_column(left, right, j, low, high):
    total = {}
    for mid in (j - 1, j, j + 1):
        rows = [i for i in range(max(mid, j) - 1, min(mid, j) + 2) if low <= i <= high]
        if not rows:
            continue
        stacked = jnp.concatenate([left(i, mid) for i in rows], axis=0)
        result = jnp.dot(stacked, as_right(right(mid, j)), preferred_element_type=F32)
        width = result.shape[0] // len(rows)
        for n, i in enumerate(rows):
            part = result[n * width : (n + 1) * width]
            total[i] = part if i not in total else total[i] + part
    return total


def times_i(value):
    width = value.shape[0]
    return joined(-value[:, width:], value[:, :width])


def taylor_first(columns, low, high, get_left, get_q, hp_ref):
    for j in columns:
        for i, value in band_column(get_left, get_q, j, low, high).items():
            hp_ref[i + 1, j - i + 1] = value.astype(BF16)


def propagate(ranges, get_q, get_hp, get_left, get_right, moved_ref, wh_ref, write):
    def get(ref):
        return lambda i, j: ref[i + 1, j - i + 1]

    def product(left, right):
        for low, high in ranges:
            for j in range(low - 1, high + 2):
                for i, value in band_column(left, right, j, low, high).items():
                    yield i, j, value

    for i, j, value in product(get_left, get_hp):
        moved = get_q(i, j).astype(F32) - HALF_STEP * times_i(get_hp(i, j).astype(F32)) - SECOND_ORDER * value
        moved_ref[i + 1, j - i + 1] = moved.astype(BF16)
    for i, j, value in product(get(moved_ref), get_right):
        wh_ref[i + 1, j - i + 1] = value.astype(BF16)
    for i, j, value in product(get(wh_ref), get_right):
        moved = moved_ref[i + 1, j - i + 1].astype(F32)
        wh = wh_ref[i + 1, j - i + 1].astype(F32)
        write(i, j, (moved + HALF_STEP * times_i(wh) - SECOND_ORDER * value).astype(BF16))


def lanes_rows(shape):
    return lax.broadcasted_iota(jnp.int32, shape, 1), lax.broadcasted_iota(jnp.int32, shape, 0)


def pack_hermitian(re, im):
    lane, row = lanes_rows(re.shape)
    return jnp.where(row <= lane, re, im)


def unpack_hermitian(packed):
    lane, row = lanes_rows(packed.shape)
    packed = packed.astype(F32)
    turned = packed.T
    re = jnp.where(row <= lane, packed, turned)
    im = jnp.where(row > lane, packed, jnp.where(row < lane, -turned, 0.0))
    return joined(re, im).astype(BF16)


def pack_symmetric(block, folded):
    lane, row = lanes_rows(block.shape)
    half = block.shape[0] // 2
    both = jnp.where(lane == row, block, block + block.T) if folded else block
    lane, row = lanes_rows((half, block.shape[1]))
    packed = jnp.where(lane >= row, both[:half], pltpu.roll(both[half:], half, 1))
    diagonal = jnp.sum(jnp.where(lane == row + half, both[half:], 0.0), axis=0, keepdims=True)
    return packed, diagonal


def unpack_triangle(packed, diagonal):
    half, width = packed.shape
    lane, row = lanes_rows(packed.shape)
    top = jnp.where(lane >= row, packed, 0.0)
    below = jnp.where(lane < row + half, pltpu.roll(packed, half, 1), jnp.where(lane == row + half, diagonal, 0.0))
    return jnp.concatenate([top, jnp.where(lane < half, 0.0, below)], axis=0)


def symmetric(value):
    return 0.5 * (value + value.T)


def send_kernel(count, dens, core, grid_old, send_a, send_b, bands, grids, sems):
    last = count - 1
    places = [(dens, last, 1), (dens, last - 1, 2), (core, last, 1), (core, last, 0),
              (dens, 0, 1), (dens, 1, 0), (core, 0, 1), (core, 0, 2)]
    copies = [
        pltpu.make_async_copy(ref.at[:, i, k], bands.at[n], sems.at[n]) for n, (ref, i, k) in enumerate(places)
    ]
    copies += [
        pltpu.make_async_copy(grid_old.at[i], grids.at[n], sems.at[8 + n]) for n, i in enumerate((last, 0))
    ]
    for copy in copies:
        copy.start()
    for copy in copies:
        copy.wait()

    def message(first, grid):
        h_re = (bands[first + 2, 0].astype(F32) + symmetric(grids[grid])).astype(BF16)
        return [pack_hermitian(bands[first, 0], bands[first, 1]), bands[first + 1, 0], bands[first + 1, 1],
                pack_hermitian(h_re, bands[first + 2, 1]), bands[first + 3, 0], bands[first + 3, 1]]

    right = message(0, 0)
    left = message(4, 1)
    even = lax.axis_index("col") % 2 == 0

    @pl.when(even)
    def _():
        for n, (x, y) in enumerate(zip(right, left)):
            send_a[n] = x
            send_b[n] = y

    @pl.when(jnp.logical_not(even))
    def _():
        for n, (x, y) in enumerate(zip(right, left)):
            send_a[n] = y
            send_b[n] = x


def halo_reader(got_a, got_b):
    even = lax.axis_index("col") % 2 == 0

    def low(n):
        return jnp.where(even, got_b[n], got_a[n])

    def high(n):
        return jnp.where(even, got_a[n], got_b[n])

    return low, high


def set_diagonals(rows, count, leads, absorption, diag_re, diag_im, left_ref, right_ref):
    width = left_ref.shape[1]
    lane, row = lanes_rows((width, width))
    first = (lax.axis_index("row") * lax.axis_size("col") + lax.axis_index("col")) * count
    for i in rows:
        re = diag_re(i)
        im = diag_im(i).astype(F32)
        gamma = jnp.float32(0.0)
        for n in range(leads.shape[0]):
            gamma += jnp.where(leads[n] == first + i, absorption[n], 0.0)
        shift = jnp.where(lane == row, gamma, 0.0)
        left_ref[i + 1] = joined(re, (im - shift).astype(BF16))
        right_ref[i + 1] = joined(re, (im + shift).astype(BF16))


def band_at(ref):
    return lambda i, j: joined(ref[0, i, j - i + 1], ref[1, i, j - i + 1])


def band_writer(ref):
    def write(i, j, value):
        width = value.shape[0]
        ref[0, i, j - i + 1] = value[:, :width]
        ref[1, i, j - i + 1] = value[:, width:]

    return write


def old_diagonals(rows, count, leads, absorption, core, grid_old, left_ref, right_ref, ends=None):
    width = core.shape[-1]

    def diag_re(i):
        if i == -1:
            return ends[0][:, :width]
        if i == count:
            return ends[1][:, :width]
        return (core[0, i, 1].astype(F32) + symmetric(grid_old[i])).astype(BF16)

    def diag_im(i):
        return ends[0][:, width:] if i == -1 else ends[1][:, width:] if i == count else core[1, i, 1]

    set_diagonals(rows, count, leads, absorption, diag_re, diag_im, left_ref, right_ref)


def new_diagonals(rows, count, leads, absorption, core, diag_new, left_ref, right_ref, ends=None, ends_re=None):
    width = core.shape[-1]

    def diag_re(i):
        if i == -1:
            return ends_re[0]
        if i == count:
            return ends_re[1]
        return diag_new[i]

    def diag_im(i):
        return ends[0][:, width:] if i == -1 else ends[1][:, width:] if i == count else core[1, i, 1]

    set_diagonals(rows, count, leads, absorption, diag_re, diag_im, left_ref, right_ref)


def band_access(count, core, far_low, far_high, low_edge, high_edge, diag_ref):
    def get(i, j):
        if i == j:
            return diag_ref[i + 1]
        if i == -1:
            return far_low() if j == -2 else low_edge[...]
        if i == count:
            return far_high() if j == count + 1 else high_edge[...]
        return joined(core[0, i, j - i + 1], core[1, i, j - i + 1])

    return get


def brick_tables(count, owners, place, which):
    lane, row = lanes_rows(owners.shape)
    own = lax.axis_index("row")
    source = owners[...] // count // lax.axis_size("col")
    slot = jnp.zeros(owners.shape, jnp.int32)
    for t in range(owners.shape[1] - 1):
        slot += jnp.where((lane > t) & (source == source[:, t : t + 1]), 1, 0)
    mine = jnp.where(source == own, owners[...] % count, -1)
    own_source = jnp.sum(jnp.where(row == own, source, 0), axis=0, keepdims=True)
    own_slot = jnp.sum(jnp.where(row == own, slot, 0), axis=0, keepdims=True)
    here = own_source == row
    places = jnp.zeros(owners.shape, jnp.int32)
    bricks = jnp.zeros(owners.shape, jnp.int32)
    for n in range(CAP):
        places = jnp.where(lane == n, jnp.max(jnp.where(slot == n, mine, -1), axis=1, keepdims=True), places)
        brick = jnp.max(jnp.where(here & (own_slot == n), lane, 0), axis=1, keepdims=True)
        bricks = jnp.where(lane == n, brick, bricks)
    place[...] = places
    which[...] = bricks


def first_inner_kernel(count, leads, absorption, dens, core, grid_old, owners, hp_ref, half, place, which, moved_ref, wh_ref, left_ref, right_ref):
    brick_tables(count, owners, place, which)
    old_diagonals(range(count), count, leads, absorption, core, grid_old, left_ref, right_ref)
    get_left = band_access(count, core, None, None, None, None, left_ref)
    get_right = band_access(count, core, None, None, None, None, right_ref)
    get_q = band_at(dens)

    def get_hp(i, j):
        return hp_ref[i + 1, j - i + 1]

    taylor_first(range(count), 1, count - 2, get_left, get_q, hp_ref)
    propagate([(2, count - 3)], get_q, get_hp, get_left, get_right, moved_ref, wh_ref, band_writer(half))


def first_outer_kernel(count, leads, absorption, place, dens, core, grid_old, got_a, got_b, hp_in, half_in,
                       half, send_a, send_b, *rest):
    outgoing, (hp_ref, moved_ref, wh_ref, left_ref, right_ref, edges, packed, diagonals) = rest[:-8], rest[-8:]
    low, high = halo_reader(got_a, got_b)
    last = count - 1
    edges[0] = dagger(band_at(dens)(0, -1))
    edges[1] = dagger(band_at(dens)(last, count))
    edges[2] = dagger(band_at(core)(0, -1))
    edges[3] = dagger(band_at(core)(last, count))
    edges[4] = unpack_hermitian(low(0))
    edges[5] = unpack_hermitian(high(0))
    ends = unpack_hermitian(low(3)), unpack_hermitian(high(3))
    rows = [-1, 0, 1, 2, count - 3, count - 2, last, count]
    old_diagonals(rows, count, leads, absorption, core, grid_old, left_ref, right_ref, ends)
    half[:, 2 : count - 2] = half_in[:, 2 : count - 2]

    def get_q(i, j):
        if i == -2:
            return joined(low(1), low(2))
        if i == -1:
            return edges[4] if j == -1 else edges[0]
        if i == count:
            return edges[5] if j == count else edges[1]
        if i == count + 1:
            return joined(high(1), high(2))
        return band_at(dens)(i, j)

    def get_hp(i, j):
        ref = hp_in if 1 <= i <= count - 2 else hp_ref
        return ref[i + 1, j - i + 1]

    def far_low():
        return joined(low(4), low(5))

    def far_high():
        return joined(high(4), high(5))

    get_left = band_access(count, core, far_low, far_high, edges.at[2], edges.at[3], left_ref)
    get_right = band_access(count, core, far_low, far_high, edges.at[2], edges.at[3], right_ref)
    write = band_writer(half)
    taylor_first(range(-1, 2), -1, 0, get_left, get_q, hp_ref)
    taylor_first(range(last - 1, count + 1), last, count, get_left, get_q, hp_ref)
    propagate([(0, 1), (last - 1, last)], get_q, get_hp, get_left, get_right, moved_ref, wh_ref, write)

    right = [(last, 1), (last, 2), (last - 1, 2)]
    left = [(0, 1), (0, 0), (1, 0)]

    def send(to_a, to_b):
        for n in range(3):
            for part in range(2):
                send_a[2 * n + part] = half[part, to_a[n][0], to_a[n][1]]
                send_b[2 * n + part] = half[part, to_b[n][0], to_b[n][1]]

    even = lax.axis_index("col") % 2 == 0

    @pl.when(even)
    def _():
        send(right, left)

    @pl.when(jnp.logical_not(even))
    def _():
        send(left, right)

    for i in range(count):
        top, diagonal = pack_symmetric(half[0, i, 1].astype(F32), True)
        packed[i] = top.astype(BF16)
        diagonals[i] = jnp.broadcast_to(diagonal, diagonals.shape[1:])

    height, width = packed.shape[1:]
    _, row = lanes_rows((TILE, width))

    for offset, out in enumerate(outgoing):
        p = lax.axis_index("row") ^ offset
        tail = jnp.zeros((TILE, width), F32)
        for n in range(CAP):
            source = jnp.maximum(place[p, n], 0)
            out[n * height : (n + 1) * height] = packed[source]
            tail = jnp.where(row == n, diagonals[source][:1], tail)
        out[CAP * height :] = tail.astype(BF16)


def brick_kernel(chunk, offsets, which, colloc, *rest):
    incoming, returned = rest[: len(offsets)], rest[len(offsets) :]
    points, width = colloc.shape[1:]
    scale = GRID_FACTOR * width / points
    height = width // 2
    _, tail_row = lanes_rows((TILE, width))
    tails = [jnp.zeros((TILE, width), F32) for _ in offsets]
    jobs = [(m, n, which[lax.axis_index("row") ^ offset, n]) for m, offset in enumerate(offsets) for n in range(CAP)]

    def block(job):
        m, n, _ = job
        last = incoming[m][CAP * height :].astype(F32)
        return unpack_triangle(incoming[m][n * height : (n + 1) * height].astype(F32), last[n : n + 1])

    def put(job, result):
        m, n, _ = job
        packed, diagonal = pack_symmetric(scale * result, False)
        returned[m][n * height : (n + 1) * height] = packed.astype(BF16)
        tails[m] = jnp.where(tail_row == n, diagonal, tails[m])

    for first, second in zip(jobs[::2], jobs[1::2]):
        c0, c1 = colloc.at[first[2]], colloc.at[second[2]]
        q0, q1 = block(first), block(second)
        zero = jnp.zeros_like(q0)
        both = jnp.concatenate([joined(q0, zero), joined(zero, q1)], axis=0).astype(BF16)
        columns = []
        for g in range(0, points, chunk):
            turned = jnp.concatenate([c0[g : g + chunk].T, c1[g : g + chunk].T], axis=0)
            wide = turned.astype(F32)
            projected = jnp.dot(both, turned, preferred_element_type=F32) * wide
            weighted = []
            for n in range(2):
                rows = slice(n * width, (n + 1) * width)
                dens = jnp.sum(projected[rows], axis=0, keepdims=True)
                potential = dens * lax.rsqrt(1.0 + dens * dens)
                weighted.append((potential * wide[rows]).astype(BF16))
            columns.append(jnp.concatenate(weighted, axis=0))
        result = jnp.dot(jnp.concatenate(columns, axis=1), joined(c0[...], c1[...]), preferred_element_type=F32)
        put(first, result[:width, :width])
        put(second, result[width:, width:])
    for out, tail in zip(returned, tails):
        out[CAP * height :] = tail.astype(BF16)


def collect_kernel(count, place, core, *rest):
    arriving, (grid_term, diag_new, send_a, send_b, total, tails) = rest[:-6], rest[-6:]
    width = core.shape[-1]
    height = width // 2
    total[...] = jnp.zeros_like(total)
    tails[...] = jnp.zeros_like(tails)
    for offset, block in enumerate(arriving):
        p = lax.axis_index("row") ^ offset
        last = block[CAP * height :].astype(F32)
        for n in range(CAP):
            at = place[p, n]
            kept = at >= 0
            at = jnp.maximum(at, 0)
            total[at] += jnp.where(kept, block[n * height : (n + 1) * height].astype(F32), 0.0)
            tails[at] += jnp.where(kept, last[n : n + 1], 0.0)
    lane, row = lanes_rows((width, width))
    for i in range(count):
        triangle = unpack_triangle(total[i], tails[i][:1])
        term = jnp.where(lane == row, triangle, triangle + triangle.T)
        grid_term[i] = term
        diag_new[i] = (core[0, i, 0].astype(F32) + term).astype(BF16)
    right, left = diag_new[count - 1], diag_new[0]
    even = lax.axis_index("col") % 2 == 0
    send_a[0] = jnp.where(even, right, left)
    send_b[0] = jnp.where(even, left, right)


def half_access(count, half, half_a, half_b):
    low, high = halo_reader(half_a, half_b)

    def get_q(i, j):
        if i < 0:
            n = 0 if i == -1 and j == -1 else 2 if i == -1 else 4
            return joined(low(n), low(n + 1))
        if i >= count:
            n = 0 if i == count and j == count else 2 if i == count else 4
            return joined(high(n), high(n + 1))
        return band_at(half)(i, j)

    return get_q


def second_inner_kernel(count, leads, absorption, half, core, diag_new, half_a, half_b,
                        out, hp_ref, moved_ref, wh_ref, left_ref, right_ref):
    new_diagonals(range(count), count, leads, absorption, core, diag_new, left_ref, right_ref)
    get_left = band_access(count, core, None, None, None, None, left_ref)
    get_right = band_access(count, core, None, None, None, None, right_ref)
    get_q = half_access(count, half, half_a, half_b)

    def get_hp(i, j):
        return hp_ref[i + 1, j - i + 1]

    taylor_first(range(-1, count + 1), 0, count - 1, get_left, get_q, hp_ref)
    propagate([(1, count - 2)], get_q, get_hp, get_left, get_right, moved_ref, wh_ref, band_writer(out))


def second_outer_kernel(count, leads, absorption, half, core, diag_new, core_a, core_b, half_a, half_b, diag_a, diag_b,
                        hp_in, out_in, out, hp_ref, moved_ref, wh_ref, left_ref, right_ref, edges, ready, sems):
    core_low, core_high = halo_reader(core_a, core_b)
    diag_low, diag_high = halo_reader(diag_a, diag_b)
    last = count - 1
    edges[0] = dagger(band_at(core)(0, -1))
    edges[1] = dagger(band_at(core)(last, count))
    ends = unpack_hermitian(core_low(3)), unpack_hermitian(core_high(3))
    rows = [-1, 0, 1, count - 2, last, count]
    new_diagonals(rows, count, leads, absorption, core, diag_new, left_ref, right_ref, ends, (diag_low(0), diag_high(0)))
    get_q = half_access(count, half, half_a, half_b)

    def far_low():
        return joined(core_low(4), core_low(5))

    def far_high():
        return joined(core_high(4), core_high(5))

    get_left = band_access(count, core, far_low, far_high, edges.at[0], edges.at[1], left_ref)
    get_right = band_access(count, core, far_low, far_high, edges.at[0], edges.at[1], right_ref)

    def get_hp(i, j):
        ref = hp_in if 0 <= i < count else hp_ref
        return ref[i + 1, j - i + 1]

    def write(i, j, value):
        width = value.shape[0]
        n = 0 if i == 0 else 1
        ready[0, n, j - i + 1] = value[:, :width]
        ready[1, n, j - i + 1] = value[:, width:]

    taylor_first(range(-1, 1), -1, -1, get_left, get_q, hp_ref)
    taylor_first(range(last, count + 1), count, count, get_left, get_q, hp_ref)
    propagate([(0, 0), (last, last)], get_q, get_hp, get_left, get_right, moved_ref, wh_ref, write)
    copies = []
    for n, i in enumerate((0, last)):
        copies.append(pltpu.make_async_copy(ready.at[:, n], out.at[:, i], sems.at[n]))
        copies[-1].start()
    for copy in copies:
        copy.wait()


def exchange(send_a, send_b, total):
    first = [(i, i ^ 1) for i in range(total)]
    second = [(i, i + 1) if i % 2 else (i, i - 1) for i in range(1, total - 1)]
    axes = ("row", "col")
    return lax.ppermute(send_a, axes, first), lax.ppermute(send_b, axes, second)


def shards(density, core, grid_old, lead_blocks, absorption, collocation, brick_block):
    count = density.shape[1]
    width = density.shape[-1]
    row_size = lax.axis_size("row")
    total = row_size * lax.axis_size("col")
    bricks = brick_block.shape[1]
    vmem = pl.BlockSpec(memory_space=pltpu.VMEM)
    hbm = pl.BlockSpec(memory_space=pltpu.HBM)

    message = jax.ShapeDtypeStruct((6, width, width), BF16)
    table = jax.ShapeDtypeStruct(brick_block.shape, jnp.int32)
    send_a, send_b = call(
        functools.partial(send_kernel, count),
        (message, message),
        flops=1 << 20,
        vmem=8,
        in_specs=[hbm] * 3,
        scratch=[
            pltpu.VMEM((8, 2, width, width), BF16),
            pltpu.VMEM((2, width, width), F32),
            pltpu.SemaphoreType.DMA((10,)),
        ],
    )(*(in_hbm(x) for x in (density, core, grid_old)))
    got_a, got_b = exchange(send_a, send_b, total)

    def band_scratch(rows):
        return pltpu.VMEM((rows, 3, width, 2 * width), BF16)

    def sides(n):
        return pltpu.VMEM((n, width, 2 * width), BF16)

    hp_shape = jax.ShapeDtypeStruct((count + 2, 3, width, 2 * width), BF16)
    inner_scratch = [band_scratch(count + 2)] * 2 + [sides(count + 2)] * 2
    outer_scratch = [band_scratch(count + 2)] * 3 + [sides(count + 2)] * 2
    hp, half_inner, place, which = call(
        functools.partial(first_inner_kernel, count),
        (hp_shape, jax.ShapeDtypeStruct(density.shape, BF16), table, table),
        flops=PROP_FLOPS,
        vmem=16,
        scalars=2,
        in_specs=[vmem] * 4,
        scratch=inner_scratch,
    )(lead_blocks, absorption, density, core, grid_old, brick_block)
    packed_rows = CAP * width // 2 + TILE
    packed_shape = jax.ShapeDtypeStruct((packed_rows, width), BF16)
    half_message = jax.ShapeDtypeStruct((6, width, width), BF16)
    half, send_a, send_b, *outgoing = call(
        functools.partial(first_outer_kernel, count),
        (
            jax.ShapeDtypeStruct(density.shape, BF16),
            half_message,
            half_message,
        )
        + (packed_shape,) * row_size,
        flops=PROP_FLOPS,
        vmem=20,
        scalars=3,
        in_specs=[vmem] * 7,
        scratch=outer_scratch
        + [
            pltpu.VMEM((6, width, 2 * width), BF16),
            pltpu.VMEM((count, width // 2, width), BF16),
            pltpu.VMEM((count, 8, width), F32),
        ],
    )(lead_blocks, absorption, place, density, core, grid_old, got_a, got_b, hp, half_inner)

    half_a, half_b = exchange(send_a, send_b, total)

    def across(x, offset):
        return lax.ppermute(x, "row", [(i, i ^ offset) for i in range(row_size)]) if offset else x

    order = [0] + list(range(row_size // 2, row_size)) + list(range(1, row_size // 2))
    incoming = {offset: across(outgoing[offset], offset) for offset in order}
    points = collocation.shape[1]
    arriving = {}
    for offsets in zip(order[::2], order[1::2]):
        returned = call(
            functools.partial(brick_kernel, points // 4, offsets),
            (packed_shape,) * 2,
            flops=4 * 6 * points * width**2,
            vmem=8,
            scalars=1,
            in_specs=[vmem] * 3,
        )(which, collocation, *(incoming[offset] for offset in offsets))
        for offset, x in zip(offsets, returned):
            arriving[offset] = across(x, offset)

    diag_message = jax.ShapeDtypeStruct((1, width, width), BF16)
    grid_term, diag_new, send_a, send_b = call(
        functools.partial(collect_kernel, count),
        (
            jax.ShapeDtypeStruct((count, width, width), F32),
            jax.ShapeDtypeStruct((count, width, width), BF16),
            diag_message,
            diag_message,
        ),
        flops=1 << 20,
        vmem=8,
        scalars=1,
        grid=(1,),
        in_specs=[block_spec((1, count, 1, width, width), (0, 0, 1, 0, 0))] + [vmem] * row_size,
        scratch=[pltpu.VMEM((count, width // 2, width), F32), pltpu.VMEM((count, 8, width), F32)],
    )(place, core, *(arriving[offset] for offset in range(row_size)))
    diag_a, diag_b = exchange(send_a, send_b, total)

    inner, hp = call(
        functools.partial(second_inner_kernel, count),
        (jax.ShapeDtypeStruct(density.shape, BF16), hp_shape),
        flops=PROP_FLOPS,
        vmem=16,
        scalars=2,
        in_specs=[vmem] * 5,
        scratch=inner_scratch,
    )(lead_blocks, absorption, half, core, diag_new, half_a, half_b)
    density_next = call(
        functools.partial(second_outer_kernel, count),
        pltpu.HBM(density.shape, BF16),
        flops=PROP_FLOPS,
        vmem=16,
        scalars=2,
        in_specs=[vmem] * 10 + [hbm],
        out_specs=hbm,
        scratch=outer_scratch + [sides(2), pltpu.VMEM((2, 2, 3, width, width), BF16), pltpu.SemaphoreType.DMA((2,))],
        aliases={12: 0},
    )(lead_blocks, absorption, half, core, diag_new, got_a, got_b, half_a, half_b, diag_a, diag_b, hp, in_hbm(inner))
    return (density_next, grid_term)


def solution(mesh):
    band = P(None, ("row", "col"), None, None, None)
    blocks = P(("row", "col"), None, None)
    return jax.shard_map(
        shards,
        mesh=mesh,
        in_specs=(band, band, blocks, P(), P(), blocks, P(None, "col")),
        out_specs=(band, blocks),
        check_vma=False,
    )
```

```python
import functools

import jax
import jax.numpy as jnp
from jax import lax
from jax.experimental import pallas as pl
from jax.experimental.pallas import tpu as pltpu
from jax.sharding import PartitionSpec as P

CAP = 3
HALF_STEP = 0.2
SECOND_ORDER = 0.5 * HALF_STEP * HALF_STEP
GRID_FACTOR = 0.1
F32 = jnp.float32
BF16 = jnp.bfloat16
PROP_FLOPS = 1 << 32
MIB = 1024 * 1024
TILE = 16


def call(kernel, out_shape, flops, vmem, scalars=0, grid=(), in_specs=None, out_specs=None, scratch=()):
    whole = pl.BlockSpec(memory_space=pltpu.VMEM)
    return pl.pallas_call(
        kernel,
        out_shape=out_shape,
        grid_spec=pltpu.PrefetchScalarGridSpec(
            num_scalar_prefetch=scalars,
            grid=grid,
            in_specs=in_specs,
            out_specs=jax.tree.map(lambda _: whole, out_shape) if out_specs is None else out_specs,
            scratch_shapes=scratch,
        ),
        compiler_params=pltpu.CompilerParams(vmem_limit_bytes=vmem * MIB),
        cost_estimate=pl.CostEstimate(flops=flops, bytes_accessed=4 << 20, transcendentals=0),
    )


def in_hbm(x):
    return pltpu.with_memory_space_constraint(x, pltpu.HBM)


def block_spec(shape, index):
    return pl.BlockSpec(shape, lambda *_: index)


def joined(re, im):
    return jnp.concatenate([re, im], axis=1)


def dagger(value):
    width = value.shape[0]
    re = value[:, :width].astype(F32).T
    im = value[:, width:].astype(F32).T
    return joined(re, -im).astype(BF16)


def as_right(value):
    width = value.shape[0]
    return jnp.concatenate([value, joined(-value[:, width:], value[:, :width])], axis=0)


def band_column(left, right, j, low, high):
    total = {}
    for mid in (j - 1, j, j + 1):
        rows = [i for i in range(max(mid, j) - 1, min(mid, j) + 2) if low <= i <= high]
        if not rows:
            continue
        stacked = jnp.concatenate([left(i, mid) for i in rows], axis=0)
        result = jnp.dot(stacked, as_right(right(mid, j)), preferred_element_type=F32)
        width = result.shape[0] // len(rows)
        for n, i in enumerate(rows):
            part = result[n * width : (n + 1) * width]
            total[i] = part if i not in total else total[i] + part
    return total


def times_i(value):
    width = value.shape[0]
    return joined(-value[:, width:], value[:, :width])


def taylor_first(columns, low, high, get_left, get_q, hp_ref):
    for j in columns:
        for i, value in band_column(get_left, get_q, j, low, high).items():
            hp_ref[i + 1, j - i + 1] = value.astype(BF16)


def propagate(ranges, get_q, get_hp, get_left, get_right, moved_ref, wh_ref, write):
    def get(ref):
        return lambda i, j: ref[i + 1, j - i + 1]

    def product(left, right):
        for low, high in ranges:
            for j in range(low - 1, high + 2):
                for i, value in band_column(left, right, j, low, high).items():
                    yield i, j, value

    for i, j, value in product(get_left, get_hp):
        moved = get_q(i, j).astype(F32) - HALF_STEP * times_i(get_hp(i, j).astype(F32)) - SECOND_ORDER * value
        moved_ref[i + 1, j - i + 1] = moved.astype(BF16)
    for i, j, value in product(get(moved_ref), get_right):
        wh_ref[i + 1, j - i + 1] = value.astype(BF16)
    for i, j, value in product(get(wh_ref), get_right):
        moved = moved_ref[i + 1, j - i + 1].astype(F32)
        wh = wh_ref[i + 1, j - i + 1].astype(F32)
        write(i, j, (moved + HALF_STEP * times_i(wh) - SECOND_ORDER * value).astype(BF16))


def lanes_rows(shape):
    return lax.broadcasted_iota(jnp.int32, shape, 1), lax.broadcasted_iota(jnp.int32, shape, 0)


def pack_hermitian(re, im):
    lane, row = lanes_rows(re.shape)
    return jnp.where(row <= lane, re, im)


def unpack_hermitian(packed):
    lane, row = lanes_rows(packed.shape)
    packed = packed.astype(F32)
    turned = packed.T
    re = jnp.where(row <= lane, packed, turned)
    im = jnp.where(row > lane, packed, jnp.where(row < lane, -turned, 0.0))
    return joined(re, im).astype(BF16)


def pack_symmetric(block, folded):
    lane, row = lanes_rows(block.shape)
    half = block.shape[0] // 2
    both = jnp.where(lane == row, block, block + block.T) if folded else block
    lane, row = lanes_rows((half, block.shape[1]))
    packed = jnp.where(lane >= row, both[:half], pltpu.roll(both[half:], half, 1))
    diagonal = jnp.sum(jnp.where(lane == row + half, both[half:], 0.0), axis=0, keepdims=True)
    return packed, diagonal


def unpack_triangle(packed, diagonal):
    half, width = packed.shape
    lane, row = lanes_rows(packed.shape)
    top = jnp.where(lane >= row, packed, 0.0)
    below = jnp.where(lane < row + half, pltpu.roll(packed, half, 1), jnp.where(lane == row + half, diagonal, 0.0))
    return jnp.concatenate([top, jnp.where(lane < half, 0.0, below)], axis=0)


def symmetric(value):
    return 0.5 * (value + value.T)


def send_kernel(count, dens, core, grid_old, send_a, send_b, bands, grids, sems):
    last = count - 1
    places = [(dens, last, 1), (dens, last - 1, 2), (core, last, 1), (core, last, 0),
              (dens, 0, 1), (dens, 1, 0), (core, 0, 1), (core, 0, 2)]
    copies = [
        pltpu.make_async_copy(ref.at[:, i, k], bands.at[n], sems.at[n]) for n, (ref, i, k) in enumerate(places)
    ]
    copies += [
        pltpu.make_async_copy(grid_old.at[i], grids.at[n], sems.at[8 + n]) for n, i in enumerate((last, 0))
    ]
    for copy in copies:
        copy.start()
    for copy in copies:
        copy.wait()

    def message(first, grid):
        h_re = (bands[first + 2, 0].astype(F32) + symmetric(grids[grid])).astype(BF16)
        return [pack_hermitian(bands[first, 0], bands[first, 1]), bands[first + 1, 0], bands[first + 1, 1],
                pack_hermitian(h_re, bands[first + 2, 1]), bands[first + 3, 0], bands[first + 3, 1]]

    right = message(0, 0)
    left = message(4, 1)
    even = lax.axis_index("col") % 2 == 0

    @pl.when(even)
    def _():
        for n, (x, y) in enumerate(zip(right, left)):
            send_a[n] = x
            send_b[n] = y

    @pl.when(jnp.logical_not(even))
    def _():
        for n, (x, y) in enumerate(zip(right, left)):
            send_a[n] = y
            send_b[n] = x


def partner(orders, n):
    even, odd = orders[0][n], orders[1][n]
    offset = even if even == odd else jnp.where(lax.axis_index("col") % 2 == 0, even, odd)
    return lax.axis_index("row") ^ offset


def halo_reader(got_a, got_b):
    even = lax.axis_index("col") % 2 == 0

    def low(n):
        return jnp.where(even, got_b[n], got_a[n])

    def high(n):
        return jnp.where(even, got_a[n], got_b[n])

    return low, high


def set_diagonals(rows, count, leads, absorption, diag_re, diag_im, left_ref, right_ref):
    width = left_ref.shape[1]
    lane, row = lanes_rows((width, width))
    first = (lax.axis_index("row") * lax.axis_size("col") + lax.axis_index("col")) * count
    for i in rows:
        re = diag_re(i)
        im = diag_im(i).astype(F32)
        gamma = jnp.float32(0.0)
        for n in range(leads.shape[0]):
            gamma += jnp.where(leads[n] == first + i, absorption[n], 0.0)
        shift = jnp.where(lane == row, gamma, 0.0)
        left_ref[i + 1] = joined(re, (im - shift).astype(BF16))
        right_ref[i + 1] = joined(re, (im + shift).astype(BF16))


def band_at(ref):
    return lambda i, j: joined(ref[0, i, j - i + 1], ref[1, i, j - i + 1])


def band_writer(ref, first=0):
    def write(i, j, value):
        width = value.shape[0]
        ref[0, i - first, j - i + 1] = value[:, :width]
        ref[1, i - first, j - i + 1] = value[:, width:]

    return write


def old_diagonals(rows, count, leads, absorption, core, grid_old, left_ref, right_ref, ends=None):
    width = core.shape[-1]

    def diag_re(i):
        if i == -1:
            return ends[0][:, :width]
        if i == count:
            return ends[1][:, :width]
        return (core[0, i, 1].astype(F32) + symmetric(grid_old[i])).astype(BF16)

    def diag_im(i):
        return ends[0][:, width:] if i == -1 else ends[1][:, width:] if i == count else core[1, i, 1]

    set_diagonals(rows, count, leads, absorption, diag_re, diag_im, left_ref, right_ref)


def new_diagonals(rows, count, leads, absorption, core, diag_new, left_ref, right_ref, ends=None, ends_re=None):
    width = core.shape[-1]

    def diag_re(i):
        if i == -1:
            return ends_re[0]
        if i == count:
            return ends_re[1]
        return diag_new[i]

    def diag_im(i):
        return ends[0][:, width:] if i == -1 else ends[1][:, width:] if i == count else core[1, i, 1]

    set_diagonals(rows, count, leads, absorption, diag_re, diag_im, left_ref, right_ref)


def band_access(count, core, far_low, far_high, low_edge, high_edge, diag_ref):
    def get(i, j):
        if i == j:
            return diag_ref[i + 1]
        if i == -1:
            return far_low() if j == -2 else low_edge[...]
        if i == count:
            return far_high() if j == count + 1 else high_edge[...]
        return joined(core[0, i, j - i + 1], core[1, i, j - i + 1])

    return get


def put_half(count, half, target, start, right):
    last = count - 1
    blocks = [(last, 1), (last, 2), (last - 1, 2)] if right else [(0, 1), (0, 0), (1, 0)]
    for n, (i, k) in enumerate(blocks):
        for part in range(2):
            target[start + 2 * n + part] = half[part, i, k]


def brick_tables(count, owners, place, which):
    lane, row = lanes_rows(owners.shape)
    own = lax.axis_index("row")
    source = owners[...] // count // lax.axis_size("col")
    slot = jnp.zeros(owners.shape, jnp.int32)
    for t in range(owners.shape[1] - 1):
        slot += jnp.where((lane > t) & (source == source[:, t : t + 1]), 1, 0)
    mine = jnp.where(source == own, owners[...] % count, -1)
    own_source = jnp.sum(jnp.where(row == own, source, 0), axis=0, keepdims=True)
    own_slot = jnp.sum(jnp.where(row == own, slot, 0), axis=0, keepdims=True)
    here = own_source == row
    places = jnp.zeros(owners.shape, jnp.int32)
    bricks = jnp.zeros(owners.shape, jnp.int32)
    for n in range(CAP):
        places = jnp.where(lane == n, jnp.max(jnp.where(slot == n, mine, -1), axis=1, keepdims=True), places)
        brick = jnp.max(jnp.where(here & (own_slot == n), lane, 0), axis=1, keepdims=True)
        bricks = jnp.where(lane == n, brick, bricks)
    place[...] = places
    which[...] = bricks


def first_inner_kernel(count, leads, absorption, dens, core, grid_old, owners, hp_ref, half, place, which, moved_ref, wh_ref, left_ref, right_ref):
    brick_tables(count, owners, place, which)
    old_diagonals(range(count), count, leads, absorption, core, grid_old, left_ref, right_ref)
    get_left = band_access(count, core, None, None, None, None, left_ref)
    get_right = band_access(count, core, None, None, None, None, right_ref)
    get_q = band_at(dens)

    def get_hp(i, j):
        return hp_ref[i + 1, j - i + 1]

    taylor_first(range(count), 1, count - 2, get_left, get_q, hp_ref)
    propagate([(2, count - 3)], get_q, get_hp, get_left, get_right, moved_ref, wh_ref, band_writer(half))


def first_outer_kernel(count, orders, leads, absorption, place, dens, core, grid_old, got_a, got_b, hp_in, half_in,
                       half, send_b, *rest):
    outgoing, (hp_ref, moved_ref, wh_ref, left_ref, right_ref, edges, packed, diagonals) = rest[:-8], rest[-8:]
    low, high = halo_reader(got_a, got_b)
    last = count - 1
    edges[0] = dagger(band_at(dens)(0, -1))
    edges[1] = dagger(band_at(dens)(last, count))
    edges[2] = dagger(band_at(core)(0, -1))
    edges[3] = dagger(band_at(core)(last, count))
    edges[4] = unpack_hermitian(low(0))
    edges[5] = unpack_hermitian(high(0))
    ends = unpack_hermitian(low(3)), unpack_hermitian(high(3))
    rows = [-1, 0, 1, 2, count - 3, count - 2, last, count]
    old_diagonals(rows, count, leads, absorption, core, grid_old, left_ref, right_ref, ends)
    half[:, 2 : count - 2] = half_in[:, 2 : count - 2]

    def get_q(i, j):
        if i == -2:
            return joined(low(1), low(2))
        if i == -1:
            return edges[4] if j == -1 else edges[0]
        if i == count:
            return edges[5] if j == count else edges[1]
        if i == count + 1:
            return joined(high(1), high(2))
        return band_at(dens)(i, j)

    def get_hp(i, j):
        ref = hp_in if 1 <= i <= count - 2 else hp_ref
        return ref[i + 1, j - i + 1]

    def far_low():
        return joined(low(4), low(5))

    def far_high():
        return joined(high(4), high(5))

    get_left = band_access(count, core, far_low, far_high, edges.at[2], edges.at[3], left_ref)
    get_right = band_access(count, core, far_low, far_high, edges.at[2], edges.at[3], right_ref)
    write = band_writer(half)
    taylor_first(range(-1, 2), -1, 0, get_left, get_q, hp_ref)
    taylor_first(range(last - 1, count + 1), last, count, get_left, get_q, hp_ref)
    propagate([(0, 1), (last - 1, last)], get_q, get_hp, get_left, get_right, moved_ref, wh_ref, write)

    even = lax.axis_index("col") % 2 == 0

    @pl.when(even)
    def _():
        put_half(count, half, send_b, 0, False)

    @pl.when(jnp.logical_not(even))
    def _():
        put_half(count, half, send_b, 0, True)

    for i in range(count):
        top, diagonal = pack_symmetric(half[0, i, 1].astype(F32), True)
        packed[i] = top.astype(BF16)
        diagonals[i] = jnp.broadcast_to(diagonal, diagonals.shape[1:])

    height, width = packed.shape[1:]
    _, row = lanes_rows((TILE, width))

    for number, out in enumerate(outgoing):
        p = partner(orders, number)
        tail = jnp.zeros((TILE, width), F32)
        for n in range(CAP):
            source = jnp.maximum(place[p, n], 0)
            out[n * height : (n + 1) * height] = packed[source]
            tail = jnp.where(row == n, diagonals[source][:1], tail)
        out[CAP * height :] = tail.astype(BF16)


def brick_kernel(chunk, orders, numbers, which, colloc, unread, *rest):
    incoming, returned = rest[: len(numbers)], rest[len(numbers) :]
    points, width = colloc.shape[1:]
    scale = GRID_FACTOR * width / points
    height = width // 2
    _, tail_row = lanes_rows((TILE, width))
    tails = [jnp.zeros((TILE, width), F32) for _ in numbers]
    jobs = [(m, n, which[partner(orders, number), n]) for m, number in enumerate(numbers) for n in range(CAP)]

    def block(job):
        m, n, _ = job
        last = incoming[m][CAP * height :].astype(F32)
        return unpack_triangle(incoming[m][n * height : (n + 1) * height].astype(F32), last[n : n + 1])

    def put(job, result):
        m, n, _ = job
        packed, diagonal = pack_symmetric(scale * result, False)
        returned[m][n * height : (n + 1) * height] = packed.astype(BF16)
        tails[m] = jnp.where(tail_row == n, diagonal, tails[m])

    for first, second in zip(jobs[::2], jobs[1::2]):
        c0, c1 = colloc.at[first[2]], colloc.at[second[2]]
        q0, q1 = block(first), block(second)
        zero = jnp.zeros_like(q0)
        both = jnp.concatenate([joined(q0, zero), joined(zero, q1)], axis=0).astype(BF16)
        columns = []
        for g in range(0, points, chunk):
            turned = jnp.concatenate([c0[g : g + chunk].T, c1[g : g + chunk].T], axis=0)
            wide = turned.astype(F32)
            projected = jnp.dot(both, turned, preferred_element_type=F32) * wide
            weighted = []
            for n in range(2):
                rows = slice(n * width, (n + 1) * width)
                dens = jnp.sum(projected[rows], axis=0, keepdims=True)
                potential = dens * lax.rsqrt(1.0 + dens * dens)
                weighted.append((potential * wide[rows]).astype(BF16))
            columns.append(jnp.concatenate(weighted, axis=0))
        result = jnp.dot(jnp.concatenate(columns, axis=1), joined(c0[...], c1[...]), preferred_element_type=F32)
        put(first, result[:width, :width])
        put(second, result[width:, width:])
    for out, tail in zip(returned, tails):
        out[CAP * height :] = tail.astype(BF16)


def collect_kernel(count, orders, place, core, half, *rest):
    arriving, (term, diag_new, send_a, send_b, total, tails) = rest[:-6], rest[-6:]
    width = core.shape[-1]
    height = width // 2
    total[...] = jnp.zeros_like(total)
    tails[...] = jnp.zeros_like(tails)
    for number, block in enumerate(arriving):
        p = partner(orders, number)
        last = block[CAP * height :].astype(F32)
        for n in range(CAP):
            at = place[p, n]
            kept = at >= 0
            at = jnp.maximum(at, 0)
            total[at] += jnp.where(kept, block[n * height : (n + 1) * height].astype(F32), 0.0)
            tails[at] += jnp.where(kept, last[n : n + 1], 0.0)
    lane, row = lanes_rows((width, width))
    for i in range(count):
        triangle = unpack_triangle(total[i], tails[i][:1])
        whole = jnp.where(lane == row, triangle, triangle + triangle.T)
        term[i] = whole
        diag_new[i] = (core[0, i, 0].astype(F32) + whole).astype(BF16)

    even = lax.axis_index("col") % 2 == 0
    last = count - 1

    @pl.when(even)
    def _():
        send_a[0] = diag_new[last]
        send_b[0] = diag_new[0]
        put_half(count, half, send_a, 1, True)

    @pl.when(jnp.logical_not(even))
    def _():
        send_a[0] = diag_new[0]
        send_b[0] = diag_new[last]
        put_half(count, half, send_a, 1, False)


def second_inner_kernel(count, leads, absorption, half, core, diag_new, term, out, hp_ref, grid_term,
                        moved_ref, wh_ref, left_ref, right_ref, sem):
    copy = pltpu.make_async_copy(term, grid_term, sem.at[0])
    copy.start()
    new_diagonals(range(count), count, leads, absorption, core, diag_new, left_ref, right_ref)
    get_left = band_access(count, core, None, None, None, None, left_ref)
    get_right = band_access(count, core, None, None, None, None, right_ref)
    get_q = band_at(half)

    def get_hp(i, j):
        return hp_ref[i + 1, j - i + 1]

    taylor_first(range(count), 1, count - 2, get_left, get_q, hp_ref)
    propagate([(2, count - 3)], get_q, get_hp, get_left, get_right, moved_ref, wh_ref, band_writer(out, 2))
    copy.wait()


def second_outer_kernel(count, leads, absorption, half, core, diag_new, core_a, core_b, got_a, got_b, half_b,
                        hp_in, inner, out, hp_ref, moved_ref, wh_ref, left_ref, right_ref, edges, ready, sems):
    copies = [pltpu.make_async_copy(inner, out.at[:, pl.ds(2, count - 4)], sems.at[2])]
    copies[0].start()
    core_low, core_high = halo_reader(core_a, core_b)
    even = lax.axis_index("col") % 2 == 0

    def low(n):
        return jnp.where(even, got_b[0] if n == 0 else half_b[n - 1], got_a[n])

    def high(n):
        return jnp.where(even, got_a[n], got_b[0] if n == 0 else half_b[n - 1])

    last = count - 1
    edges[0] = dagger(band_at(core)(0, -1))
    edges[1] = dagger(band_at(core)(last, count))
    ends = unpack_hermitian(core_low(3)), unpack_hermitian(core_high(3))
    rows = [-1, 0, 1, 2, count - 3, count - 2, last, count]
    new_diagonals(rows, count, leads, absorption, core, diag_new, left_ref, right_ref, ends, (low(0), high(0)))

    def get_q(i, j):
        if 0 <= i < count:
            return band_at(half)(i, j)
        n = 1 if i == j else 3 if i in (-1, count) else 5
        side = low if i < 0 else high
        return joined(side(n), side(n + 1))

    def far_low():
        return joined(core_low(4), core_low(5))

    def far_high():
        return joined(core_high(4), core_high(5))

    get_left = band_access(count, core, far_low, far_high, edges.at[0], edges.at[1], left_ref)
    get_right = band_access(count, core, far_low, far_high, edges.at[0], edges.at[1], right_ref)

    def get_hp(i, j):
        ref = hp_in if 1 <= i <= count - 2 else hp_ref
        return ref[i + 1, j - i + 1]

    def write(i, j, value):
        width = value.shape[0]
        n = i if i < 2 else i - count + 4
        ready[0, n, j - i + 1] = value[:, :width]
        ready[1, n, j - i + 1] = value[:, width:]

    taylor_first(range(-1, 2), -1, 0, get_left, get_q, hp_ref)
    taylor_first(range(last - 1, count + 1), last, count, get_left, get_q, hp_ref)
    propagate([(0, 1), (last - 1, last)], get_q, get_hp, get_left, get_right, moved_ref, wh_ref, write)
    for n, i in enumerate((0, last - 1)):
        copies.append(pltpu.make_async_copy(ready.at[:, pl.ds(2 * n, 2)], out.at[:, pl.ds(i, 2)], sems.at[n]))
        copies[-1].start()
    for copy in copies:
        copy.wait()


def exchange_a(x, total):
    return lax.ppermute(x, ("row", "col"), [(i, i ^ 1) for i in range(total)])


def exchange_b(x, total):
    return lax.ppermute(x, ("row", "col"), [(i, i + 1) if i % 2 else (i, i - 1) for i in range(1, total - 1)])


def shards(density, core, grid_old, lead_blocks, absorption, collocation, brick_block):
    count = density.shape[1]
    width = density.shape[-1]
    row_size = lax.axis_size("row")
    col_size = lax.axis_size("col")
    total = row_size * col_size
    near, far = list(range(1, row_size // 2)), list(range(row_size // 2, row_size))
    orders = [[0] + far + near, [0] + far + near]
    bricks = brick_block.shape[1]
    vmem = pl.BlockSpec(memory_space=pltpu.VMEM)
    hbm = pl.BlockSpec(memory_space=pltpu.HBM)

    message = jax.ShapeDtypeStruct((6, width, width), BF16)
    table = jax.ShapeDtypeStruct(brick_block.shape, jnp.int32)
    send_a, send_b = call(
        functools.partial(send_kernel, count),
        (message, message),
        flops=1 << 20,
        vmem=8,
        in_specs=[hbm] * 3,
        scratch=[
            pltpu.VMEM((8, 2, width, width), BF16),
            pltpu.VMEM((2, width, width), F32),
            pltpu.SemaphoreType.DMA((10,)),
        ],
    )(*(in_hbm(x) for x in (density, core, grid_old)))
    got_a, got_b = exchange_a(send_a, total), exchange_b(send_b, total)

    def band_scratch(rows):
        return pltpu.VMEM((rows, 3, width, 2 * width), BF16)

    def sides(n):
        return pltpu.VMEM((n, width, 2 * width), BF16)

    hp_shape = jax.ShapeDtypeStruct((count + 2, 3, width, 2 * width), BF16)
    inner_scratch = [band_scratch(count + 2)] * 2 + [sides(count + 2)] * 2
    outer_scratch = [band_scratch(count + 2)] * 3 + [sides(count + 2)] * 2
    hp, half_inner, place, which = call(
        functools.partial(first_inner_kernel, count),
        (hp_shape, jax.ShapeDtypeStruct(density.shape, BF16), table, table),
        flops=PROP_FLOPS,
        vmem=16,
        scalars=2,
        in_specs=[vmem] * 4,
        scratch=inner_scratch,
    )(lead_blocks, absorption, density, core, grid_old, brick_block)
    packed_rows = CAP * width // 2 + TILE
    packed_shape = jax.ShapeDtypeStruct((packed_rows, width), BF16)
    half_message = jax.ShapeDtypeStruct((6, width, width), BF16)
    half, send_b, *outgoing = call(
        functools.partial(first_outer_kernel, count, orders),
        (
            jax.ShapeDtypeStruct(density.shape, BF16),
            half_message,
        )
        + (packed_shape,) * row_size,
        flops=PROP_FLOPS,
        vmem=20,
        scalars=3,
        in_specs=[vmem] * 7,
        scratch=outer_scratch
        + [
            pltpu.VMEM((6, width, 2 * width), BF16),
            pltpu.VMEM((count, width // 2, width), BF16),
            pltpu.VMEM((count, 8, width), F32),
        ],
    )(lead_blocks, absorption, place, density, core, grid_old, got_a, got_b, hp, half_inner)


    def across(x, number):
        if number == 0:
            return x
        pairs = []
        for row in range(row_size):
            for col in range(col_size):
                pairs.append((row * col_size + col, (row ^ orders[col % 2][number]) * col_size + col))
        return lax.ppermute(x, ("row", "col"), pairs)

    half_b = exchange_b(send_b, total)
    incoming = [across(x, number) for number, x in enumerate(outgoing)]
    points = collocation.shape[1]
    arriving = []
    before = which
    for numbers in zip(range(0, row_size, 2), range(1, row_size, 2)):
        returned = call(
            functools.partial(brick_kernel, points // 4, orders, numbers),
            (packed_shape,) * 2,
            flops=4 * 6 * points * width**2,
            vmem=8,
            scalars=1,
            in_specs=[vmem, pl.BlockSpec(memory_space=pl.ANY), vmem, vmem],
        )(which, collocation, before, *(incoming[number] for number in numbers))
        arriving += [across(x, number) for number, x in zip(numbers, returned)]
        before = returned[0]

    term, diag_new, send_a, send_b = call(
        functools.partial(collect_kernel, count, orders),
        (
            jax.ShapeDtypeStruct((count, width, width), F32),
            jax.ShapeDtypeStruct((count, width, width), BF16),
            jax.ShapeDtypeStruct((7, width, width), BF16),
            jax.ShapeDtypeStruct((1, width, width), BF16),
        ),
        flops=1 << 20,
        vmem=8,
        scalars=1,
        grid=(1,),
        in_specs=[block_spec((1, count, 1, width, width), (0, 0, 1, 0, 0))] + [vmem] * (row_size + 1),
        scratch=[pltpu.VMEM((count, width // 2, width), F32), pltpu.VMEM((count, 8, width), F32)],
    )(place, core, half, *arriving)
    half_a, diag_b = exchange_a(send_a, total), exchange_b(send_b, total)

    inner, hp, grid_term = call(
        functools.partial(second_inner_kernel, count),
        (
            jax.ShapeDtypeStruct((2, count - 4, 3, width, width), BF16),
            hp_shape,
            pltpu.HBM((count, width, width), F32),
        ),
        flops=PROP_FLOPS,
        vmem=16,
        scalars=2,
        in_specs=[vmem] * 4,
        out_specs=(vmem, vmem, hbm),
        scratch=inner_scratch + [pltpu.SemaphoreType.DMA((1,))],
    )(lead_blocks, absorption, half, core, diag_new, term)
    density_next = call(
        functools.partial(second_outer_kernel, count),
        pltpu.HBM(density.shape, BF16),
        flops=PROP_FLOPS,
        vmem=16,
        scalars=2,
        in_specs=[vmem] * 10,
        out_specs=hbm,
        scratch=outer_scratch + [sides(2), pltpu.VMEM((2, 4, 3, width, width), BF16), pltpu.SemaphoreType.DMA((3,))],
    )(lead_blocks, absorption, half, core, diag_new, got_a, got_b, half_a, diag_b, half_b, hp, inner)
    return (density_next, grid_term)


def solution(mesh):
    band = P(None, ("row", "col"), None, None, None)
    blocks = P(("row", "col"), None, None)
    return jax.shard_map(
        shards,
        mesh=mesh,
        in_specs=(band, band, blocks, P(), P(), blocks, P(None, "col")),
        out_specs=(band, blocks),
        check_vma=False,
    )
```

```python
import functools

import jax
import jax.numpy as jnp
from jax import lax
from jax.experimental import pallas as pl
from jax.experimental.pallas import tpu as pltpu
from jax.sharding import PartitionSpec as P

CAP = 3
HALF_STEP = 0.2
SECOND_ORDER = 0.5 * HALF_STEP * HALF_STEP
GRID_FACTOR = 0.1
F32 = jnp.float32
BF16 = jnp.bfloat16
PROP_FLOPS = 1 << 32
MIB = 1024 * 1024
TILE = 16


def call(kernel, out_shape, flops, vmem, scalars=0, grid=(), in_specs=None, out_specs=None, scratch=()):
    whole = pl.BlockSpec(memory_space=pltpu.VMEM)
    return pl.pallas_call(
        kernel,
        out_shape=out_shape,
        grid_spec=pltpu.PrefetchScalarGridSpec(
            num_scalar_prefetch=scalars,
            grid=grid,
            in_specs=in_specs,
            out_specs=jax.tree.map(lambda _: whole, out_shape) if out_specs is None else out_specs,
            scratch_shapes=scratch,
        ),
        compiler_params=pltpu.CompilerParams(vmem_limit_bytes=vmem * MIB),
        cost_estimate=pl.CostEstimate(flops=flops, bytes_accessed=4 << 20, transcendentals=0),
    )


def in_hbm(x):
    return pltpu.with_memory_space_constraint(x, pltpu.HBM)


def block_spec(shape, index):
    return pl.BlockSpec(shape, lambda *_: index)


def joined(re, im):
    return jnp.concatenate([re, im], axis=1)


def dagger(value):
    width = value.shape[0]
    re = value[:, :width].astype(F32).T
    im = value[:, width:].astype(F32).T
    return joined(re, -im).astype(BF16)


def as_right(value):
    width = value.shape[0]
    return jnp.concatenate([value, joined(-value[:, width:], value[:, :width])], axis=0)


def band_column(left, right, j, low, high):
    total = {}
    for mid in (j - 1, j, j + 1):
        rows = [i for i in range(max(mid, j) - 1, min(mid, j) + 2) if low <= i <= high]
        if not rows:
            continue
        stacked = jnp.concatenate([left(i, mid) for i in rows], axis=0)
        result = jnp.dot(stacked, as_right(right(mid, j)), preferred_element_type=F32)
        width = result.shape[0] // len(rows)
        for n, i in enumerate(rows):
            part = result[n * width : (n + 1) * width]
            total[i] = part if i not in total else total[i] + part
    return total


def times_i(value):
    width = value.shape[0]
    return joined(-value[:, width:], value[:, :width])


def taylor_first(columns, low, high, get_left, get_q, hp_ref):
    for j in columns:
        for i, value in band_column(get_left, get_q, j, low, high).items():
            hp_ref[i + 1, j - i + 1] = value.astype(BF16)


def propagate(ranges, get_q, get_hp, get_left, get_right, moved_ref, wh_ref, write):
    def get(ref):
        return lambda i, j: ref[i + 1, j - i + 1]

    def product(left, right):
        for low, high in ranges:
            for j in range(low - 1, high + 2):
                for i, value in band_column(left, right, j, low, high).items():
                    yield i, j, value

    for i, j, value in product(get_left, get_hp):
        moved = get_q(i, j).astype(F32) - HALF_STEP * times_i(get_hp(i, j).astype(F32)) - SECOND_ORDER * value
        moved_ref[i + 1, j - i + 1] = moved.astype(BF16)
    for i, j, value in product(get(moved_ref), get_right):
        wh_ref[i + 1, j - i + 1] = value.astype(BF16)
    for i, j, value in product(get(wh_ref), get_right):
        moved = moved_ref[i + 1, j - i + 1].astype(F32)
        wh = wh_ref[i + 1, j - i + 1].astype(F32)
        write(i, j, (moved + HALF_STEP * times_i(wh) - SECOND_ORDER * value).astype(BF16))


def lanes_rows(shape):
    return lax.broadcasted_iota(jnp.int32, shape, 1), lax.broadcasted_iota(jnp.int32, shape, 0)


def pack_hermitian(re, im):
    lane, row = lanes_rows(re.shape)
    return jnp.where(row <= lane, re, im)


def unpack_hermitian(packed):
    lane, row = lanes_rows(packed.shape)
    packed = packed.astype(F32)
    turned = packed.T
    re = jnp.where(row <= lane, packed, turned)
    im = jnp.where(row > lane, packed, jnp.where(row < lane, -turned, 0.0))
    return joined(re, im).astype(BF16)


def pack_symmetric(block, folded):
    lane, row = lanes_rows(block.shape)
    half = block.shape[0] // 2
    both = jnp.where(lane == row, block, block + block.T) if folded else block
    lane, row = lanes_rows((half, block.shape[1]))
    packed = jnp.where(lane >= row, both[:half], pltpu.roll(both[half:], half, 1))
    diagonal = jnp.sum(jnp.where(lane == row + half, both[half:], 0.0), axis=0, keepdims=True)
    return packed, diagonal


def unpack_triangle(packed, diagonal):
    half, width = packed.shape
    lane, row = lanes_rows(packed.shape)
    top = jnp.where(lane >= row, packed, 0.0)
    below = jnp.where(lane < row + half, pltpu.roll(packed, half, 1), jnp.where(lane == row + half, diagonal, 0.0))
    return jnp.concatenate([top, jnp.where(lane < half, 0.0, below)], axis=0)


def symmetric(value):
    return 0.5 * (value + value.T)


def send_kernel(count, dens, core, grid_old, send_a, send_b, bands, grids, sems):
    last = count - 1
    places = [(dens, last, 1), (dens, last - 1, 2), (core, last, 1), (core, last, 0),
              (dens, 0, 1), (dens, 1, 0), (core, 0, 1), (core, 0, 2)]
    copies = [
        pltpu.make_async_copy(ref.at[:, i, k], bands.at[n], sems.at[n]) for n, (ref, i, k) in enumerate(places)
    ]
    copies += [
        pltpu.make_async_copy(grid_old.at[i], grids.at[n], sems.at[8 + n]) for n, i in enumerate((last, 0))
    ]
    for copy in copies:
        copy.start()
    for copy in copies:
        copy.wait()

    def message(first, grid):
        h_re = (bands[first + 2, 0].astype(F32) + symmetric(grids[grid])).astype(BF16)
        return [pack_hermitian(bands[first, 0], bands[first, 1]), bands[first + 1, 0], bands[first + 1, 1],
                pack_hermitian(h_re, bands[first + 2, 1]), bands[first + 3, 0], bands[first + 3, 1]]

    right = message(0, 0)
    left = message(4, 1)
    even = lax.axis_index("col") % 2 == 0

    @pl.when(even)
    def _():
        for n, (x, y) in enumerate(zip(right, left)):
            send_a[n] = x
            send_b[n] = y

    @pl.when(jnp.logical_not(even))
    def _():
        for n, (x, y) in enumerate(zip(right, left)):
            send_a[n] = y
            send_b[n] = x


def partner(orders, n):
    even, odd = orders[0][n], orders[1][n]
    offset = even if even == odd else jnp.where(lax.axis_index("col") % 2 == 0, even, odd)
    return lax.axis_index("row") ^ offset


def halo_reader(got_a, got_b):
    even = lax.axis_index("col") % 2 == 0

    def low(n):
        return jnp.where(even, got_b[n], got_a[n])

    def high(n):
        return jnp.where(even, got_a[n], got_b[n])

    return low, high


def set_diagonals(rows, count, leads, absorption, diag_re, diag_im, left_ref, right_ref):
    width = left_ref.shape[1]
    lane, row = lanes_rows((width, width))
    first = (lax.axis_index("row") * lax.axis_size("col") + lax.axis_index("col")) * count
    for i in rows:
        re = diag_re(i)
        im = diag_im(i).astype(F32)
        gamma = jnp.float32(0.0)
        for n in range(leads.shape[0]):
            gamma += jnp.where(leads[n] == first + i, absorption[n], 0.0)
        shift = jnp.where(lane == row, gamma, 0.0)
        left_ref[i + 1] = joined(re, (im - shift).astype(BF16))
        right_ref[i + 1] = joined(re, (im + shift).astype(BF16))


def band_at(ref):
    return lambda i, j: joined(ref[0, i, j - i + 1], ref[1, i, j - i + 1])


def band_writer(ref, first=0):
    def write(i, j, value):
        width = value.shape[0]
        ref[0, i - first, j - i + 1] = value[:, :width]
        ref[1, i - first, j - i + 1] = value[:, width:]

    return write


def old_diagonals(rows, count, leads, absorption, core, grid_old, left_ref, right_ref, ends=None):
    width = core.shape[-1]

    def diag_re(i):
        if i == -1:
            return ends[0][:, :width]
        if i == count:
            return ends[1][:, :width]
        return (core[0, i, 1].astype(F32) + symmetric(grid_old[i])).astype(BF16)

    def diag_im(i):
        return ends[0][:, width:] if i == -1 else ends[1][:, width:] if i == count else core[1, i, 1]

    set_diagonals(rows, count, leads, absorption, diag_re, diag_im, left_ref, right_ref)


def new_diagonals(rows, count, leads, absorption, core, diag_new, left_ref, right_ref, ends=None, ends_re=None):
    width = core.shape[-1]

    def diag_re(i):
        if i == -1:
            return ends_re[0]
        if i == count:
            return ends_re[1]
        return diag_new[i]

    def diag_im(i):
        return ends[0][:, width:] if i == -1 else ends[1][:, width:] if i == count else core[1, i, 1]

    set_diagonals(rows, count, leads, absorption, diag_re, diag_im, left_ref, right_ref)


def band_access(count, core, far_low, far_high, low_edge, high_edge, diag_ref):
    def get(i, j):
        if i == j:
            return diag_ref[i + 1]
        if i == -1:
            return far_low() if j == -2 else low_edge[...]
        if i == count:
            return far_high() if j == count + 1 else high_edge[...]
        return joined(core[0, i, j - i + 1], core[1, i, j - i + 1])

    return get


def put_half(count, half, target, start, right):
    last = count - 1
    blocks = [(last, 1), (last, 2), (last - 1, 2)] if right else [(0, 1), (0, 0), (1, 0)]
    for n, (i, k) in enumerate(blocks):
        for part in range(2):
            target[start + 2 * n + part] = half[part, i, k]


def brick_tables(count, owners, place, which):
    lane, row = lanes_rows(owners.shape)
    own = lax.axis_index("row")
    source = owners[...] // count // lax.axis_size("col")
    slot = jnp.zeros(owners.shape, jnp.int32)
    for t in range(owners.shape[1] - 1):
        slot += jnp.where((lane > t) & (source == source[:, t : t + 1]), 1, 0)
    mine = jnp.where(source == own, owners[...] % count, -1)
    own_source = jnp.sum(jnp.where(row == own, source, 0), axis=0, keepdims=True)
    own_slot = jnp.sum(jnp.where(row == own, slot, 0), axis=0, keepdims=True)
    here = own_source == row
    places = jnp.zeros(owners.shape, jnp.int32)
    bricks = jnp.zeros(owners.shape, jnp.int32)
    for n in range(CAP):
        places = jnp.where(lane == n, jnp.max(jnp.where(slot == n, mine, -1), axis=1, keepdims=True), places)
        brick = jnp.max(jnp.where(here & (own_slot == n), lane, 0), axis=1, keepdims=True)
        bricks = jnp.where(lane == n, brick, bricks)
    place[...] = places
    which[...] = bricks


def first_inner_kernel(count, leads, absorption, dens, core, grid_old, owners, hp_ref, half, place, which, moved_ref, wh_ref, left_ref, right_ref):
    brick_tables(count, owners, place, which)
    old_diagonals(range(count), count, leads, absorption, core, grid_old, left_ref, right_ref)
    get_left = band_access(count, core, None, None, None, None, left_ref)
    get_right = band_access(count, core, None, None, None, None, right_ref)
    get_q = band_at(dens)

    def get_hp(i, j):
        return hp_ref[i + 1, j - i + 1]

    taylor_first(range(count), 1, count - 2, get_left, get_q, hp_ref)
    propagate([(2, count - 3)], get_q, get_hp, get_left, get_right, moved_ref, wh_ref, band_writer(half))


def first_outer_kernel(count, orders, leads, absorption, place, dens, core, grid_old, got_a, got_b, hp_in, half_in,
                       half, send_b, *rest):
    outgoing, (hp_ref, moved_ref, wh_ref, left_ref, right_ref, edges, packed, diagonals) = rest[:-8], rest[-8:]
    low, high = halo_reader(got_a, got_b)
    last = count - 1
    edges[0] = dagger(band_at(dens)(0, -1))
    edges[1] = dagger(band_at(dens)(last, count))
    edges[2] = dagger(band_at(core)(0, -1))
    edges[3] = dagger(band_at(core)(last, count))
    edges[4] = unpack_hermitian(low(0))
    edges[5] = unpack_hermitian(high(0))
    ends = unpack_hermitian(low(3)), unpack_hermitian(high(3))
    rows = [-1, 0, 1, 2, count - 3, count - 2, last, count]
    old_diagonals(rows, count, leads, absorption, core, grid_old, left_ref, right_ref, ends)
    half[:, 2 : count - 2] = half_in[:, 2 : count - 2]

    def get_q(i, j):
        if i == -2:
            return joined(low(1), low(2))
        if i == -1:
            return edges[4] if j == -1 else edges[0]
        if i == count:
            return edges[5] if j == count else edges[1]
        if i == count + 1:
            return joined(high(1), high(2))
        return band_at(dens)(i, j)

    def get_hp(i, j):
        ref = hp_in if 1 <= i <= count - 2 else hp_ref
        return ref[i + 1, j - i + 1]

    def far_low():
        return joined(low(4), low(5))

    def far_high():
        return joined(high(4), high(5))

    get_left = band_access(count, core, far_low, far_high, edges.at[2], edges.at[3], left_ref)
    get_right = band_access(count, core, far_low, far_high, edges.at[2], edges.at[3], right_ref)
    write = band_writer(half)
    taylor_first(range(-1, 2), -1, 0, get_left, get_q, hp_ref)
    taylor_first(range(last - 1, count + 1), last, count, get_left, get_q, hp_ref)
    propagate([(0, 1), (last - 1, last)], get_q, get_hp, get_left, get_right, moved_ref, wh_ref, write)

    even = lax.axis_index("col") % 2 == 0

    @pl.when(even)
    def _():
        put_half(count, half, send_b, 0, False)

    @pl.when(jnp.logical_not(even))
    def _():
        put_half(count, half, send_b, 0, True)

    for i in range(count):
        top, diagonal = pack_symmetric(half[0, i, 1].astype(F32), True)
        packed[i] = top.astype(BF16)
        diagonals[i] = jnp.broadcast_to(diagonal, diagonals.shape[1:])

    height, width = packed.shape[1:]
    _, row = lanes_rows((TILE, width))

    for number, out in enumerate(outgoing):
        p = partner(orders, number)
        tail = jnp.zeros((TILE, width), F32)
        for n in range(CAP):
            source = jnp.maximum(place[p, n], 0)
            out[n * height : (n + 1) * height] = packed[source]
            tail = jnp.where(row == n, diagonals[source][:1], tail)
        out[CAP * height :] = tail.astype(BF16)


def brick_kernel(chunk, orders, numbers, which, colloc, unread, *rest):
    incoming, returned = rest[: len(numbers)], rest[len(numbers) :]
    points, width = colloc.shape[1:]
    scale = GRID_FACTOR * width / points
    height = width // 2
    _, tail_row = lanes_rows((TILE, width))
    tails = [jnp.zeros((TILE, width), F32) for _ in numbers]
    jobs = [(m, n, which[partner(orders, number), n]) for m, number in enumerate(numbers) for n in range(CAP)]

    def block(job):
        m, n, _ = job
        last = incoming[m][CAP * height :].astype(F32)
        return unpack_triangle(incoming[m][n * height : (n + 1) * height].astype(F32), last[n : n + 1])

    def put(job, result):
        m, n, _ = job
        packed, diagonal = pack_symmetric(scale * result, False)
        returned[m][n * height : (n + 1) * height] = packed.astype(BF16)
        tails[m] = jnp.where(tail_row == n, diagonal, tails[m])

    for first, second in zip(jobs[::2], jobs[1::2]):
        c0, c1 = colloc.at[first[2]], colloc.at[second[2]]
        q0, q1 = block(first), block(second)
        zero = jnp.zeros_like(q0)
        both = jnp.concatenate([joined(q0, zero), joined(zero, q1)], axis=0).astype(BF16)
        columns = []
        for g in range(0, points, chunk):
            turned = jnp.concatenate([c0[g : g + chunk].T, c1[g : g + chunk].T], axis=0)
            wide = turned.astype(F32)
            projected = jnp.dot(both, turned, preferred_element_type=F32) * wide
            weighted = []
            for n in range(2):
                rows = slice(n * width, (n + 1) * width)
                dens = jnp.sum(projected[rows], axis=0, keepdims=True)
                potential = dens * lax.rsqrt(1.0 + dens * dens)
                weighted.append((potential * wide[rows]).astype(BF16))
            columns.append(jnp.concatenate(weighted, axis=0))
        result = jnp.dot(jnp.concatenate(columns, axis=1), joined(c0[...], c1[...]), preferred_element_type=F32)
        put(first, result[:width, :width])
        put(second, result[width:, width:])
    for out, tail in zip(returned, tails):
        out[CAP * height :] = tail.astype(BF16)


def collect_kernel(count, orders, place, core, half, *rest):
    arriving, (term, diag_new, send_a, send_b, total, tails) = rest[:-6], rest[-6:]
    width = core.shape[-1]
    height = width // 2
    total[...] = jnp.zeros_like(total)
    tails[...] = jnp.zeros_like(tails)
    for number, block in enumerate(arriving):
        p = partner(orders, number)
        last = block[CAP * height :].astype(F32)
        for n in range(CAP):
            at = place[p, n]
            kept = at >= 0
            at = jnp.maximum(at, 0)
            total[at] += jnp.where(kept, block[n * height : (n + 1) * height].astype(F32), 0.0)
            tails[at] += jnp.where(kept, last[n : n + 1], 0.0)
    lane, row = lanes_rows((width, width))
    for i in range(count):
        triangle = unpack_triangle(total[i], tails[i][:1])
        whole = jnp.where(lane == row, triangle, triangle + triangle.T)
        term[i] = whole
        diag_new[i] = (core[0, i, 0].astype(F32) + whole).astype(BF16)

    even = lax.axis_index("col") % 2 == 0
    last = count - 1

    @pl.when(even)
    def _():
        send_a[0] = diag_new[last]
        send_b[0] = diag_new[0]
        put_half(count, half, send_a, 1, True)

    @pl.when(jnp.logical_not(even))
    def _():
        send_a[0] = diag_new[0]
        send_b[0] = diag_new[last]
        put_half(count, half, send_a, 1, False)


def second_inner_kernel(count, leads, absorption, half, core, diag_new, term, out, hp_ref, grid_term,
                        moved_ref, wh_ref, left_ref, right_ref, sem):
    copy = pltpu.make_async_copy(term, grid_term, sem.at[0])
    copy.start()
    new_diagonals(range(count), count, leads, absorption, core, diag_new, left_ref, right_ref)
    get_left = band_access(count, core, None, None, None, None, left_ref)
    get_right = band_access(count, core, None, None, None, None, right_ref)
    get_q = band_at(half)

    def get_hp(i, j):
        return hp_ref[i + 1, j - i + 1]

    taylor_first(range(count), 1, count - 2, get_left, get_q, hp_ref)
    propagate([(2, count - 3)], get_q, get_hp, get_left, get_right, moved_ref, wh_ref, band_writer(out, 2))
    copy.wait()


def second_outer_kernel(count, leads, absorption, half, core, diag_new, core_a, core_b, got_a, got_b, half_b,
                        hp_in, inner, out, hp_ref, moved_ref, wh_ref, left_ref, right_ref, edges, ready, sems):
    copies = [pltpu.make_async_copy(inner, out.at[:, pl.ds(2, count - 4)], sems.at[2])]
    for n, i in enumerate((0, count - 2)):
        copies.append(pltpu.make_async_copy(ready.at[:, pl.ds(2 * n, 2)], out.at[:, pl.ds(i, 2)], sems.at[n]))
    copies[0].start()
    core_low, core_high = halo_reader(core_a, core_b)
    even = lax.axis_index("col") % 2 == 0

    def low(n):
        return jnp.where(even, got_b[0] if n == 0 else half_b[n - 1], got_a[n])

    def high(n):
        return jnp.where(even, got_a[n], got_b[0] if n == 0 else half_b[n - 1])

    last = count - 1
    edges[0] = dagger(band_at(core)(0, -1))
    edges[1] = dagger(band_at(core)(last, count))
    ends = unpack_hermitian(core_low(3)), unpack_hermitian(core_high(3))
    rows = [-1, 0, 1, 2, count - 3, count - 2, last, count]
    new_diagonals(rows, count, leads, absorption, core, diag_new, left_ref, right_ref, ends, (low(0), high(0)))

    def get_q(i, j):
        if 0 <= i < count:
            return band_at(half)(i, j)
        n = 1 if i == j else 3 if i in (-1, count) else 5
        side = low if i < 0 else high
        return joined(side(n), side(n + 1))

    def far_low():
        return joined(core_low(4), core_low(5))

    def far_high():
        return joined(core_high(4), core_high(5))

    get_left = band_access(count, core, far_low, far_high, edges.at[0], edges.at[1], left_ref)
    get_right = band_access(count, core, far_low, far_high, edges.at[0], edges.at[1], right_ref)

    def get_hp(i, j):
        ref = hp_in if 1 <= i <= count - 2 else hp_ref
        return ref[i + 1, j - i + 1]

    def write(i, j, value):
        width = value.shape[0]
        n = i if i < 2 else i - count + 4
        ready[0, n, j - i + 1] = value[:, :width]
        ready[1, n, j - i + 1] = value[:, width:]
        if (i, j) == (1, 2):
            copies[1].start()
        if (i, j) == (last, count):
            copies[2].start()

    taylor_first(range(-1, 2), -1, 0, get_left, get_q, hp_ref)
    taylor_first(range(last - 1, count + 1), last, count, get_left, get_q, hp_ref)
    propagate([(0, 1), (last - 1, last)], get_q, get_hp, get_left, get_right, moved_ref, wh_ref, write)
    for copy in copies:
        copy.wait()


def exchange_a(x, total):
    return lax.ppermute(x, ("row", "col"), [(i, i ^ 1) for i in range(total)])


def exchange_b(x, total):
    return lax.ppermute(x, ("row", "col"), [(i, i + 1) if i % 2 else (i, i - 1) for i in range(1, total - 1)])


def shards(density, core, grid_old, lead_blocks, absorption, collocation, brick_block):
    count = density.shape[1]
    width = density.shape[-1]
    row_size = lax.axis_size("row")
    col_size = lax.axis_size("col")
    total = row_size * col_size
    near, far = list(range(1, row_size // 2)), list(range(row_size // 2, row_size))
    orders = [[0] + far + near, [0] + far + near]
    bricks = brick_block.shape[1]
    vmem = pl.BlockSpec(memory_space=pltpu.VMEM)
    hbm = pl.BlockSpec(memory_space=pltpu.HBM)

    message = jax.ShapeDtypeStruct((6, width, width), BF16)
    table = jax.ShapeDtypeStruct(brick_block.shape, jnp.int32)
    send_a, send_b = call(
        functools.partial(send_kernel, count),
        (message, message),
        flops=1 << 20,
        vmem=8,
        in_specs=[hbm] * 3,
        scratch=[
            pltpu.VMEM((8, 2, width, width), BF16),
            pltpu.VMEM((2, width, width), F32),
            pltpu.SemaphoreType.DMA((10,)),
        ],
    )(*(in_hbm(x) for x in (density, core, grid_old)))
    got_a, got_b = exchange_a(send_a, total), exchange_b(send_b, total)

    def band_scratch(rows):
        return pltpu.VMEM((rows, 3, width, 2 * width), BF16)

    def sides(n):
        return pltpu.VMEM((n, width, 2 * width), BF16)

    hp_shape = jax.ShapeDtypeStruct((count + 2, 3, width, 2 * width), BF16)
    inner_scratch = [band_scratch(count + 2)] * 2 + [sides(count + 2)] * 2
    outer_scratch = [band_scratch(count + 2)] * 3 + [sides(count + 2)] * 2
    hp, half_inner, place, which = call(
        functools.partial(first_inner_kernel, count),
        (hp_shape, jax.ShapeDtypeStruct(density.shape, BF16), table, table),
        flops=PROP_FLOPS,
        vmem=16,
        scalars=2,
        in_specs=[vmem] * 4,
        scratch=inner_scratch,
    )(lead_blocks, absorption, density, core, grid_old, brick_block)
    packed_rows = CAP * width // 2 + TILE
    packed_shape = jax.ShapeDtypeStruct((packed_rows, width), BF16)
    half_message = jax.ShapeDtypeStruct((6, width, width), BF16)
    half, send_b, *outgoing = call(
        functools.partial(first_outer_kernel, count, orders),
        (
            jax.ShapeDtypeStruct(density.shape, BF16),
            half_message,
        )
        + (packed_shape,) * row_size,
        flops=PROP_FLOPS,
        vmem=20,
        scalars=3,
        in_specs=[vmem] * 7,
        scratch=outer_scratch
        + [
            pltpu.VMEM((6, width, 2 * width), BF16),
            pltpu.VMEM((count, width // 2, width), BF16),
            pltpu.VMEM((count, 8, width), F32),
        ],
    )(lead_blocks, absorption, place, density, core, grid_old, got_a, got_b, hp, half_inner)


    def across(x, number):
        if number == 0:
            return x
        pairs = []
        for row in range(row_size):
            for col in range(col_size):
                pairs.append((row * col_size + col, (row ^ orders[col % 2][number]) * col_size + col))
        return lax.ppermute(x, ("row", "col"), pairs)

    half_b = exchange_b(send_b, total)
    incoming = [across(x, number) for number, x in enumerate(outgoing)]
    points = collocation.shape[1]
    arriving = []
    before = which
    ends = list(range(2, row_size - 3, 2)) + [row_size]
    for numbers in [range(a, b) for a, b in zip([0] + ends, ends)]:
        returned = call(
            functools.partial(brick_kernel, points // 4, orders, numbers),
            (packed_shape,) * len(numbers),
            flops=4 * CAP * len(numbers) * points * width**2,
            vmem=8,
            scalars=1,
            in_specs=[vmem, pl.BlockSpec(memory_space=pl.ANY)] + [vmem] * len(numbers),
        )(which, collocation, before, *(incoming[number] for number in numbers))
        arriving += [across(x, number) for number, x in zip(numbers, returned)]
        before = returned[0]

    term, diag_new, send_a, send_b = call(
        functools.partial(collect_kernel, count, orders),
        (
            jax.ShapeDtypeStruct((count, width, width), F32),
            jax.ShapeDtypeStruct((count, width, width), BF16),
            jax.ShapeDtypeStruct((7, width, width), BF16),
            jax.ShapeDtypeStruct((1, width, width), BF16),
        ),
        flops=1 << 20,
        vmem=8,
        scalars=1,
        grid=(1,),
        in_specs=[block_spec((1, count, 1, width, width), (0, 0, 1, 0, 0))] + [vmem] * (row_size + 1),
        scratch=[pltpu.VMEM((count, width // 2, width), F32), pltpu.VMEM((count, 8, width), F32)],
    )(place, core, half, *arriving)
    half_a, diag_b = exchange_a(send_a, total), exchange_b(send_b, total)

    inner, hp, grid_term = call(
        functools.partial(second_inner_kernel, count),
        (
            jax.ShapeDtypeStruct((2, count - 4, 3, width, width), BF16),
            hp_shape,
            pltpu.HBM((count, width, width), F32),
        ),
        flops=PROP_FLOPS,
        vmem=16,
        scalars=2,
        in_specs=[vmem] * 4,
        out_specs=(vmem, vmem, hbm),
        scratch=inner_scratch + [pltpu.SemaphoreType.DMA((1,))],
    )(lead_blocks, absorption, half, core, diag_new, term)
    density_next = call(
        functools.partial(second_outer_kernel, count),
        pltpu.HBM(density.shape, BF16),
        flops=PROP_FLOPS,
        vmem=16,
        scalars=2,
        in_specs=[vmem] * 10,
        out_specs=hbm,
        scratch=outer_scratch + [sides(2), pltpu.VMEM((2, 4, 3, width, width), BF16), pltpu.SemaphoreType.DMA((3,))],
    )(lead_blocks, absorption, half, core, diag_new, got_a, got_b, half_a, diag_b, half_b, hp, inner)
    return (density_next, grid_term)


def solution(mesh):
    band = P(None, ("row", "col"), None, None, None)
    blocks = P(("row", "col"), None, None)
    return jax.shard_map(
        shards,
        mesh=mesh,
        in_specs=(band, band, blocks, P(), P(), blocks, P(None, "col")),
        out_specs=(band, blocks),
        check_vma=False,
    )
```

```python
import functools

import jax
import jax.numpy as jnp
from jax import lax
from jax.experimental import pallas as pl
from jax.experimental.pallas import tpu as pltpu
from jax.sharding import PartitionSpec as P

CAP = 3
HALF_STEP = 0.2
SECOND_ORDER = 0.5 * HALF_STEP * HALF_STEP
GRID_FACTOR = 0.1
F32 = jnp.float32
BF16 = jnp.bfloat16
PROP_FLOPS = 1 << 32
MIB = 1024 * 1024
TILE = 16


def call(kernel, out_shape, flops, vmem, scalars=0, grid=(), in_specs=None, out_specs=None, scratch=()):
    whole = pl.BlockSpec(memory_space=pltpu.VMEM)
    return pl.pallas_call(
        kernel,
        out_shape=out_shape,
        grid_spec=pltpu.PrefetchScalarGridSpec(
            num_scalar_prefetch=scalars,
            grid=grid,
            in_specs=in_specs,
            out_specs=jax.tree.map(lambda _: whole, out_shape) if out_specs is None else out_specs,
            scratch_shapes=scratch,
        ),
        compiler_params=pltpu.CompilerParams(vmem_limit_bytes=vmem * MIB),
        cost_estimate=pl.CostEstimate(flops=flops, bytes_accessed=4 << 20, transcendentals=0),
    )


def in_hbm(x):
    return pltpu.with_memory_space_constraint(x, pltpu.HBM)


def block_spec(shape, index):
    return pl.BlockSpec(shape, lambda *_: index)


def joined(re, im):
    return jnp.concatenate([re, im], axis=1)


def dagger(value):
    width = value.shape[0]
    re = value[:, :width].astype(F32).T
    im = value[:, width:].astype(F32).T
    return joined(re, -im).astype(BF16)


def as_right(value):
    width = value.shape[0]
    return jnp.concatenate([value, joined(-value[:, width:], value[:, :width])], axis=0)


def band_column(left, right, j, low, high):
    total = {}
    for mid in (j - 1, j, j + 1):
        rows = [i for i in range(max(mid, j) - 1, min(mid, j) + 2) if low <= i <= high]
        if not rows:
            continue
        stacked = jnp.concatenate([left(i, mid) for i in rows], axis=0)
        result = jnp.dot(stacked, as_right(right(mid, j)), preferred_element_type=F32)
        width = result.shape[0] // len(rows)
        for n, i in enumerate(rows):
            part = result[n * width : (n + 1) * width]
            total[i] = part if i not in total else total[i] + part
    return total


def times_i(value):
    width = value.shape[0]
    return joined(-value[:, width:], value[:, :width])


def taylor_first(columns, low, high, get_left, get_q, hp_ref):
    for j in columns:
        for i, value in band_column(get_left, get_q, j, low, high).items():
            hp_ref[i + 1, j - i + 1] = value.astype(BF16)


def propagate(ranges, get_q, get_hp, get_left, get_right, moved_ref, wh_ref, write):
    def get(ref):
        return lambda i, j: ref[i + 1, j - i + 1]

    def product(left, right):
        for low, high in ranges:
            for j in range(low - 1, high + 2):
                for i, value in band_column(left, right, j, low, high).items():
                    yield i, j, value

    for i, j, value in product(get_left, get_hp):
        moved = get_q(i, j).astype(F32) - HALF_STEP * times_i(get_hp(i, j).astype(F32)) - SECOND_ORDER * value
        moved_ref[i + 1, j - i + 1] = moved.astype(BF16)
    for i, j, value in product(get(moved_ref), get_right):
        wh_ref[i + 1, j - i + 1] = value.astype(BF16)
    for i, j, value in product(get(wh_ref), get_right):
        moved = moved_ref[i + 1, j - i + 1].astype(F32)
        wh = wh_ref[i + 1, j - i + 1].astype(F32)
        write(i, j, (moved + HALF_STEP * times_i(wh) - SECOND_ORDER * value).astype(BF16))


def lanes_rows(shape):
    return lax.broadcasted_iota(jnp.int32, shape, 1), lax.broadcasted_iota(jnp.int32, shape, 0)


def pack_hermitian(re, im):
    lane, row = lanes_rows(re.shape)
    return jnp.where(row <= lane, re, im)


def unpack_hermitian(packed):
    lane, row = lanes_rows(packed.shape)
    packed = packed.astype(F32)
    turned = packed.T
    re = jnp.where(row <= lane, packed, turned)
    im = jnp.where(row > lane, packed, jnp.where(row < lane, -turned, 0.0))
    return joined(re, im).astype(BF16)


def pack_symmetric(block, folded):
    lane, row = lanes_rows(block.shape)
    half = block.shape[0] // 2
    both = jnp.where(lane == row, block, block + block.T) if folded else block
    lane, row = lanes_rows((half, block.shape[1]))
    packed = jnp.where(lane >= row, both[:half], pltpu.roll(both[half:], half, 1))
    diagonal = jnp.sum(jnp.where(lane == row + half, both[half:], 0.0), axis=0, keepdims=True)
    return packed, diagonal


def unpack_triangle(packed, diagonal):
    half, width = packed.shape
    lane, row = lanes_rows(packed.shape)
    top = jnp.where(lane >= row, packed, 0.0)
    below = jnp.where(lane < row + half, pltpu.roll(packed, half, 1), jnp.where(lane == row + half, diagonal, 0.0))
    return jnp.concatenate([top, jnp.where(lane < half, 0.0, below)], axis=0)


def symmetric(value):
    return 0.5 * (value + value.T)


def halo_message(q, q_far, h, h_far, grid):
    h_re = (h[0].astype(F32) + symmetric(grid)).astype(BF16)
    return [pack_hermitian(*q), *q_far, pack_hermitian(h_re, h[1]), *h_far]


def send_kernel(count, dens, core, grid_old, send_b, bands, grid, sems):
    even = lax.axis_index("col") % 2 == 0
    last = count - 1
    edge = jnp.where(even, 0, last)
    next_edge = jnp.where(even, 1, last - 1)
    places = [(dens, edge, 1), (dens, next_edge, jnp.where(even, 0, 2)),
              (core, edge, 1), (core, edge, jnp.where(even, 2, 0))]
    copies = [
        pltpu.make_async_copy(ref.at[:, i, k], bands.at[n], sems.at[n]) for n, (ref, i, k) in enumerate(places)
    ]
    copies.append(pltpu.make_async_copy(grid_old.at[edge], grid, sems.at[4]))
    for copy in copies:
        copy.start()
    for copy in copies:
        copy.wait()
    pairs = [(bands[n, 0], bands[n, 1]) for n in range(4)]
    for n, x in enumerate(halo_message(*pairs, grid[...])):
        send_b[n] = x


def partner(orders, n):
    even, odd = orders[0][n], orders[1][n]
    offset = even if even == odd else jnp.where(lax.axis_index("col") % 2 == 0, even, odd)
    return lax.axis_index("row") ^ offset


def halo_reader(got_a, got_b):
    even = lax.axis_index("col") % 2 == 0

    def low(n):
        return jnp.where(even, got_b[n], got_a[n])

    def high(n):
        return jnp.where(even, got_a[n], got_b[n])

    return low, high


def set_diagonals(rows, count, leads, absorption, diag_re, diag_im, left_ref, right_ref):
    width = left_ref.shape[1]
    lane, row = lanes_rows((width, width))
    first = (lax.axis_index("row") * lax.axis_size("col") + lax.axis_index("col")) * count
    for i in rows:
        re = diag_re(i)
        im = diag_im(i).astype(F32)
        gamma = jnp.float32(0.0)
        for n in range(leads.shape[0]):
            gamma += jnp.where(leads[n] == first + i, absorption[n], 0.0)
        shift = jnp.where(lane == row, gamma, 0.0)
        left_ref[i + 1] = joined(re, (im - shift).astype(BF16))
        right_ref[i + 1] = joined(re, (im + shift).astype(BF16))


def band_at(ref):
    return lambda i, j: joined(ref[0, i, j - i + 1], ref[1, i, j - i + 1])


def band_writer(ref, first=0):
    def write(i, j, value):
        width = value.shape[0]
        ref[0, i - first, j - i + 1] = value[:, :width]
        ref[1, i - first, j - i + 1] = value[:, width:]

    return write


def old_diagonals(rows, count, leads, absorption, core, grid_old, left_ref, right_ref, ends=None):
    width = core.shape[-1]

    def diag_re(i):
        if i == -1:
            return ends[0][:, :width]
        if i == count:
            return ends[1][:, :width]
        return (core[0, i, 1].astype(F32) + symmetric(grid_old[i])).astype(BF16)

    def diag_im(i):
        return ends[0][:, width:] if i == -1 else ends[1][:, width:] if i == count else core[1, i, 1]

    set_diagonals(rows, count, leads, absorption, diag_re, diag_im, left_ref, right_ref)


def new_diagonals(rows, count, leads, absorption, core, diag_new, left_ref, right_ref, ends=None, ends_re=None):
    width = core.shape[-1]

    def diag_re(i):
        if i == -1:
            return ends_re[0]
        if i == count:
            return ends_re[1]
        return diag_new[i]

    def diag_im(i):
        return ends[0][:, width:] if i == -1 else ends[1][:, width:] if i == count else core[1, i, 1]

    set_diagonals(rows, count, leads, absorption, diag_re, diag_im, left_ref, right_ref)


def band_access(count, core, far_low, far_high, low_edge, high_edge, diag_ref):
    def get(i, j):
        if i == j:
            return diag_ref[i + 1]
        if i == -1:
            return far_low() if j == -2 else low_edge[...]
        if i == count:
            return far_high() if j == count + 1 else high_edge[...]
        return joined(core[0, i, j - i + 1], core[1, i, j - i + 1])

    return get


def put_half(count, half, target, start, right):
    last = count - 1
    blocks = [(last, 1), (last, 2), (last - 1, 2)] if right else [(0, 1), (0, 0), (1, 0)]
    for n, (i, k) in enumerate(blocks):
        for part in range(2):
            target[start + 2 * n + part] = half[part, i, k]


def brick_tables(count, owners, place, which):
    lane, row = lanes_rows(owners.shape)
    own = lax.axis_index("row")
    source = owners[...] // count // lax.axis_size("col")
    slot = jnp.zeros(owners.shape, jnp.int32)
    for t in range(owners.shape[1] - 1):
        slot += jnp.where((lane > t) & (source == source[:, t : t + 1]), 1, 0)
    mine = jnp.where(source == own, owners[...] % count, -1)
    own_source = jnp.sum(jnp.where(row == own, source, 0), axis=0, keepdims=True)
    own_slot = jnp.sum(jnp.where(row == own, slot, 0), axis=0, keepdims=True)
    here = own_source == row
    places = jnp.zeros(owners.shape, jnp.int32)
    bricks = jnp.zeros(owners.shape, jnp.int32)
    for n in range(CAP):
        places = jnp.where(lane == n, jnp.max(jnp.where(slot == n, mine, -1), axis=1, keepdims=True), places)
        brick = jnp.max(jnp.where(here & (own_slot == n), lane, 0), axis=1, keepdims=True)
        bricks = jnp.where(lane == n, brick, bricks)
    place[...] = places
    which[...] = bricks


def first_inner_kernel(count, leads, absorption, dens, core, grid_old, owners, hp_ref, half, place, which, send_a, moved_ref, wh_ref, left_ref, right_ref):
    brick_tables(count, owners, place, which)
    even = lax.axis_index("col") % 2 == 0
    last = count - 1

    def put_message(edge, next_edge, near, far):
        places = [(dens, edge, 1), (dens, next_edge, near), (core, edge, 1), (core, edge, far)]
        pairs = [(ref[0, i, k], ref[1, i, k]) for ref, i, k in places]
        for n, x in enumerate(halo_message(*pairs, grid_old[edge])):
            send_a[n] = x

    @pl.when(even)
    def _():
        put_message(last, last - 1, 2, 0)

    @pl.when(jnp.logical_not(even))
    def _():
        put_message(0, 1, 0, 2)

    old_diagonals(range(count), count, leads, absorption, core, grid_old, left_ref, right_ref)
    get_left = band_access(count, core, None, None, None, None, left_ref)
    get_right = band_access(count, core, None, None, None, None, right_ref)
    get_q = band_at(dens)

    def get_hp(i, j):
        return hp_ref[i + 1, j - i + 1]

    taylor_first(range(count), 1, count - 2, get_left, get_q, hp_ref)
    propagate([(2, count - 3)], get_q, get_hp, get_left, get_right, moved_ref, wh_ref, band_writer(half))


def first_outer_kernel(count, orders, leads, absorption, place, dens, core, grid_old, got_a, got_b, hp_in, half_in,
                       half, send_b, *rest):
    outgoing, (hp_ref, moved_ref, wh_ref, left_ref, right_ref, edges, packed, diagonals) = rest[:-8], rest[-8:]
    low, high = halo_reader(got_a, got_b)
    last = count - 1
    edges[0] = dagger(band_at(dens)(0, -1))
    edges[1] = dagger(band_at(dens)(last, count))
    edges[2] = dagger(band_at(core)(0, -1))
    edges[3] = dagger(band_at(core)(last, count))
    edges[4] = unpack_hermitian(low(0))
    edges[5] = unpack_hermitian(high(0))
    ends = unpack_hermitian(low(3)), unpack_hermitian(high(3))
    rows = [-1, 0, 1, 2, count - 3, count - 2, last, count]
    old_diagonals(rows, count, leads, absorption, core, grid_old, left_ref, right_ref, ends)
    half[:, 2 : count - 2] = half_in[:, 2 : count - 2]

    def get_q(i, j):
        if i == -2:
            return joined(low(1), low(2))
        if i == -1:
            return edges[4] if j == -1 else edges[0]
        if i == count:
            return edges[5] if j == count else edges[1]
        if i == count + 1:
            return joined(high(1), high(2))
        return band_at(dens)(i, j)

    def get_hp(i, j):
        ref = hp_in if 1 <= i <= count - 2 else hp_ref
        return ref[i + 1, j - i + 1]

    def far_low():
        return joined(low(4), low(5))

    def far_high():
        return joined(high(4), high(5))

    get_left = band_access(count, core, far_low, far_high, edges.at[2], edges.at[3], left_ref)
    get_right = band_access(count, core, far_low, far_high, edges.at[2], edges.at[3], right_ref)
    write = band_writer(half)
    taylor_first(range(-1, 2), -1, 0, get_left, get_q, hp_ref)
    taylor_first(range(last - 1, count + 1), last, count, get_left, get_q, hp_ref)
    propagate([(0, 1), (last - 1, last)], get_q, get_hp, get_left, get_right, moved_ref, wh_ref, write)

    even = lax.axis_index("col") % 2 == 0

    @pl.when(even)
    def _():
        put_half(count, half, send_b, 0, False)

    @pl.when(jnp.logical_not(even))
    def _():
        put_half(count, half, send_b, 0, True)

    for i in range(count):
        top, diagonal = pack_symmetric(half[0, i, 1].astype(F32), True)
        packed[i] = top.astype(BF16)
        diagonals[i] = jnp.broadcast_to(diagonal, diagonals.shape[1:])

    height, width = packed.shape[1:]
    _, row = lanes_rows((TILE, width))

    for number, out in enumerate(outgoing):
        p = partner(orders, number)
        tail = jnp.zeros((TILE, width), F32)
        for n in range(CAP):
            source = jnp.maximum(place[p, n], 0)
            out[n * height : (n + 1) * height] = packed[source]
            tail = jnp.where(row == n, diagonals[source][:1], tail)
        out[CAP * height :] = tail.astype(BF16)


def brick_kernel(chunk, orders, numbers, which, colloc, unread, *rest):
    incoming, returned = rest[: len(numbers)], rest[len(numbers) :]
    points, width = colloc.shape[1:]
    scale = GRID_FACTOR * width / points
    height = width // 2
    _, tail_row = lanes_rows((TILE, width))
    tails = [jnp.zeros((TILE, width), F32) for _ in numbers]
    jobs = [(m, n, which[partner(orders, number), n]) for m, number in enumerate(numbers) for n in range(CAP)]

    def block(job):
        m, n, _ = job
        last = incoming[m][CAP * height :].astype(F32)
        return unpack_triangle(incoming[m][n * height : (n + 1) * height].astype(F32), last[n : n + 1])

    def put(job, result):
        m, n, _ = job
        packed, diagonal = pack_symmetric(scale * result, False)
        returned[m][n * height : (n + 1) * height] = packed.astype(BF16)
        tails[m] = jnp.where(tail_row == n, diagonal, tails[m])

    for first, second in zip(jobs[::2], jobs[1::2]):
        c0, c1 = colloc.at[first[2]], colloc.at[second[2]]
        q0, q1 = block(first), block(second)
        zero = jnp.zeros_like(q0)
        both = jnp.concatenate([joined(q0, zero), joined(zero, q1)], axis=0).astype(BF16)
        columns = []
        for g in range(0, points, chunk):
            turned = jnp.concatenate([c0[g : g + chunk].T, c1[g : g + chunk].T], axis=0)
            wide = turned.astype(F32)
            projected = jnp.dot(both, turned, preferred_element_type=F32) * wide
            weighted = []
            for n in range(2):
                rows = slice(n * width, (n + 1) * width)
                dens = jnp.sum(projected[rows], axis=0, keepdims=True)
                potential = dens * lax.rsqrt(1.0 + dens * dens)
                weighted.append((potential * wide[rows]).astype(BF16))
            columns.append(jnp.concatenate(weighted, axis=0))
        result = jnp.dot(jnp.concatenate(columns, axis=1), joined(c0[...], c1[...]), preferred_element_type=F32)
        put(first, result[:width, :width])
        put(second, result[width:, width:])
    for out, tail in zip(returned, tails):
        out[CAP * height :] = tail.astype(BF16)


def collect_kernel(count, orders, place, core, half, *rest):
    arriving, (term, diag_new, send_a, send_b, total, tails) = rest[:-6], rest[-6:]
    width = core.shape[-1]
    height = width // 2
    total[...] = jnp.zeros_like(total)
    tails[...] = jnp.zeros_like(tails)
    for number, block in enumerate(arriving):
        p = partner(orders, number)
        last = block[CAP * height :].astype(F32)
        for n in range(CAP):
            at = place[p, n]
            kept = at >= 0
            at = jnp.maximum(at, 0)
            total[at] += jnp.where(kept, block[n * height : (n + 1) * height].astype(F32), 0.0)
            tails[at] += jnp.where(kept, last[n : n + 1], 0.0)
    lane, row = lanes_rows((width, width))
    for i in range(count):
        triangle = unpack_triangle(total[i], tails[i][:1])
        whole = jnp.where(lane == row, triangle, triangle + triangle.T)
        term[i] = whole
        diag_new[i] = (core[0, i, 0].astype(F32) + whole).astype(BF16)

    even = lax.axis_index("col") % 2 == 0
    last = count - 1

    @pl.when(even)
    def _():
        send_a[0] = diag_new[last]
        send_b[0] = diag_new[0]
        put_half(count, half, send_a, 1, True)

    @pl.when(jnp.logical_not(even))
    def _():
        send_a[0] = diag_new[0]
        send_b[0] = diag_new[last]
        put_half(count, half, send_a, 1, False)


def second_inner_kernel(count, leads, absorption, half, core, diag_new, term, out, hp_ref, grid_term,
                        moved_ref, wh_ref, left_ref, right_ref, sem):
    copy = pltpu.make_async_copy(term, grid_term, sem.at[0])
    copy.start()
    new_diagonals(range(count), count, leads, absorption, core, diag_new, left_ref, right_ref)
    get_left = band_access(count, core, None, None, None, None, left_ref)
    get_right = band_access(count, core, None, None, None, None, right_ref)
    get_q = band_at(half)

    def get_hp(i, j):
        return hp_ref[i + 1, j - i + 1]

    taylor_first(range(count), 1, count - 2, get_left, get_q, hp_ref)
    propagate([(2, count - 3)], get_q, get_hp, get_left, get_right, moved_ref, wh_ref, band_writer(out, 2))
    copy.wait()


def second_outer_kernel(count, leads, absorption, half, core, diag_new, core_a, core_b, got_a, got_b, half_b,
                        hp_in, inner, out, hp_ref, moved_ref, wh_ref, left_ref, right_ref, edges, ready, sems):
    copies = [pltpu.make_async_copy(inner, out.at[:, pl.ds(2, count - 4)], sems.at[2])]
    for n, i in enumerate((0, count - 2)):
        copies.append(pltpu.make_async_copy(ready.at[:, pl.ds(2 * n, 2)], out.at[:, pl.ds(i, 2)], sems.at[n]))
    copies[0].start()
    core_low, core_high = halo_reader(core_a, core_b)
    even = lax.axis_index("col") % 2 == 0

    def low(n):
        return jnp.where(even, got_b[0] if n == 0 else half_b[n - 1], got_a[n])

    def high(n):
        return jnp.where(even, got_a[n], got_b[0] if n == 0 else half_b[n - 1])

    last = count - 1
    edges[0] = dagger(band_at(core)(0, -1))
    edges[1] = dagger(band_at(core)(last, count))
    ends = unpack_hermitian(core_low(3)), unpack_hermitian(core_high(3))
    rows = [-1, 0, 1, 2, count - 3, count - 2, last, count]
    new_diagonals(rows, count, leads, absorption, core, diag_new, left_ref, right_ref, ends, (low(0), high(0)))

    def get_q(i, j):
        if 0 <= i < count:
            return band_at(half)(i, j)
        n = 1 if i == j else 3 if i in (-1, count) else 5
        side = low if i < 0 else high
        return joined(side(n), side(n + 1))

    def far_low():
        return joined(core_low(4), core_low(5))

    def far_high():
        return joined(core_high(4), core_high(5))

    get_left = band_access(count, core, far_low, far_high, edges.at[0], edges.at[1], left_ref)
    get_right = band_access(count, core, far_low, far_high, edges.at[0], edges.at[1], right_ref)

    def get_hp(i, j):
        ref = hp_in if 1 <= i <= count - 2 else hp_ref
        return ref[i + 1, j - i + 1]

    def write(i, j, value):
        width = value.shape[0]
        n = i if i < 2 else i - count + 4
        ready[0, n, j - i + 1] = value[:, :width]
        ready[1, n, j - i + 1] = value[:, width:]
        if (i, j) == (1, 2):
            copies[1].start()
        if (i, j) == (last, count):
            copies[2].start()

    taylor_first(range(-1, 2), -1, 0, get_left, get_q, hp_ref)
    taylor_first(range(last - 1, count + 1), last, count, get_left, get_q, hp_ref)
    propagate([(0, 1), (last - 1, last)], get_q, get_hp, get_left, get_right, moved_ref, wh_ref, write)
    for copy in copies:
        copy.wait()


def exchange_a(x, total):
    return lax.ppermute(x, ("row", "col"), [(i, i ^ 1) for i in range(total)])


def exchange_b(x, total):
    return lax.ppermute(x, ("row", "col"), [(i, i + 1) if i % 2 else (i, i - 1) for i in range(1, total - 1)])


def shards(density, core, grid_old, lead_blocks, absorption, collocation, brick_block):
    count = density.shape[1]
    width = density.shape[-1]
    row_size = lax.axis_size("row")
    col_size = lax.axis_size("col")
    total = row_size * col_size
    near, far = list(range(1, row_size // 2)), list(range(row_size // 2, row_size))
    orders = [[0] + far + near, [0] + far + near]
    bricks = brick_block.shape[1]
    vmem = pl.BlockSpec(memory_space=pltpu.VMEM)
    hbm = pl.BlockSpec(memory_space=pltpu.HBM)

    message = jax.ShapeDtypeStruct((6, width, width), BF16)
    table = jax.ShapeDtypeStruct(brick_block.shape, jnp.int32)
    send_b = call(
        functools.partial(send_kernel, count),
        message,
        flops=1 << 20,
        vmem=8,
        in_specs=[hbm] * 3,
        scratch=[
            pltpu.VMEM((4, 2, width, width), BF16),
            pltpu.VMEM((width, width), F32),
            pltpu.SemaphoreType.DMA((5,)),
        ],
    )(*(in_hbm(x) for x in (density, core, grid_old)))
    got_b = exchange_b(send_b, total)

    def band_scratch(rows):
        return pltpu.VMEM((rows, 3, width, 2 * width), BF16)

    def sides(n):
        return pltpu.VMEM((n, width, 2 * width), BF16)

    hp_shape = jax.ShapeDtypeStruct((count + 2, 3, width, 2 * width), BF16)
    inner_scratch = [band_scratch(count + 2)] * 2 + [sides(count + 2)] * 2
    outer_scratch = [band_scratch(count + 2)] * 3 + [sides(count + 2)] * 2
    hp, half_inner, place, which, send_a = call(
        functools.partial(first_inner_kernel, count),
        (hp_shape, jax.ShapeDtypeStruct(density.shape, BF16), table, table, message),
        flops=PROP_FLOPS,
        vmem=16,
        scalars=2,
        in_specs=[vmem] * 4,
        scratch=inner_scratch,
    )(lead_blocks, absorption, density, core, grid_old, brick_block)
    got_a = exchange_a(send_a, total)
    packed_rows = CAP * width // 2 + TILE
    packed_shape = jax.ShapeDtypeStruct((packed_rows, width), BF16)
    half_message = jax.ShapeDtypeStruct((6, width, width), BF16)
    half, send_b, *outgoing = call(
        functools.partial(first_outer_kernel, count, orders),
        (
            jax.ShapeDtypeStruct(density.shape, BF16),
            half_message,
        )
        + (packed_shape,) * row_size,
        flops=PROP_FLOPS,
        vmem=20,
        scalars=3,
        in_specs=[vmem] * 7,
        scratch=outer_scratch
        + [
            pltpu.VMEM((6, width, 2 * width), BF16),
            pltpu.VMEM((count, width // 2, width), BF16),
            pltpu.VMEM((count, 8, width), F32),
        ],
    )(lead_blocks, absorption, place, density, core, grid_old, got_a, got_b, hp, half_inner)


    def across(x, number):
        if number == 0:
            return x
        pairs = []
        for row in range(row_size):
            for col in range(col_size):
                pairs.append((row * col_size + col, (row ^ orders[col % 2][number]) * col_size + col))
        return lax.ppermute(x, ("row", "col"), pairs)

    half_b = exchange_b(send_b, total)
    incoming = [across(x, number) for number, x in enumerate(outgoing)]
    points = collocation.shape[1]
    arriving = []
    before = which
    ends = list(range(2, row_size - 3, 2)) + [row_size]
    for numbers in [range(a, b) for a, b in zip([0] + ends, ends)]:
        returned = call(
            functools.partial(brick_kernel, points // 4, orders, numbers),
            (packed_shape,) * len(numbers),
            flops=4 * CAP * len(numbers) * points * width**2,
            vmem=8,
            scalars=1,
            in_specs=[vmem, pl.BlockSpec(memory_space=pl.ANY)] + [vmem] * len(numbers),
        )(which, collocation, before, *(incoming[number] for number in numbers))
        arriving += [across(x, number) for number, x in zip(numbers, returned)]
        before = returned[0]

    term, diag_new, send_a, send_b = call(
        functools.partial(collect_kernel, count, orders),
        (
            jax.ShapeDtypeStruct((count, width, width), F32),
            jax.ShapeDtypeStruct((count, width, width), BF16),
            jax.ShapeDtypeStruct((7, width, width), BF16),
            jax.ShapeDtypeStruct((1, width, width), BF16),
        ),
        flops=1 << 20,
        vmem=8,
        scalars=1,
        grid=(1,),
        in_specs=[block_spec((1, count, 1, width, width), (0, 0, 1, 0, 0))] + [vmem] * (row_size + 1),
        scratch=[pltpu.VMEM((count, width // 2, width), F32), pltpu.VMEM((count, 8, width), F32)],
    )(place, core, half, *arriving)
    half_a, diag_b = exchange_a(send_a, total), exchange_b(send_b, total)

    inner, hp, grid_term = call(
        functools.partial(second_inner_kernel, count),
        (
            jax.ShapeDtypeStruct((2, count - 4, 3, width, width), BF16),
            hp_shape,
            pltpu.HBM((count, width, width), F32),
        ),
        flops=PROP_FLOPS,
        vmem=16,
        scalars=2,
        in_specs=[vmem] * 4,
        out_specs=(vmem, vmem, hbm),
        scratch=inner_scratch + [pltpu.SemaphoreType.DMA((1,))],
    )(lead_blocks, absorption, half, core, diag_new, term)
    density_next = call(
        functools.partial(second_outer_kernel, count),
        pltpu.HBM(density.shape, BF16),
        flops=PROP_FLOPS,
        vmem=16,
        scalars=2,
        in_specs=[vmem] * 10,
        out_specs=hbm,
        scratch=outer_scratch + [sides(2), pltpu.VMEM((2, 4, 3, width, width), BF16), pltpu.SemaphoreType.DMA((3,))],
    )(lead_blocks, absorption, half, core, diag_new, got_a, got_b, half_a, diag_b, half_b, hp, inner)
    return (density_next, grid_term)


def solution(mesh):
    band = P(None, ("row", "col"), None, None, None)
    blocks = P(("row", "col"), None, None)
    return jax.shard_map(
        shards,
        mesh=mesh,
        in_specs=(band, band, blocks, P(), P(), blocks, P(None, "col")),
        out_specs=(band, blocks),
        check_vma=False,
    )
```

```python
import functools

import jax
import jax.numpy as jnp
from jax import lax
from jax.experimental import pallas as pl
from jax.experimental.pallas import tpu as pltpu
from jax.sharding import PartitionSpec as P

CAP = 3
HALF_STEP = 0.2
SECOND_ORDER = 0.5 * HALF_STEP * HALF_STEP
GRID_FACTOR = 0.1
F32 = jnp.float32
BF16 = jnp.bfloat16
PROP_FLOPS = 1 << 32
MIB = 1024 * 1024
TILE = 16


def call(kernel, out_shape, flops, vmem, scalars=0, grid=(), in_specs=None, out_specs=None, scratch=()):
    whole = pl.BlockSpec(memory_space=pltpu.VMEM)
    return pl.pallas_call(
        kernel,
        out_shape=out_shape,
        grid_spec=pltpu.PrefetchScalarGridSpec(
            num_scalar_prefetch=scalars,
            grid=grid,
            in_specs=in_specs,
            out_specs=jax.tree.map(lambda _: whole, out_shape) if out_specs is None else out_specs,
            scratch_shapes=scratch,
        ),
        compiler_params=pltpu.CompilerParams(vmem_limit_bytes=vmem * MIB),
        cost_estimate=pl.CostEstimate(flops=flops, bytes_accessed=4 << 20, transcendentals=0),
    )


def in_hbm(x):
    return pltpu.with_memory_space_constraint(x, pltpu.HBM)


def block_spec(shape, index):
    return pl.BlockSpec(shape, lambda *_: index)


def joined(re, im):
    return jnp.concatenate([re, im], axis=1)


def dagger(value):
    width = value.shape[0]
    re = value[:, :width].astype(F32).T
    im = value[:, width:].astype(F32).T
    return joined(re, -im).astype(BF16)


def as_right(value):
    width = value.shape[0]
    return jnp.concatenate([value, joined(-value[:, width:], value[:, :width])], axis=0)


def band_column(left, right, j, low, high):
    total = {}
    for mid in (j - 1, j, j + 1):
        rows = [i for i in range(max(mid, j) - 1, min(mid, j) + 2) if low <= i <= high]
        if not rows:
            continue
        stacked = jnp.concatenate([left(i, mid) for i in rows], axis=0)
        result = jnp.dot(stacked, as_right(right(mid, j)), preferred_element_type=F32)
        width = result.shape[0] // len(rows)
        for n, i in enumerate(rows):
            part = result[n * width : (n + 1) * width]
            total[i] = part if i not in total else total[i] + part
    return total


def times_i(value):
    width = value.shape[0]
    return joined(-value[:, width:], value[:, :width])


def taylor_first(columns, low, high, get_left, get_q, hp_ref):
    for j in columns:
        for i, value in band_column(get_left, get_q, j, low, high).items():
            hp_ref[i + 1, j - i + 1] = value.astype(BF16)


def propagate(ranges, get_q, get_hp, get_left, get_right, moved_ref, wh_ref, write):
    def get(ref):
        return lambda i, j: ref[i + 1, j - i + 1]

    def product(left, right):
        for low, high in ranges:
            for j in range(low - 1, high + 2):
                for i, value in band_column(left, right, j, low, high).items():
                    yield i, j, value

    for i, j, value in product(get_left, get_hp):
        moved = get_q(i, j).astype(F32) - HALF_STEP * times_i(get_hp(i, j).astype(F32)) - SECOND_ORDER * value
        moved_ref[i + 1, j - i + 1] = moved.astype(BF16)
    for i, j, value in product(get(moved_ref), get_right):
        wh_ref[i + 1, j - i + 1] = value.astype(BF16)
    for i, j, value in product(get(wh_ref), get_right):
        moved = moved_ref[i + 1, j - i + 1].astype(F32)
        wh = wh_ref[i + 1, j - i + 1].astype(F32)
        write(i, j, (moved + HALF_STEP * times_i(wh) - SECOND_ORDER * value).astype(BF16))


def lanes_rows(shape):
    return lax.broadcasted_iota(jnp.int32, shape, 1), lax.broadcasted_iota(jnp.int32, shape, 0)


def pack_hermitian(re, im):
    lane, row = lanes_rows(re.shape)
    return jnp.where(row <= lane, re, im)


def unpack_hermitian(packed):
    lane, row = lanes_rows(packed.shape)
    packed = packed.astype(F32)
    turned = packed.T
    re = jnp.where(row <= lane, packed, turned)
    im = jnp.where(row > lane, packed, jnp.where(row < lane, -turned, 0.0))
    return joined(re, im).astype(BF16)


def pack_symmetric(block, folded):
    lane, row = lanes_rows(block.shape)
    half = block.shape[0] // 2
    both = jnp.where(lane == row, block, block + block.T) if folded else block
    lane, row = lanes_rows((half, block.shape[1]))
    packed = jnp.where(lane >= row, both[:half], pltpu.roll(both[half:], half, 1))
    diagonal = jnp.sum(jnp.where(lane == row + half, both[half:], 0.0), axis=0, keepdims=True)
    return packed, diagonal


def unpack_triangle(packed, diagonal):
    half, width = packed.shape
    lane, row = lanes_rows(packed.shape)
    top = jnp.where(lane >= row, packed, 0.0)
    below = jnp.where(lane < row + half, pltpu.roll(packed, half, 1), jnp.where(lane == row + half, diagonal, 0.0))
    return jnp.concatenate([top, jnp.where(lane < half, 0.0, below)], axis=0)


def symmetric(value):
    return 0.5 * (value + value.T)


def halo_message(q, q_far, h, h_far, grid):
    h_re = (h[0].astype(F32) + symmetric(grid)).astype(BF16)
    return [pack_hermitian(*q), *q_far, pack_hermitian(h_re, h[1]), *h_far]


def send_kernel(count, dens, core, grid_old, send_b, bands, grid, sems):
    even = lax.axis_index("col") % 2 == 0
    last = count - 1
    edge = jnp.where(even, 0, last)
    next_edge = jnp.where(even, 1, last - 1)
    places = [(dens, edge, 1), (dens, next_edge, jnp.where(even, 0, 2)),
              (core, edge, 1), (core, edge, jnp.where(even, 2, 0))]
    copies = [
        pltpu.make_async_copy(ref.at[:, i, k], bands.at[n], sems.at[n]) for n, (ref, i, k) in enumerate(places)
    ]
    copies.append(pltpu.make_async_copy(grid_old.at[edge], grid, sems.at[4]))
    for copy in copies:
        copy.start()
    for copy in copies:
        copy.wait()
    pairs = [(bands[n, 0], bands[n, 1]) for n in range(4)]
    for n, x in enumerate(halo_message(*pairs, grid[...])):
        send_b[n] = x


def partner(orders, n):
    even, odd = orders[0][n], orders[1][n]
    offset = even if even == odd else jnp.where(lax.axis_index("col") % 2 == 0, even, odd)
    return lax.axis_index("row") ^ offset


def halo_reader(got_a, got_b):
    even = lax.axis_index("col") % 2 == 0

    def low(n):
        return jnp.where(even, got_b[n], got_a[n])

    def high(n):
        return jnp.where(even, got_a[n], got_b[n])

    return low, high


def set_diagonals(rows, count, leads, absorption, diag_re, diag_im, left_ref, right_ref):
    width = left_ref.shape[1]
    lane, row = lanes_rows((width, width))
    first = (lax.axis_index("row") * lax.axis_size("col") + lax.axis_index("col")) * count
    for i in rows:
        re = diag_re(i)
        im = diag_im(i).astype(F32)
        gamma = jnp.float32(0.0)
        for n in range(leads.shape[0]):
            gamma += jnp.where(leads[n] == first + i, absorption[n], 0.0)
        shift = jnp.where(lane == row, gamma, 0.0)
        left_ref[i + 1] = joined(re, (im - shift).astype(BF16))
        right_ref[i + 1] = joined(re, (im + shift).astype(BF16))


def band_at(ref):
    return lambda i, j: joined(ref[0, i, j - i + 1], ref[1, i, j - i + 1])


def band_writer(ref, first=0):
    def write(i, j, value):
        width = value.shape[0]
        ref[0, i - first, j - i + 1] = value[:, :width]
        ref[1, i - first, j - i + 1] = value[:, width:]

    return write


def old_diagonals(rows, count, leads, absorption, core, grid_old, left_ref, right_ref, ends=None):
    width = core.shape[-1]

    def diag_re(i):
        if i == -1:
            return ends[0][:, :width]
        if i == count:
            return ends[1][:, :width]
        return (core[0, i, 1].astype(F32) + symmetric(grid_old[i])).astype(BF16)

    def diag_im(i):
        return ends[0][:, width:] if i == -1 else ends[1][:, width:] if i == count else core[1, i, 1]

    set_diagonals(rows, count, leads, absorption, diag_re, diag_im, left_ref, right_ref)


def new_diagonals(rows, count, leads, absorption, core, diag_new, left_ref, right_ref, ends=None, ends_re=None):
    width = core.shape[-1]

    def diag_re(i):
        if i == -1:
            return ends_re[0]
        if i == count:
            return ends_re[1]
        return diag_new[i]

    def diag_im(i):
        return ends[0][:, width:] if i == -1 else ends[1][:, width:] if i == count else core[1, i, 1]

    set_diagonals(rows, count, leads, absorption, diag_re, diag_im, left_ref, right_ref)


def band_access(count, core, far_low, far_high, low_edge, high_edge, diag_ref):
    def get(i, j):
        if i == j:
            return diag_ref[i + 1]
        if i == -1:
            return far_low() if j == -2 else low_edge[...]
        if i == count:
            return far_high() if j == count + 1 else high_edge[...]
        return joined(core[0, i, j - i + 1], core[1, i, j - i + 1])

    return get


def put_half(count, half, target, start, right):
    last = count - 1
    blocks = [(last, 1), (last, 2), (last - 1, 2)] if right else [(0, 1), (0, 0), (1, 0)]
    for n, (i, k) in enumerate(blocks):
        for part in range(2):
            target[start + 2 * n + part] = half[part, i, k]


def brick_tables(count, owners, place, which):
    lane, row = lanes_rows(owners.shape)
    own = lax.axis_index("row")
    source = owners[...] // count // lax.axis_size("col")
    slot = jnp.zeros(owners.shape, jnp.int32)
    for t in range(owners.shape[1] - 1):
        slot += jnp.where((lane > t) & (source == source[:, t : t + 1]), 1, 0)
    mine = jnp.where(source == own, owners[...] % count, -1)
    own_source = jnp.sum(jnp.where(row == own, source, 0), axis=0, keepdims=True)
    own_slot = jnp.sum(jnp.where(row == own, slot, 0), axis=0, keepdims=True)
    here = own_source == row
    places = jnp.zeros(owners.shape, jnp.int32)
    bricks = jnp.zeros(owners.shape, jnp.int32)
    for n in range(CAP):
        places = jnp.where(lane == n, jnp.max(jnp.where(slot == n, mine, -1), axis=1, keepdims=True), places)
        brick = jnp.max(jnp.where(here & (own_slot == n), lane, 0), axis=1, keepdims=True)
        bricks = jnp.where(lane == n, brick, bricks)
    place[...] = places
    which[...] = bricks


def first_inner_kernel(count, leads, absorption, dens, core, grid_old, owners, hp_ref, half, place, which, send_a, moved_ref, wh_ref, left_ref, right_ref):
    brick_tables(count, owners, place, which)
    even = lax.axis_index("col") % 2 == 0
    last = count - 1

    def put_message(edge, next_edge, near, far):
        places = [(dens, edge, 1), (dens, next_edge, near), (core, edge, 1), (core, edge, far)]
        pairs = [(ref[0, i, k], ref[1, i, k]) for ref, i, k in places]
        for n, x in enumerate(halo_message(*pairs, grid_old[edge])):
            send_a[n] = x

    @pl.when(even)
    def _():
        put_message(last, last - 1, 2, 0)

    @pl.when(jnp.logical_not(even))
    def _():
        put_message(0, 1, 0, 2)

    old_diagonals(range(count), count, leads, absorption, core, grid_old, left_ref, right_ref)
    get_left = band_access(count, core, None, None, None, None, left_ref)
    get_right = band_access(count, core, None, None, None, None, right_ref)
    get_q = band_at(dens)

    def get_hp(i, j):
        return hp_ref[i + 1, j - i + 1]

    taylor_first(range(count), 1, count - 2, get_left, get_q, hp_ref)
    propagate([(2, count - 3)], get_q, get_hp, get_left, get_right, moved_ref, wh_ref, band_writer(half))


def first_outer_kernel(count, orders, leads, absorption, place, dens, core, grid_old, got_a, got_b, hp_in, half_in,
                       half, send_b, *rest):
    outgoing, (hp_ref, moved_ref, wh_ref, left_ref, right_ref, edges, packed, diagonals) = rest[:-8], rest[-8:]
    low, high = halo_reader(got_a, got_b)
    last = count - 1
    edges[0] = dagger(band_at(dens)(0, -1))
    edges[1] = dagger(band_at(dens)(last, count))
    edges[2] = dagger(band_at(core)(0, -1))
    edges[3] = dagger(band_at(core)(last, count))
    edges[4] = unpack_hermitian(low(0))
    edges[5] = unpack_hermitian(high(0))
    ends = unpack_hermitian(low(3)), unpack_hermitian(high(3))
    rows = [-1, 0, 1, 2, count - 3, count - 2, last, count]
    old_diagonals(rows, count, leads, absorption, core, grid_old, left_ref, right_ref, ends)
    half[:, 2 : count - 2] = half_in[:, 2 : count - 2]

    def get_q(i, j):
        if i == -2:
            return joined(low(1), low(2))
        if i == -1:
            return edges[4] if j == -1 else edges[0]
        if i == count:
            return edges[5] if j == count else edges[1]
        if i == count + 1:
            return joined(high(1), high(2))
        return band_at(dens)(i, j)

    def get_hp(i, j):
        ref = hp_in if 1 <= i <= count - 2 else hp_ref
        return ref[i + 1, j - i + 1]

    def far_low():
        return joined(low(4), low(5))

    def far_high():
        return joined(high(4), high(5))

    get_left = band_access(count, core, far_low, far_high, edges.at[2], edges.at[3], left_ref)
    get_right = band_access(count, core, far_low, far_high, edges.at[2], edges.at[3], right_ref)
    write = band_writer(half)
    taylor_first(range(-1, 2), -1, 0, get_left, get_q, hp_ref)
    taylor_first(range(last - 1, count + 1), last, count, get_left, get_q, hp_ref)
    propagate([(0, 1), (last - 1, last)], get_q, get_hp, get_left, get_right, moved_ref, wh_ref, write)

    even = lax.axis_index("col") % 2 == 0

    @pl.when(even)
    def _():
        put_half(count, half, send_b, 0, False)

    @pl.when(jnp.logical_not(even))
    def _():
        put_half(count, half, send_b, 0, True)

    for i in range(count):
        top, diagonal = pack_symmetric(half[0, i, 1].astype(F32), True)
        packed[i] = top.astype(BF16)
        diagonals[i] = jnp.broadcast_to(diagonal, diagonals.shape[1:])

    height, width = packed.shape[1:]
    _, row = lanes_rows((TILE, width))

    for number, out in enumerate(outgoing):
        p = partner(orders, number)
        tail = jnp.zeros((TILE, width), F32)
        for n in range(CAP):
            source = jnp.maximum(place[p, n], 0)
            out[n * height : (n + 1) * height] = packed[source]
            tail = jnp.where(row == n, diagonals[source][:1], tail)
        out[CAP * height :] = tail.astype(BF16)


def brick_kernel(chunk, orders, numbers, which, colloc, unread, *rest):
    incoming, returned = rest[: len(numbers)], rest[len(numbers) :]
    points, width = colloc.shape[1:]
    scale = GRID_FACTOR * width / points
    height = width // 2
    _, tail_row = lanes_rows((TILE, width))
    tails = [jnp.zeros((TILE, width), F32) for _ in numbers]
    jobs = [(m, n, which[partner(orders, number), n]) for m, number in enumerate(numbers) for n in range(CAP)]

    def block(job):
        m, n, _ = job
        last = incoming[m][CAP * height :].astype(F32)
        return unpack_triangle(incoming[m][n * height : (n + 1) * height].astype(F32), last[n : n + 1])

    def put(job, result):
        m, n, _ = job
        packed, diagonal = pack_symmetric(scale * result, False)
        returned[m][n * height : (n + 1) * height] = packed.astype(BF16)
        tails[m] = jnp.where(tail_row == n, diagonal, tails[m])

    for first, second in zip(jobs[::2], jobs[1::2]):
        c0, c1 = colloc.at[first[2]], colloc.at[second[2]]
        q0, q1 = block(first), block(second)
        zero = jnp.zeros_like(q0)
        both = jnp.concatenate([joined(q0, zero), joined(zero, q1)], axis=0).astype(BF16)
        columns = []
        for g in range(0, points, chunk):
            turned = jnp.concatenate([c0[g : g + chunk].T, c1[g : g + chunk].T], axis=0)
            wide = turned.astype(F32)
            projected = jnp.dot(both, turned, preferred_element_type=F32) * wide
            weighted = []
            for n in range(2):
                rows = slice(n * width, (n + 1) * width)
                dens = jnp.sum(projected[rows], axis=0, keepdims=True)
                potential = dens * lax.rsqrt(1.0 + dens * dens)
                weighted.append((potential * wide[rows]).astype(BF16))
            columns.append(jnp.concatenate(weighted, axis=0))
        result = jnp.dot(jnp.concatenate(columns, axis=1), joined(c0[...], c1[...]), preferred_element_type=F32)
        put(first, result[:width, :width])
        put(second, result[width:, width:])
    for out, tail in zip(returned, tails):
        out[CAP * height :] = tail.astype(BF16)


def collect_kernel(count, orders, place, core, half, *rest):
    arriving, (term, diag_new, send_a, send_b, total, tails) = rest[:-6], rest[-6:]
    width = core.shape[-1]
    height = width // 2
    total[...] = jnp.zeros_like(total)
    tails[...] = jnp.zeros_like(tails)
    for number, block in enumerate(arriving):
        p = partner(orders, number)
        last = block[CAP * height :].astype(F32)
        for n in range(CAP):
            at = place[p, n]
            kept = at >= 0
            at = jnp.maximum(at, 0)
            total[at] += jnp.where(kept, block[n * height : (n + 1) * height].astype(F32), 0.0)
            tails[at] += jnp.where(kept, last[n : n + 1], 0.0)
    lane, row = lanes_rows((width, width))
    for i in range(count):
        triangle = unpack_triangle(total[i], tails[i][:1])
        whole = jnp.where(lane == row, triangle, triangle + triangle.T)
        term[i] = whole
        diag_new[i] = (core[0, i, 0].astype(F32) + whole).astype(BF16)

    even = lax.axis_index("col") % 2 == 0
    last = count - 1

    @pl.when(even)
    def _():
        send_a[0] = diag_new[last]
        send_b[0] = diag_new[0]
        put_half(count, half, send_a, 1, True)

    @pl.when(jnp.logical_not(even))
    def _():
        send_a[0] = diag_new[0]
        send_b[0] = diag_new[last]
        put_half(count, half, send_a, 1, False)


def second_inner_kernel(count, leads, absorption, half, core, diag_new, term, out, hp_ref, grid_term,
                        moved_ref, wh_ref, left_ref, right_ref, sem):
    copy = pltpu.make_async_copy(term, grid_term, sem.at[0])
    copy.start()
    new_diagonals(range(count), count, leads, absorption, core, diag_new, left_ref, right_ref)
    get_left = band_access(count, core, None, None, None, None, left_ref)
    get_right = band_access(count, core, None, None, None, None, right_ref)
    get_q = band_at(half)

    def get_hp(i, j):
        return hp_ref[i + 1, j - i + 1]

    taylor_first(range(count), 1, count - 2, get_left, get_q, hp_ref)
    propagate([(2, count - 3)], get_q, get_hp, get_left, get_right, moved_ref, wh_ref, band_writer(out, 2))
    copy.wait()


def second_outer_kernel(count, leads, absorption, half, core, diag_new, core_a, core_b, got_a, got_b, half_b,
                        hp_in, inner, out, hp_ref, moved_ref, wh_ref, left_ref, right_ref, edges, ready, sems):
    copies = [pltpu.make_async_copy(inner, out.at[:, pl.ds(2, count - 4)], sems.at[2])]
    for n, i in enumerate((0, count - 2)):
        copies.append(pltpu.make_async_copy(ready.at[:, pl.ds(2 * n, 2)], out.at[:, pl.ds(i, 2)], sems.at[n]))
    copies[0].start()
    core_low, core_high = halo_reader(core_a, core_b)
    even = lax.axis_index("col") % 2 == 0

    def low(n):
        return jnp.where(even, got_b[0] if n == 0 else half_b[n - 1], got_a[n])

    def high(n):
        return jnp.where(even, got_a[n], got_b[0] if n == 0 else half_b[n - 1])

    last = count - 1
    edges[0] = dagger(band_at(core)(0, -1))
    edges[1] = dagger(band_at(core)(last, count))
    ends = unpack_hermitian(core_low(3)), unpack_hermitian(core_high(3))
    rows = [-1, 0, 1, 2, count - 3, count - 2, last, count]
    new_diagonals(rows, count, leads, absorption, core, diag_new, left_ref, right_ref, ends, (low(0), high(0)))

    def get_q(i, j):
        if 0 <= i < count:
            return band_at(half)(i, j)
        n = 1 if i == j else 3 if i in (-1, count) else 5
        side = low if i < 0 else high
        return joined(side(n), side(n + 1))

    def far_low():
        return joined(core_low(4), core_low(5))

    def far_high():
        return joined(core_high(4), core_high(5))

    get_left = band_access(count, core, far_low, far_high, edges.at[0], edges.at[1], left_ref)
    get_right = band_access(count, core, far_low, far_high, edges.at[0], edges.at[1], right_ref)

    def get_hp(i, j):
        ref = hp_in if 1 <= i <= count - 2 else hp_ref
        return ref[i + 1, j - i + 1]

    def write(i, j, value):
        width = value.shape[0]
        n = i if i < 2 else i - count + 4
        ready[0, n, j - i + 1] = value[:, :width]
        ready[1, n, j - i + 1] = value[:, width:]
        if (i, j) == (1, 2):
            copies[1].start()
        if (i, j) == (last, count):
            copies[2].start()

    taylor_first(range(-1, 2), -1, 0, get_left, get_q, hp_ref)
    taylor_first(range(last - 1, count + 1), last, count, get_left, get_q, hp_ref)
    propagate([(0, 1), (last - 1, last)], get_q, get_hp, get_left, get_right, moved_ref, wh_ref, write)
    for copy in copies:
        copy.wait()


def exchange_a(x, total):
    return lax.ppermute(x, ("row", "col"), [(i, i ^ 1) for i in range(total)])


def exchange_b(x, total):
    return lax.ppermute(x, ("row", "col"), [(i, i + 1) if i % 2 else (i, i - 1) for i in range(1, total - 1)])


def shards(density, core, grid_old, lead_blocks, absorption, collocation, brick_block):
    count = density.shape[1]
    width = density.shape[-1]
    row_size = lax.axis_size("row")
    col_size = lax.axis_size("col")
    total = row_size * col_size
    near, far = list(range(1, row_size // 2)), list(range(row_size // 2, row_size))
    orders = [[0] + far + near, [0] + far + near]
    bricks = brick_block.shape[1]
    vmem = pl.BlockSpec(memory_space=pltpu.VMEM)
    hbm = pl.BlockSpec(memory_space=pltpu.HBM)

    message = jax.ShapeDtypeStruct((6, width, width), BF16)
    table = jax.ShapeDtypeStruct(brick_block.shape, jnp.int32)
    send_b = call(
        functools.partial(send_kernel, count),
        message,
        flops=1 << 20,
        vmem=8,
        in_specs=[hbm] * 3,
        scratch=[
            pltpu.VMEM((4, 2, width, width), BF16),
            pltpu.VMEM((width, width), F32),
            pltpu.SemaphoreType.DMA((5,)),
        ],
    )(*(in_hbm(x) for x in (density, core, grid_old)))
    got_b = exchange_b(send_b, total)

    def band_scratch(rows):
        return pltpu.VMEM((rows, 3, width, 2 * width), BF16)

    def sides(n):
        return pltpu.VMEM((n, width, 2 * width), BF16)

    hp_shape = jax.ShapeDtypeStruct((count + 2, 3, width, 2 * width), BF16)
    inner_scratch = [band_scratch(count + 2)] * 2 + [sides(count + 2)] * 2
    outer_scratch = [band_scratch(count + 2)] * 3 + [sides(count + 2)] * 2
    hp, half_inner, place, which, send_a = call(
        functools.partial(first_inner_kernel, count),
        (hp_shape, jax.ShapeDtypeStruct(density.shape, BF16), table, table, message),
        flops=PROP_FLOPS,
        vmem=16,
        scalars=2,
        in_specs=[vmem] * 4,
        scratch=inner_scratch,
    )(lead_blocks, absorption, density, core, grid_old, brick_block)
    got_a = exchange_a(send_a, total)
    packed_rows = CAP * width // 2 + TILE
    packed_shape = jax.ShapeDtypeStruct((packed_rows, width), BF16)
    half_message = jax.ShapeDtypeStruct((6, width, width), BF16)
    half, send_b, *outgoing = call(
        functools.partial(first_outer_kernel, count, orders),
        (
            jax.ShapeDtypeStruct(density.shape, BF16),
            half_message,
        )
        + (packed_shape,) * row_size,
        flops=PROP_FLOPS,
        vmem=20,
        scalars=3,
        in_specs=[vmem] * 7,
        scratch=outer_scratch
        + [
            pltpu.VMEM((6, width, 2 * width), BF16),
            pltpu.VMEM((count, width // 2, width), BF16),
            pltpu.VMEM((count, 8, width), F32),
        ],
    )(lead_blocks, absorption, place, density, core, grid_old, got_a, got_b, hp, half_inner)


    def across(x, number):
        if number == 0:
            return x
        pairs = []
        for row in range(row_size):
            for col in range(col_size):
                pairs.append((row * col_size + col, (row ^ orders[col % 2][number]) * col_size + col))
        return lax.ppermute(x, ("row", "col"), pairs)

    half_b = exchange_b(send_b, total)
    incoming = [across(x, number) for number, x in enumerate(outgoing)]
    points = collocation.shape[1]
    arriving = []
    before = which
    ends = list(range(2, row_size - 3, 2)) + [row_size]
    for numbers in [range(a, b) for a, b in zip([0] + ends, ends)]:
        returned = call(
            functools.partial(brick_kernel, points // 4, orders, numbers),
            (packed_shape,) * len(numbers),
            flops=4 * CAP * len(numbers) * points * width**2,
            vmem=8,
            scalars=1,
            in_specs=[vmem, pl.BlockSpec(memory_space=pl.ANY)] + [vmem] * len(numbers),
        )(which, collocation, before, *(incoming[number] for number in numbers))
        arriving += [across(x, number) for number, x in zip(numbers, returned)]
        before = half_b if numbers[-1] + 4 >= row_size - 1 else returned[0]

    term, diag_new, send_a, send_b = call(
        functools.partial(collect_kernel, count, orders),
        (
            jax.ShapeDtypeStruct((count, width, width), F32),
            jax.ShapeDtypeStruct((count, width, width), BF16),
            jax.ShapeDtypeStruct((7, width, width), BF16),
            jax.ShapeDtypeStruct((1, width, width), BF16),
        ),
        flops=1 << 20,
        vmem=8,
        scalars=1,
        grid=(1,),
        in_specs=[block_spec((1, count, 1, width, width), (0, 0, 1, 0, 0))] + [vmem] * (row_size + 1),
        scratch=[pltpu.VMEM((count, width // 2, width), F32), pltpu.VMEM((count, 8, width), F32)],
    )(place, core, half, *arriving)
    half_a, diag_b = exchange_a(send_a, total), exchange_b(send_b, total)

    inner, hp, grid_term = call(
        functools.partial(second_inner_kernel, count),
        (
            jax.ShapeDtypeStruct((2, count - 4, 3, width, width), BF16),
            hp_shape,
            pltpu.HBM((count, width, width), F32),
        ),
        flops=PROP_FLOPS,
        vmem=16,
        scalars=2,
        in_specs=[vmem] * 4,
        out_specs=(vmem, vmem, hbm),
        scratch=inner_scratch + [pltpu.SemaphoreType.DMA((1,))],
    )(lead_blocks, absorption, half, core, diag_new, term)
    density_next = call(
        functools.partial(second_outer_kernel, count),
        pltpu.HBM(density.shape, BF16),
        flops=PROP_FLOPS,
        vmem=16,
        scalars=2,
        in_specs=[vmem] * 10,
        out_specs=hbm,
        scratch=outer_scratch + [sides(2), pltpu.VMEM((2, 4, 3, width, width), BF16), pltpu.SemaphoreType.DMA((3,))],
    )(lead_blocks, absorption, half, core, diag_new, got_a, got_b, half_a, diag_b, half_b, hp, inner)
    return (density_next, grid_term)


def solution(mesh):
    band = P(None, ("row", "col"), None, None, None)
    blocks = P(("row", "col"), None, None)
    return jax.shard_map(
        shards,
        mesh=mesh,
        in_specs=(band, band, blocks, P(), P(), blocks, P(None, "col")),
        out_specs=(band, blocks),
        check_vma=False,
    )
```
